128 devices in a mesh: row: 8 (over z, core), col: 16 (over x, y).
Axes of the slice: x: 4, y: 4, z: 4, core: 2. Of those that a mesh axis runs over, the one named last changes fastest.
Arguments:
- tensor: bfloat16 [64, 64, 4096], P('col', 'row'), may hold values from -1.5 to 1.5
- bond_weights: float32 [2, 64], replicated, may hold values from 0.5 to 2
- start_blocks: float32 [64, 64, 128], P('col', 'row'), may hold values from -6 to 6
Outputs:
- projectors: float32 [64, 64, 128], P('col', 'row')
- new_tensor: float32 [64, 8, 4096], P('col', 'row')
The draws below stay inside these ranges and needn't reach their ends.
All inputs are finite; a program needn't handle non-finite values.
Results may differ from the reference program's by a relative error of at most 0.02.
Values may be sent and summed in bfloat16 or wider, within the bound.
No kernel may reach another device: no remote copies, remote signals or barrier semaphores. Data moves between devices by JAX's collectives and lax.ppermute only.
A program may use at most 128 MiB of HBM per device.

```python
import math
import jax
import jax.numpy as jnp
from jax import lax

D = 64
RANK = 64
ITERS = 3
DWIN = 8
N_ROW = 8
N_COL = 16


def draw_tensor(key, part):
    fresh_key = jax.random.fold_in(key, 11)
    up_key = jax.random.fold_in(key, 12)
    down_key = jax.random.fold_in(key, 13)
    fresh_part = jax.random.normal(fresh_key, (D, D, D, D), jnp.float32) * 0.15
    along_up = jax.random.normal(up_key, (D, D, D, 1), jnp.float32) * 0.15
    along_down = jax.random.normal(down_key, (D, D, 1, D), jnp.float32) * 0.15
    combined = jnp.clip(fresh_part + along_up + along_down, -1.5, 1.5)
    return combined.reshape(D, D, D * D).astype(jnp.bfloat16)


def block_scale(key, extent, cuts, smallest, top_value):
    def one(dim, shards_of):
        draws = jax.random.uniform(jax.random.fold_in(jax.random.fold_in(key, 6), dim), (shards_of,), jnp.float32, smallest / len(cuts), top_value / len(cuts))
        return jnp.repeat(jnp.exp(draws), extent[dim] // shards_of).reshape((-1,) + (1,) * (len(extent) - dim - 1))

    factor_of = one(*cuts[0])
    for cut in cuts[1:]:
        factor_of = factor_of * one(*cut)
    return factor_of


def scatter_about(key, dims, spread, most, shards=(), kind=jnp.bfloat16):
    result = spread * jax.random.normal(key, dims, jnp.float32)
    if shards:
        result = result * block_scale(key, dims, shards, -0.22, 0.18)
    return jnp.clip(result, -most, most).astype(kind)


def setup_inputs(seed: int = 0) -> dict:
    key_of = jax.random.split(jax.random.key(seed), 4)
    tensor = draw_tensor(jax.random.fold_in(key_of[3], 71), 0)
    bond_weights = jnp.clip(jnp.exp(jax.random.uniform(key_of[1], (2, D), jnp.float32, math.log(0.5), math.log(2.0))), 0.5, 2.0)
    start_blocks = scatter_about(key_of[2], (D, D, 2 * RANK), 1.0, 6.0, ((0, 16), (1, 8)), jnp.float32)
    return dict(tensor=tensor, bond_weights=bond_weights, start_blocks=start_blocks)


PRECISION_TOP = lax.Precision.HIGHEST

def rounded(value):
    return lax.optimization_barrier(value.astype(jnp.bfloat16)).astype(jnp.float32)

def summed_blocks(operand, block_size, count, axis, contract):

    def add_block(running, block_index):
        portion = lax.dynamic_slice_in_dim(operand, block_index * block_size, block_size, axis)
        return (running + rounded(contract(portion)), None)
    running, _ = lax.scan(add_block, jnp.zeros((D, D, D, D), jnp.float32), jnp.arange(count, dtype=jnp.int32))
    return rounded(running)

def subspace(gram, initial):
    matrix = gram.reshape(D * D, D * D)
    vectors = initial.reshape(D * D, RANK)
    for iteration in range(ITERS):
        images = jnp.dot(matrix, vectors, precision=PRECISION_TOP)
        correlation = jnp.dot(images.T, images, precision=PRECISION_TOP)
        factor = jnp.linalg.cholesky(correlation)
        vectors = lax.linalg.triangular_solve(factor, images, left_side=False, lower=True, transpose_a=True)
    return vectors.reshape(D, D, RANK)

def reference(tensor, bond_weights, start_blocks):
    tensor_f32 = tensor.reshape(D, D, D, D).astype(jnp.float32)
    horizontal = bond_weights[0]
    vertical = bond_weights[1]
    copy_one = rounded(tensor_f32 * horizontal[None, :, None, None] * vertical[None, None, :, None])
    copy_two = rounded(tensor_f32 * horizontal[None, :, None, None] * vertical[None, None, None, :])
    copy_three = rounded(tensor_f32 * horizontal[:, None, None, None] * vertical[None, None, None, :])
    copy_four = rounded(tensor_f32 * vertical[None, None, :, None])
    inner_vertical = vertical[None, :, None, None] * vertical[None, None, None, :]
    inner_horizontal = horizontal[:, None, None, None] * horizontal[None, None, :, None]
    left_up = summed_blocks(copy_one, D // N_ROW, N_ROW, 1, lambda portion: jnp.einsum('lrdu,mrdv->lumv', portion, portion, precision=PRECISION_TOP) * inner_vertical)
    left_down = summed_blocks(copy_two, D // N_ROW, N_ROW, 1, lambda portion: jnp.einsum('lrdu,mreu->ldme', portion, portion, precision=PRECISION_TOP))
    right_down = summed_blocks(copy_three, D // N_COL, N_COL, 0, lambda portion: jnp.einsum('lrdu,lseu->rdse', portion, portion, precision=PRECISION_TOP) * inner_horizontal)
    gram_left = jnp.einsum('akmq,bknq->abmn', left_up, left_down, precision=PRECISION_TOP)
    gram_down = jnp.einsum('kaqe,kbqf->abef', right_down, left_down, precision=PRECISION_TOP)
    proj_left = subspace(gram_left, start_blocks[:, :, :RANK])
    proj_down = subspace(gram_down, start_blocks[:, :, RANK:])
    projectors = jnp.concatenate([proj_left, proj_down], axis=2)
    complete_basis = rounded(proj_left)

    def layer_of_slab(layer_index):
        bottom = lax.dynamic_index_in_dim(tensor_f32, layer_index, 2, keepdims=False)
        first_section = rounded(jnp.einsum('lpa,lrk->park', complete_basis, bottom, precision=PRECISION_TOP))
        latter_section = rounded(jnp.einsum('park,pskv->arsv', first_section, copy_four, precision=PRECISION_TOP))
        contracted_tensor = jnp.einsum('medw,edg->wmg', latter_section, complete_basis, precision=PRECISION_TOP)
        return contracted_tensor.reshape(D, RANK * RANK)
    layers = lax.map(layer_of_slab, jnp.arange(DWIN, dtype=jnp.int32))
    new_tensor = jnp.transpose(layers, (1, 0, 2))
    return (projectors, new_tensor)
```

```python
import jax
import jax.numpy as jnp
from jax import lax
from jax.experimental import pallas as pl
from jax.experimental.pallas import tpu as pltpu
from jax.sharding import Mesh
from jax.sharding import PartitionSpec as P

D = 64
RANK = 64
COL = ("col_0", "col_1")
ROW_COL = ("row", "col_0", "col_1")
HIGHEST = lax.Precision.HIGHEST
F32 = jnp.float32
BF16 = jnp.bfloat16
A_BLOCK = 16


def from_everyone(shard, axis):
    copies = jnp.broadcast_to(shard, (lax.axis_size(axis), *shard.shape))
    return lax.all_to_all(copies, axis, split_axis=0, concat_axis=0, tiled=True)


def in_order(tiles, dim):
    dims = list(tiles.shape[1:])
    dims[dim] *= tiles.shape[0]
    return jnp.moveaxis(tiles, 0, dim).reshape(dims)


def gathered_copies(shard, axis, dim):
    return in_order(from_everyone(shard, axis), dim)


def weighted_copy(block, scale):
    return (block.astype(F32) * scale).astype(BF16)


def two_parts(x):
    high = x.astype(BF16)
    return high, (x - high.astype(F32)).astype(BF16)


def in_index_order(y_ref):
    return jnp.transpose(y_ref[...], (1, 0, 2, 3)).reshape(D * D, 2 * RANK)


def inverse_factors(mats):
    n = RANK
    rows_at = lax.broadcasted_iota(jnp.int32, (8, 2 * n), 0)
    lanes_at = lax.broadcasted_iota(jnp.int32, (8, 2 * n), 1)
    sets = []
    for c in mats:
        blocks = []
        for i in range(n // 8):
            unit = (lanes_at == rows_at + (n + 8 * i)).astype(F32)
            part = jnp.concatenate([c[8 * i : 8 * i + 8], jnp.zeros((8, n), F32)], axis=1)
            blocks.append(part + unit)
        sets.append(blocks)
    for k in range(n):
        b, s = divmod(k, 8)
        for blocks in sets:
            row = blocks[b][s : s + 1, :]
            scaled = row / row[:, k : k + 1]
            for i in range(b, n // 8):
                column = blocks[i][:, k : k + 1]
                step = column * scaled
                if i == b:
                    step = jnp.where(rows_at > s, step, 0.0)
                blocks[i] = blocks[i] - step
    out = []
    for blocks in sets:
        done = []
        for i in range(n // 8):
            own = jnp.where(lanes_at == rows_at + 8 * i, blocks[i], 0.0)
            pivot = jnp.sum(own, axis=1, keepdims=True)
            done.append(blocks[i][:, n:] / jnp.sqrt(pivot))
        out.append(jnp.concatenate(done, axis=0))
    return out


def factors_of(y):
    c = lax.dot_general(
        y, y, (((0,), (0,)), ((), ())), precision=HIGHEST, preferred_element_type=F32
    )
    return inverse_factors([c[:RANK, :RANK], c[RANK:, RANK:]])


def store_inverse(inv_ref, left, down):
    zero = jnp.zeros((RANK, RANK), F32)
    inv_ref[:RANK, :] = jnp.concatenate([left, zero], axis=1)
    inv_ref[RANK:, :] = jnp.concatenate([zero, down], axis=1)


def images_of(y, gl_high, gl_low, gd_high, gd_low, zl_ref, zd_ref):
    y_high, y_low = two_parts(y)
    both = jnp.concatenate([y_high, y_low], axis=1)

    def product(high, low):
        main = jnp.dot(high[...], both, preferred_element_type=F32)
        rest = jnp.dot(low[...], y_high, preferred_element_type=F32)
        return main[:, : 2 * RANK] + main[:, 2 * RANK :] + rest

    z = product(gl_high, gl_low)[:, :RANK].reshape(8, 32, RANK)
    zl_ref[...] = jnp.concatenate([z[:, :16], z[:, 16:]], axis=2)
    zd_ref[...] = product(gd_high, gd_low)


def first_kernel(y_ref, glh, gll, gdh, gdl, zl_ref, zd_ref):
    images_of(in_index_order(y_ref), glh, gll, gdh, gdl, zl_ref, zd_ref)


def next_kernel(y_ref, glh, gll, gdh, gdl, zl_ref, zd_ref, inv_ref):
    y = in_index_order(y_ref)
    images_of(y, glh, gll, gdh, gdl, zl_ref, zd_ref)
    store_inverse(inv_ref, *factors_of(y))


def last_kernel(y_ref, basis_ref, inv_ref):
    y = in_index_order(y_ref)
    left, down = factors_of(y)
    store_inverse(inv_ref, left, down)
    basis = lax.dot_general(
        y[:, :RANK], left, (((1,), (1,)), ((), ())), precision=HIGHEST, preferred_element_type=F32
    )
    basis_ref[...] = basis.astype(BF16)


def vmem_call(kernel, outs, args, limit=48):
    spec = pl.BlockSpec(memory_space=pltpu.VMEM)
    return pl.pallas_call(
        kernel,
        out_shape=outs,
        in_specs=[spec] * len(args),
        out_specs=tuple([spec] * len(outs)),
        compiler_params=pltpu.CompilerParams(vmem_limit_bytes=limit << 20),
    )(*args)


def contract_kernel(bottom_ref, basis_ref, top_ref, out_ref, wide_ref, diag_ref):
    @pl.when(pl.program_id(0) == 0)
    def _():
        diag_ref[...] = jnp.zeros_like(diag_ref)

    bottom = bottom_ref[...]

    def one(a, carry):
        block = basis_ref[a]
        for i in range(4):
            diag_ref[64 * i : 64 * i + 64, 64 * i : 64 * i + 64] = block
        section = jnp.dot(bottom, diag_ref[...], preferred_element_type=F32).astype(BF16)
        start = pl.multiple_of(a * D, D)
        for q in range(16):
            wide_ref[pl.ds(start, D), 256 * q : 256 * q + 256] = section[64 * q : 64 * q + 64]
        return carry

    lax.fori_loop(0, A_BLOCK, one, 0)
    out_ref[...] = lax.dot_general(
        wide_ref[...], top_ref[...], (((1,), (1,)), ((), ())), preferred_element_type=F32
    ).astype(BF16)


def contract(bottom, basis, top):
    rows = A_BLOCK * D
    return pl.pallas_call(
        contract_kernel,
        grid=(RANK // A_BLOCK,),
        out_shape=jax.ShapeDtypeStruct((RANK * D, 256), BF16),
        in_specs=[
            pl.BlockSpec((1024, 256), lambda i: (0, 0)),
            pl.BlockSpec((A_BLOCK, D, D), lambda i: (i, 0, 0)),
            pl.BlockSpec((256, D * D), lambda i: (0, 0)),
        ],
        out_specs=pl.BlockSpec((rows, 256), lambda i: (i, 0)),
        scratch_shapes=[pltpu.VMEM((rows, D * D), BF16), pltpu.VMEM((256, 256), BF16)],
        compiler_params=pltpu.CompilerParams(vmem_limit_bytes=48 << 20),
    )(bottom, basis, top)


def body(tensor, bond_weights, start_blocks):
    col_count = lax.axis_size(COL)
    row_count = lax.axis_size("row")
    col_index = lax.axis_index(COL)
    row_index = lax.axis_index("row")
    left_block = tensor.shape[0]
    right_block = tensor.shape[1]
    horizontal = bond_weights[0]
    vertical = bond_weights[1]
    horiz_rows = lax.dynamic_slice_in_dim(horizontal, row_index * right_block, right_block)
    horiz_cols = lax.dynamic_slice_in_dim(horizontal, col_index * left_block, left_block)
    by_cols = lax.all_gather(tensor, COL, axis=0, tiled=True).reshape(D, right_block, D, D)
    first_vectors = lax.all_gather(start_blocks.reshape(32, 2 * RANK), ROW_COL)
    first_scale = horiz_rows[None, :, None, None] * vertical[None, None, :, None]
    scale_two = horiz_rows[None, :, None, None] * vertical[None, None, None, :]
    cols_one = weighted_copy(by_cols, first_scale)
    cols_two = weighted_copy(by_cols, scale_two)
    own_one = lax.dynamic_slice_in_dim(cols_one, col_index * left_block, left_block, 0)
    own_two = lax.dynamic_slice_in_dim(cols_two, col_index * left_block, left_block, 0)
    inner_vertical = vertical[None, :, None, None] * vertical[None, None, None, :]
    part_up = (
        jnp.einsum("lrdu,mrdv->lumv", own_one, cols_one, preferred_element_type=F32)
        * inner_vertical
    )
    part_down = jnp.einsum("lrdu,mreu->ldme", own_two, cols_two, preferred_element_type=F32)
    both = jnp.concatenate([part_up.astype(BF16), part_down.astype(BF16)], axis=0)
    both = lax.psum_scatter(both, "row", scatter_dimension=1, tiled=True)
    left_up, left_down = both[:left_block], both[left_block:]
    down_all = lax.all_gather(left_down, COL, axis=0, tiled=True)
    part_gram = jnp.einsum("akmq,bknq->abmn", left_up, down_all, preferred_element_type=F32)
    by_rows = gathered_copies(tensor, "row", 1).reshape(left_block, D, D, D)
    scale_three = horiz_cols[:, None, None, None] * vertical[None, None, None, :]
    weighted_rows = weighted_copy(by_rows, scale_three)
    own_rows = lax.dynamic_slice_in_dim(weighted_rows, row_index * right_block, right_block, 1)
    inner_side = horiz_rows[:, None, None, None] * horizontal[None, None, :, None]
    part_side = (
        jnp.einsum("lrdu,lseu->rdse", own_rows, weighted_rows, preferred_element_type=F32)
        * inner_side
    )
    right_down = part_side.astype(BF16)
    for axis in COL:
        right_down = lax.psum_scatter(right_down, axis, scatter_dimension=1, tiled=True)
    side_all = gathered_copies(right_down, "row", 0)
    gram_down = jnp.einsum("kaqe,kbqf->abef", side_all, down_all, preferred_element_type=F32)

    gram_left = part_gram.reshape(left_block, row_count, right_block, D * D)
    gram_left = jnp.swapaxes(gram_left, 0, 1).reshape(256, D * D)
    grams = (*two_parts(gram_left), *two_parts(gram_down.reshape(32, D * D)))
    z_outs = (
        jax.ShapeDtypeStruct((8, 16, 2 * RANK), F32),
        jax.ShapeDtypeStruct((32, 2 * RANK), F32),
    )
    inv_out = jax.ShapeDtypeStruct((2 * RANK, 2 * RANK), F32)

    def local_images(z_left, z_down):
        z_left = jnp.sum(lax.all_to_all(z_left, "row", 0, 0, tiled=True), axis=0)
        z_left = jnp.concatenate([z_left[:, :RANK], z_left[:, RANK:]], axis=0)
        return jnp.concatenate([z_left, z_down[:, RANK:]], axis=1)

    def everywhere(y):
        return from_everyone(y, ROW_COL).reshape(8, D, 8, 2 * RANK)

    def apply(y, inverse):
        return lax.dot_general(y, inverse, (((1,), (1,)), ((), ())), precision=HIGHEST)

    y = local_images(
        *vmem_call(first_kernel, z_outs, (first_vectors.reshape(8, D, 8, 2 * RANK), *grams))
    )
    for _ in range(2):
        z_left, z_down, inverse = vmem_call(
            next_kernel, (*z_outs, inv_out), (everywhere(y), *grams)
        )
        y = apply(local_images(z_left, z_down), inverse)
    basis, inverse = vmem_call(
        last_kernel, (jax.ShapeDtypeStruct((D * D, RANK), BF16), inv_out), (everywhere(y),)
    )
    projectors = apply(y, inverse).reshape(left_block, right_block, 2 * RANK)

    top_block = D // col_count
    top_local = lax.dynamic_slice_in_dim(by_cols, col_index * top_block, top_block, 3)
    top_weighted = weighted_copy(top_local, vertical[None, None, :, None])
    top_rows = jnp.transpose(top_weighted, (3, 1, 2, 0)).reshape(top_block * right_block, D * D)
    top = from_everyone(top_rows, "row").reshape(row_count, top_block, right_block, D * D)
    top = jnp.swapaxes(top, 0, 1).reshape(256, D * D)
    slab_part = jnp.transpose(by_cols[:, :, :row_count, :], (2, 3, 1, 0))
    slab = lax.all_to_all(slab_part, "row", split_axis=0, concat_axis=0, tiled=True)
    bottom = jnp.transpose(slab.reshape(row_count, 16, 4, right_block, D), (1, 0, 3, 2, 4))
    bottom = bottom.reshape(1024, 256)
    basis_first = jnp.transpose(basis.reshape(D, D, RANK), (2, 0, 1))
    second = contract(bottom, basis_first, top).reshape(RANK, D, top_block, D)
    new_tensor = jnp.einsum(
        "aruq,rqb->uab", second, basis.reshape(D, D, RANK), preferred_element_type=F32
    ).reshape(top_block, 1, RANK * RANK)
    return (projectors, new_tensor)


def solution(mesh):
    torus = Mesh(mesh.devices.reshape(mesh.shape["row"], 4, 4), ("row", "col_0", "col_1"))
    placed = (P(COL, "row", None), P(), P(COL, "row", None))
    return jax.shard_map(
        body,
        mesh=torus,
        in_specs=placed,
        out_specs=(P(COL, "row", None), P(COL, "row", None)),
        check_vma=False,
    )
```

```python
import jax
import jax.numpy as jnp
from jax import lax
from jax.experimental import pallas as pl
from jax.experimental.pallas import tpu as pltpu
from jax.sharding import Mesh
from jax.sharding import PartitionSpec as P

D = 64
RANK = 64
COL = ("col_0", "col_1")
ROW_COL = ("row", "col_0", "col_1")
HIGHEST = lax.Precision.HIGHEST
F32 = jnp.float32
BF16 = jnp.bfloat16
A_BLOCK = 16
UNROLL = 4


def from_everyone(shard, axis):
    copies = jnp.broadcast_to(shard, (lax.axis_size(axis), *shard.shape))
    return lax.all_to_all(copies, axis, split_axis=0, concat_axis=0, tiled=True)


def two_parts(x):
    high = x.astype(BF16)
    return high, (x - high.astype(F32)).astype(BF16)


def in_index_order(y_ref):
    return jnp.transpose(y_ref[...], (1, 0, 2, 3)).reshape(D * D, 2 * RANK)


def inverse_factors(mats):
    n = RANK
    rows_at = lax.broadcasted_iota(jnp.int32, (8, 2 * n), 0)
    lanes_at = lax.broadcasted_iota(jnp.int32, (8, 2 * n), 1)
    sets = []
    for c in mats:
        blocks = []
        for i in range(n // 8):
            unit = (lanes_at == rows_at + (n + 8 * i)).astype(F32)
            part = jnp.concatenate([c[8 * i : 8 * i + 8], jnp.zeros((8, n), F32)], axis=1)
            blocks.append(part + unit)
        sets.append(blocks)
    for k in range(n):
        b, s = divmod(k, 8)
        for blocks in sets:
            row = blocks[b][s : s + 1, :]
            scaled = row / row[:, k : k + 1]
            for i in range(b, n // 8):
                column = blocks[i][:, k : k + 1]
                step = column * scaled
                if i == b:
                    step = jnp.where(rows_at > s, step, 0.0)
                blocks[i] = blocks[i] - step
    out = []
    for blocks in sets:
        done = []
        for i in range(n // 8):
            own = jnp.where(lanes_at == rows_at + 8 * i, blocks[i], 0.0)
            pivot = jnp.sum(own, axis=1, keepdims=True)
            done.append(blocks[i][:, n:] / jnp.sqrt(pivot))
        out.append(jnp.concatenate(done, axis=0))
    return out


def factors_of(y):
    c = lax.dot_general(
        y, y, (((0,), (0,)), ((), ())), precision=HIGHEST, preferred_element_type=F32
    )
    return inverse_factors([c[:RANK, :RANK], c[RANK:, RANK:]])


def store_inverse(inv_ref, left, down):
    zero = jnp.zeros((RANK, RANK), F32)
    inv_ref[:RANK, :] = jnp.concatenate([left, zero], axis=1)
    inv_ref[RANK:, :] = jnp.concatenate([zero, down], axis=1)


def images_of(y, gl_high, gl_low, gd_high, gd_low, zl_ref, zd_ref):
    y_high, y_low = two_parts(y)
    both = jnp.concatenate([y_high, y_low], axis=1)

    def product(high, low):
        main = jnp.dot(high[...], both, preferred_element_type=F32)
        rest = jnp.dot(low[...], y_high, preferred_element_type=F32)
        return main[:, : 2 * RANK] + main[:, 2 * RANK :] + rest

    z = product(gl_high, gl_low)[:, :RANK].reshape(8, 32, RANK)
    zl_ref[...] = jnp.concatenate([z[:, :16], z[:, 16:]], axis=2)
    zd_ref[...] = product(gd_high, gd_low)


def first_kernel(y_ref, glh, gll, gdh, gdl, zl_ref, zd_ref):
    images_of(in_index_order(y_ref), glh, gll, gdh, gdl, zl_ref, zd_ref)


def next_kernel(y_ref, glh, gll, gdh, gdl, zl_ref, zd_ref, inv_ref):
    y = in_index_order(y_ref)
    images_of(y, glh, gll, gdh, gdl, zl_ref, zd_ref)
    store_inverse(inv_ref, *factors_of(y))


def last_kernel(y_ref, basis_ref, inv_ref):
    y = in_index_order(y_ref)
    left, down = factors_of(y)
    store_inverse(inv_ref, left, down)
    basis = lax.dot_general(
        y[:, :RANK], left, (((1,), (1,)), ((), ())), precision=HIGHEST, preferred_element_type=F32
    )
    basis_ref[...] = basis.astype(BF16)


def vmem_call(kernel, outs, args, limit=48):
    spec = pl.BlockSpec(memory_space=pltpu.VMEM)
    return pl.pallas_call(
        kernel,
        out_shape=outs,
        in_specs=[spec] * len(args),
        out_specs=tuple([spec] * len(outs)),
        compiler_params=pltpu.CompilerParams(vmem_limit_bytes=limit << 20),
    )(*args)


def fill_diagonal(diag_ref, slot, block):
    for i in range(4):
        diag_ref[slot, 64 * i : 64 * i + 64, 64 * i : 64 * i + 64] = block


def contract_kernel(
    bottom_ref, first_ref, basis_ref, top_ref, out_ref, wide_ref, diag_ref, even_ref, odd_ref, sum_ref
):
    step_id = pl.program_id(0)
    rows_here = A_BLOCK * D

    @pl.when(step_id == 0)
    def _():
        diag_ref[...] = jnp.zeros_like(diag_ref)

    bottom = bottom_ref[...]

    def sections(group, carry):
        for j in range(UNROLL):
            fill_diagonal(diag_ref, j, first_ref[group * UNROLL + j])
        for j in range(UNROLL):
            section = jnp.dot(bottom, diag_ref[j], preferred_element_type=F32).astype(BF16)
            start = pl.multiple_of((group * UNROLL + j) * D, D)
            for q in range(16):
                wide_ref[pl.ds(start, D), 256 * q : 256 * q + 256] = section[64 * q : 64 * q + 64]
        return carry

    lax.fori_loop(0, A_BLOCK // UNROLL, sections, 0)
    second = jnp.dot(wide_ref[...], top_ref[...], preferred_element_type=F32)
    second = second.astype(BF16).astype(F32)
    base = pl.multiple_of(step_id * rows_here, rows_here)
    even_ref[pl.ds(base, rows_here), :] = second[:, :128]
    odd_ref[pl.ds(base, rows_here), :] = second[:, 128:]

    @pl.when(step_id == RANK // A_BLOCK - 1)
    def _():
        sum_ref[...] = jnp.zeros_like(sum_ref)

        def products(group, carry):
            total = sum_ref[...]
            for j in range(UNROLL):
                fill_diagonal(diag_ref, j, basis_ref[group * UNROLL + j])
            for j in range(UNROLL):
                picked = pl.ds(group * UNROLL + j, RANK, stride=D)
                rows = jnp.concatenate([even_ref[picked, :], odd_ref[picked, :]], axis=1)
                total = total + jnp.dot(
                    rows.astype(BF16), diag_ref[j], preferred_element_type=F32
                )
            sum_ref[...] = total
            return carry

        lax.fori_loop(0, D // UNROLL, products, 0)
        for u in range(4):
            out_ref[u] = sum_ref[:, 64 * u : 64 * u + 64]


def contract(bottom, first, basis, top):
    whole = lambda *dims: pl.BlockSpec(dims, lambda i: (0,) * len(dims))
    return pl.pallas_call(
        contract_kernel,
        grid=(RANK // A_BLOCK,),
        out_shape=jax.ShapeDtypeStruct((4, RANK, RANK), F32),
        in_specs=[
            whole(1024, 256),
            pl.BlockSpec((A_BLOCK, D, D), lambda i: (i, 0, 0)),
            whole(D, D, RANK),
            whole(D * D, 256),
        ],
        out_specs=whole(4, RANK, RANK),
        scratch_shapes=[
            pltpu.VMEM((A_BLOCK * D, D * D), BF16),
            pltpu.VMEM((UNROLL, 256, 256), BF16),
            pltpu.VMEM((RANK * D, 128), F32),
            pltpu.VMEM((RANK * D, 128), F32),
            pltpu.VMEM((RANK, 256), F32),
        ],
        compiler_params=pltpu.CompilerParams(vmem_limit_bytes=56 << 20),
    )(bottom, first, basis, top)


def swapped_pairs(tiles):
    lane = lax.broadcasted_iota(jnp.int32, (8, 128), 1)
    stack = jnp.swapaxes(jnp.stack(tiles, axis=0), 0, 1)
    out = []
    for j in range(4):
        a, b = stack[2 * j], stack[2 * j + 1]
        low = jnp.where(lane < 64, a, pltpu.roll(b, 64, 1))
        high = jnp.where(lane < 64, pltpu.roll(a, 64, 1), b)
        out.append((low, high))
    return out


def partial_kernel(up_ref, down_ref, scale_ref, all_ref, up_out, down_out, up_acc, down_acc):
    blocks = [all_ref[c] for c in range(4)]
    order = [(t // 4 + 2 * y, t % 4) for t in range(8) for y in range(2)]
    right = jnp.concatenate([blocks[c][:, 64 * m : 64 * m + 64] for c, m in order], axis=1)
    up_acc[...] = jnp.dot(up_ref[...], right, preferred_element_type=F32) * scale_ref[...]
    rows = []
    for c, m in order:
        part = blocks[c][:, 64 * m : 64 * m + 64]
        rows.append(jnp.concatenate([part[64 * r : 64 * r + 64] for r in range(8)], axis=1))
    down_acc[...] = lax.dot_general(
        down_ref[...],
        jnp.concatenate(rows, axis=0),
        (((1,), (1,)), ((), ())),
        preferred_element_type=F32,
    )
    for acc, out in ((down_acc, down_out), (up_acc, up_out)):
        for left in range(4):
            for high in range(8):
                at = 64 * left + 8 * high
                pieces = swapped_pairs(
                    [acc[at : at + 8, 128 * t : 128 * t + 128] for t in range(8)]
                )
                for j, piece in enumerate(pieces):
                    out[high, left, 0, :, 128 * j : 128 * j + 128] = jnp.concatenate(
                        piece, axis=0
                    ).astype(BF16)


def partials(up, down, scale, by_cols):
    whole = lambda *dims: pl.BlockSpec(dims, lambda i: (0,) * len(dims))
    out = jax.ShapeDtypeStruct((8, 4, 4, 16, 512), BF16)
    out_spec = pl.BlockSpec((8, 4, 1, 16, 512), lambda i: (0, 0, i, 0, 0))
    return pl.pallas_call(
        partial_kernel,
        grid=(4,),
        out_shape=(out, out),
        in_specs=[
            whole(256, 512),
            whole(256, 512),
            whole(1, 1024),
            pl.BlockSpec((4, 512, 256), lambda i: (i, 0, 0)),
        ],
        out_specs=(out_spec, out_spec),
        scratch_shapes=[pltpu.VMEM((256, 1024), F32), pltpu.VMEM((256, 1024), F32)],
        compiler_params=pltpu.CompilerParams(vmem_limit_bytes=48 << 20),
    )(up, down, scale, by_cols)


def side_kernel(own_ref, inner_ref, rows_ref, lanes_ref, all_ref, out_ref, acc_ref):
    c = pl.program_id(0)

    @pl.when(c == 0)
    def _():
        acc_ref[...] = jnp.zeros_like(acc_ref)

    own = own_ref[:, 0].reshape(256, 256).astype(F32) * inner_ref[0]
    block = all_ref[0]
    order = [s + 4 * y for s in range(4) for y in range(2)]
    right = jnp.concatenate([block[64 * s : 64 * s + 64] for s in order], axis=0)
    acc_ref[...] += lax.dot_general(
        own.astype(BF16), right, (((1,), (1,)), ((), ())), preferred_element_type=F32
    )

    @pl.when(c == 15)
    def _():
        acc_ref[...] = acc_ref[...] * rows_ref[...] * lanes_ref[...]
        for s in range(16):
            tiles = [
                acc_ref[16 * s + 8 * t : 16 * s + 8 * t + 8, 128 * q : 128 * q + 128]
                for t in range(2)
                for q in range(4)
            ]
            pieces = swapped_pairs(tiles)
            for odd in range(2):
                low = jnp.concatenate([pieces[2 * odd][0], pieces[2 * odd + 1][0]], axis=1)
                high = jnp.concatenate([pieces[2 * odd][1], pieces[2 * odd + 1][1]], axis=1)
                for t in range(2):
                    k = 4 * s + 2 * t + odd
                    out_ref[k] = jnp.concatenate(
                        [low[4 * t : 4 * t + 4], high[4 * t : 4 * t + 4]], axis=0
                    )


def side_gram(own, inner, rows, lanes, by_cols):
    whole = lambda *dims: pl.BlockSpec(dims, lambda i: (0,) * len(dims))
    return pl.pallas_call(
        side_kernel,
        grid=(16,),
        out_shape=jax.ShapeDtypeStruct((D, 8, 256), F32),
        in_specs=[
            pl.BlockSpec((8, 1, 32, 256), lambda i: (0, i, 0, 0)),
            pl.BlockSpec((1, 1, 256), lambda i: (i, 0, 0)),
            whole(256, 1),
            whole(1, 512),
            pl.BlockSpec((1, 512, 256), lambda i: (i, 0, 0)),
        ],
        out_specs=whole(D, 8, 256),
        scratch_shapes=[pltpu.VMEM((256, 512), F32)],
        compiler_params=pltpu.CompilerParams(vmem_limit_bytes=48 << 20),
    )(own, inner, rows, lanes, by_cols)


def store_gram(acc_ref, high_ref, low_ref):
    for a_high in range(2):
        for x_high in range(8):
            tiles = []
            for a_low in range(2):
                at = 64 * (2 * a_high + a_low) + 8 * x_high
                for q in range(4):
                    tiles.append(acc_ref[at : at + 8, 128 * q : 128 * q + 128])
            for j, piece in enumerate(swapped_pairs(tiles)):
                high, low = two_parts(jnp.concatenate(piece, axis=0))
                lanes = slice(512 * x_high + 128 * j, 512 * x_high + 128 * j + 128)
                high_ref[16 * a_high : 16 * a_high + 16, lanes] = high
                low_ref[16 * a_high : 16 * a_high + 16, lanes] = low


def left_gram_kernel(up_ref, down_ref, high_ref, low_ref, acc_ref):
    acc_ref[...] = lax.dot_general(
        up_ref[...],
        down_ref[...].reshape(512, 512),
        (((1,), (1,)), ((), ())),
        preferred_element_type=F32,
    )
    store_gram(acc_ref, high_ref, low_ref)


def left_gram(up, down):
    out = jax.ShapeDtypeStruct((256, D * D), BF16)
    out_spec = pl.BlockSpec((32, D * D), lambda i: (i, 0))
    return pl.pallas_call(
        left_gram_kernel,
        grid=(8,),
        out_shape=(out, out),
        in_specs=[
            pl.BlockSpec((256, 512), lambda i: (0, 0)),
            pl.BlockSpec((2, 256, 512), lambda i: (i, 0, 0)),
        ],
        out_specs=(out_spec, out_spec),
        scratch_shapes=[pltpu.VMEM((256, 512), F32)],
        compiler_params=pltpu.CompilerParams(vmem_limit_bytes=48 << 20),
    )(up, down)


def down_gram_kernel(side_ref, down_ref, high_ref, low_ref, acc_ref):
    c = pl.program_id(0)

    @pl.when(c == 0)
    def _():
        acc_ref[...] = jnp.zeros_like(acc_ref)

    side = side_ref[...].astype(F32).reshape(8, 4, 8, 256)
    side = jnp.transpose(side, (1, 0, 2, 3)).reshape(256, 256).astype(BF16)
    acc_ref[...] += lax.dot_general(
        side, down_ref[0], (((0,), (0,)), ((), ())), preferred_element_type=F32
    )

    @pl.when(c == 15)
    def _():
        store_gram(acc_ref, high_ref, low_ref)


def down_gram(side, down):
    out = jax.ShapeDtypeStruct((32, D * D), BF16)
    out_spec = pl.BlockSpec((32, D * D), lambda i: (0, 0))
    return pl.pallas_call(
        down_gram_kernel,
        grid=(16,),
        out_shape=(out, out),
        in_specs=[
            pl.BlockSpec((8, 32, 256), lambda i: (0, i, 0)),
            pl.BlockSpec((1, 256, 512), lambda i: (i, 0, 0)),
        ],
        out_specs=(out_spec, out_spec),
        scratch_shapes=[pltpu.VMEM((256, 512), F32)],
        compiler_params=pltpu.CompilerParams(vmem_limit_bytes=48 << 20),
    )(side, down)


def body(tensor, bond_weights, start_blocks):
    row_index = lax.axis_index("row")
    horizontal = bond_weights[0]
    vertical = bond_weights[1]
    horiz_rows = lax.dynamic_slice_in_dim(horizontal, row_index * 8, 8)
    grid = tensor.reshape(4, 8, D, D)
    flat = jnp.transpose(grid, (1, 2, 0, 3)).reshape(512, 256)
    by_cols = lax.all_gather(flat, COL)

    wide = grid.astype(F32)
    square = vertical * vertical
    rows_square = (horiz_rows * horiz_rows)[None, :, None, None]
    up_scale = rows_square * square[:, None] * vertical[None, :]
    own_up = jnp.transpose((wide * up_scale).astype(BF16), (0, 3, 1, 2)).reshape(256, 512)
    own_down = jnp.transpose((wide * rows_square * square).astype(BF16), (0, 2, 1, 3))
    own_down = own_down.reshape(256, 512)
    side_piece = jnp.swapaxes(flat.reshape(8, 16, 4, 256), 0, 1).reshape(16, 32, 256)
    weighted = (wide * vertical[:, None]).astype(BF16)
    top_piece = jnp.transpose(weighted.reshape(4, 8, D, 16, 4), (3, 4, 1, 2, 0))
    pieces = jnp.concatenate([side_piece, top_piece.reshape(16, 32, 256)], axis=1)
    pieces = lax.all_to_all(pieces, COL, 0, 0, tiled=True)
    side_own = from_everyone(pieces[:, :32], "row")
    top_rows = jnp.transpose(pieces[:, 32:].reshape(16, 32, D, 4), (1, 2, 0, 3))
    top_rows = top_rows.reshape(32, D * D)

    lane_scale = jnp.tile(vertical, 16)[None, :]
    part_up, part_down = partials(own_up, own_down, lane_scale, by_cols)
    left_down = lax.psum_scatter(
        part_down.reshape(8, 4, D, 512), "row", scatter_dimension=0, tiled=True
    )
    part_up, left_down = lax.optimization_barrier((part_up, left_down))
    left_up = lax.psum_scatter(
        part_up.reshape(8, 4, D, 512), "row", scatter_dimension=0, tiled=True
    )
    down_all = lax.all_gather(left_down.reshape(256, 512), COL)

    inner = ((horizontal * horizontal)[:, None] * square[None, :]).reshape(16, 1, 256)
    lanes = jnp.repeat(jnp.transpose(horiz_rows.reshape(2, 4)).reshape(8), D)[None, :]
    side = side_gram(side_own, inner, jnp.repeat(horizontal, 4)[:, None], lanes, by_cols)
    side_all = from_everyone(side.astype(BF16).reshape(512, 256), "row")

    slab_part = by_cols.reshape(16, 8, D, 4, D)[:, :, :8]
    slab_part = jnp.transpose(slab_part, (2, 0, 1, 3, 4)).reshape(8, 128, 256)
    slab = lax.all_to_all(slab_part, "row", split_axis=0, concat_axis=0, tiled=True)
    bottom = jnp.transpose(slab.reshape(8, 16, 8, 4, 16, 4), (4, 0, 2, 5, 1, 3))
    bottom = bottom.reshape(1024, 256)

    first_vectors = from_everyone(start_blocks.reshape(32, 2 * RANK), ROW_COL)
    grams = (
        *left_gram(left_up.reshape(256, 512), down_all),
        *down_gram(side_all, down_all),
    )
    top_rows, grams = lax.optimization_barrier((top_rows, grams))
    top = lax.all_gather(top_rows, "row").reshape(8, 4, 8, D * D)
    top = jnp.transpose(top, (3, 1, 0, 2)).reshape(D * D, 256)
    z_outs = (
        jax.ShapeDtypeStruct((8, 16, 2 * RANK), F32),
        jax.ShapeDtypeStruct((32, 2 * RANK), F32),
    )
    inv_out = jax.ShapeDtypeStruct((2 * RANK, 2 * RANK), F32)

    def local_images(z_left, z_down):
        z_left = jnp.sum(lax.all_to_all(z_left, "row", 0, 0, tiled=True), axis=0)
        z_left = jnp.concatenate([z_left[:, :RANK], z_left[:, RANK:]], axis=0)
        z = jnp.concatenate([z_left, z_down[:, RANK:]], axis=1)
        z = jnp.transpose(z.reshape(2, 2, 2, 4, 2 * RANK), (0, 2, 3, 1, 4))
        return z.reshape(32, 2 * RANK)

    def everywhere(y):
        return from_everyone(y, ROW_COL).reshape(8, D, 8, 2 * RANK)

    def apply(y, inverse):
        return lax.dot_general(y, inverse, (((1,), (1,)), ((), ())), precision=HIGHEST)

    y = local_images(
        *vmem_call(first_kernel, z_outs, (first_vectors.reshape(8, D, 8, 2 * RANK), *grams))
    )
    for _ in range(2):
        z_left, z_down, inverse = vmem_call(
            next_kernel, (*z_outs, inv_out), (everywhere(y), *grams)
        )
        y = apply(local_images(z_left, z_down), inverse)
    basis, inverse = vmem_call(
        last_kernel, (jax.ShapeDtypeStruct((D * D, RANK), BF16), inv_out), (everywhere(y),)
    )
    projectors = apply(y, inverse).reshape(4, 8, 2 * RANK)
    basis = basis.reshape(D, D, RANK)
    new_tensor = contract(bottom, jnp.transpose(basis, (2, 0, 1)), basis, top)
    return (projectors, new_tensor.reshape(4, 1, RANK * RANK))


def solution(mesh):
    torus = Mesh(mesh.devices.reshape(mesh.shape["row"], 4, 4), ("row", "col_0", "col_1"))
    placed = (P(COL, "row", None), P(), P(COL, "row", None))
    return jax.shard_map(
        body,
        mesh=torus,
        in_specs=placed,
        out_specs=(P(COL, "row", None), P(COL, "row", None)),
        check_vma=False,
    )
```

```python
import jax
import jax.numpy as jnp
from jax import lax
from jax.experimental import pallas as pl
from jax.experimental.pallas import tpu as pltpu
from jax.sharding import Mesh
from jax.sharding import PartitionSpec as P

D = 64
RANK = 64
COL = ("col_0", "col_1")
ROW = ("z", "core")
SAME_CORE = ("z", "col_0", "col_1")
HIGHEST = lax.Precision.HIGHEST
F32 = jnp.float32
BF16 = jnp.bfloat16
A_BLOCK = 16
UNROLL = 4


def from_everyone(shard, axis):
    copies = jnp.broadcast_to(shard, (lax.axis_size(axis), *shard.shape))
    return lax.all_to_all(copies, axis, split_axis=0, concat_axis=0, tiled=True)


def two_parts(x):
    high = x.astype(BF16)
    return high, (x - high.astype(F32)).astype(BF16)


def in_index_order(core_ref, mine_ref, other_ref):
    first = core_ref[0] == 0
    mine, other = mine_ref[...], other_ref[...]
    halves = [jnp.where(first, mine, other), jnp.where(first, other, mine)]
    y = jnp.stack([h.reshape(4, D, 8, 2 * RANK) for h in halves], axis=1)
    y = jnp.transpose(y.reshape(8, D, 8, 2 * RANK), (1, 0, 2, 3))
    return y.reshape(D * D, 2 * RANK)


def inverse_factors(mats):
    n = RANK
    rows_at = lax.broadcasted_iota(jnp.int32, (8, 2 * n), 0)
    lanes_at = lax.broadcasted_iota(jnp.int32, (8, 2 * n), 1)
    sets = []
    for c in mats:
        blocks = []
        for i in range(n // 8):
            unit = (lanes_at == rows_at + (n + 8 * i)).astype(F32)
            part = jnp.concatenate([c[8 * i : 8 * i + 8], jnp.zeros((8, n), F32)], axis=1)
            blocks.append(part + unit)
        sets.append(blocks)
    for k in range(n):
        b, s = divmod(k, 8)
        for blocks in sets:
            row = blocks[b][s : s + 1, :]
            scaled = row / row[:, k : k + 1]
            for i in range(b, n // 8):
                column = blocks[i][:, k : k + 1]
                step = column * scaled
                if i == b:
                    step = jnp.where(rows_at > s, step, 0.0)
                blocks[i] = blocks[i] - step
    out = []
    for blocks in sets:
        done = []
        for i in range(n // 8):
            own = jnp.where(lanes_at == rows_at + 8 * i, blocks[i], 0.0)
            pivot = jnp.sum(own, axis=1, keepdims=True)
            done.append(blocks[i][:, n:] / jnp.sqrt(pivot))
        out.append(jnp.concatenate(done, axis=0))
    return out


def correlation(y):
    return lax.dot_general(
        y, y, (((0,), (0,)), ((), ())), precision=HIGHEST, preferred_element_type=F32
    )


def factors_of(c):
    return inverse_factors([c[:RANK, :RANK], c[RANK:, RANK:]])


def store_inverse(inv_ref, left, down):
    zero = jnp.zeros((RANK, RANK), F32)
    inv_ref[:RANK, :] = jnp.concatenate([left, zero], axis=1)
    inv_ref[RANK:, :] = jnp.concatenate([zero, down], axis=1)


def images_of(y, gl_high, gl_low, gd_high, gd_low, zl_ref, zd_ref):
    y_high, y_low = two_parts(y)
    both = jnp.concatenate([y_high, y_low], axis=1)

    def product(high, low):
        main = jnp.dot(high[...], both, preferred_element_type=F32)
        rest = jnp.dot(low[...], y_high, preferred_element_type=F32)
        return main[:, : 2 * RANK] + main[:, 2 * RANK :] + rest

    z = product(gl_high, gl_low)[:, :RANK].reshape(8, 32, RANK)
    zl_ref[...] = jnp.concatenate([z[:, :16], z[:, 16:]], axis=2)
    zd_ref[...] = product(gd_high, gd_low)


def images_kernel(core_ref, mine_ref, other_ref, glh, gll, gdh, gdl, zl_ref, zd_ref):
    y = in_index_order(core_ref, mine_ref, other_ref)
    images_of(y, glh, gll, gdh, gdl, zl_ref, zd_ref)


def factor_kernel(mine_ref, other_ref, inv_ref):
    c = correlation(mine_ref[...]) + correlation(other_ref[...])
    store_inverse(inv_ref, *factors_of(c))


def last_kernel(core_ref, mine_ref, other_ref, basis_ref, mixed_ref, inv_ref):
    c = correlation(mine_ref[...]) + correlation(other_ref[...])
    left, down = factors_of(c)
    store_inverse(inv_ref, left, down)
    y = in_index_order(core_ref, mine_ref, other_ref)
    basis = lax.dot_general(
        y[:, :RANK], left, (((1,), (1,)), ((), ())), precision=HIGHEST, preferred_element_type=F32
    )
    basis = basis.astype(BF16)
    basis_ref[...] = basis
    to = lax.broadcasted_iota(jnp.int32, (256, 256), 0)
    at = lax.broadcasted_iota(jnp.int32, (256, 256), 1)
    source = (to // 64) * 64 + (to % 16) * 4 + (to % 64) // 16
    picks = (at == source).astype(F32).astype(BF16)
    for q in range(16):
        rows = slice(256 * q, 256 * q + 256)
        mixed_ref[rows, :] = jnp.dot(
            picks, basis[rows], preferred_element_type=F32
        ).astype(BF16)


def folded(block):
    by_x = jnp.swapaxes(block, 0, 1)
    rows = []
    for x in range(8):
        lanes = [by_x[x][:, 64 * l : 64 * l + 64] for l in range(4)]
        turned = jnp.concatenate(lanes, axis=0).T
        rows.append(jnp.concatenate([turned[16 * q : 16 * q + 16] for q in range(4)], axis=1))
    return jnp.swapaxes(jnp.stack(rows, axis=0), 0, 1)


def fold_kernel(slab_ref, top_ref, bottom_out, top_out):
    for g in range(4):
        pair = [slab_ref[2 * g + h].astype(F32).reshape(16, 8, 256) for h in range(2)]
        both = jnp.concatenate([folded(p) for p in pair], axis=1)
        bottom_out[:, 16 * g : 16 * g + 16, :] = both.astype(BF16)
    for g in range(2):
        block = top_ref[:, 16 * g : 16 * g + 16, :].astype(F32)
        both = jnp.concatenate([folded(block[:, :8]), folded(block[:, 8:])], axis=1)
        top_out[:, 16 * g : 16 * g + 16, :] = both.astype(BF16)


def vmem_call(kernel, outs, args, scalars=0, limit=48):
    spec = pl.BlockSpec(memory_space=pltpu.VMEM)
    scalar = pl.BlockSpec(memory_space=pltpu.SMEM)
    return pl.pallas_call(
        kernel,
        out_shape=tuple(outs),
        in_specs=[scalar] * scalars + [spec] * (len(args) - scalars),
        out_specs=tuple([spec] * len(outs)),
        compiler_params=pltpu.CompilerParams(vmem_limit_bytes=limit << 20),
    )(*args)


def fill_diagonal(diag_ref, slot, block):
    for i in range(4):
        diag_ref[slot, 64 * i : 64 * i + 64, 64 * i : 64 * i + 64] = block


def contract_kernel(
    bottom_ref, first_ref, basis_ref, tops_ref, out_ref, top_ref, wide_ref, diag_ref, even_ref, odd_ref, sum_ref
):
    step_id = pl.program_id(0)
    rows_here = A_BLOCK * D

    @pl.when(step_id == 0)
    def _():
        diag_ref[...] = jnp.zeros_like(diag_ref)
        for q in range(16):
            part = tops_ref[:, q].astype(F32).reshape(8, 4, 8, 256)
            part = jnp.transpose(part, (1, 0, 2, 3)).reshape(256, 256)
            top_ref[256 * q : 256 * q + 256, :] = part.T.astype(BF16)

    bottom = bottom_ref[...]

    def sections(group, carry):
        for j in range(UNROLL):
            fill_diagonal(diag_ref, j, first_ref[group * UNROLL + j])
        for j in range(UNROLL):
            section = jnp.dot(bottom, diag_ref[j], preferred_element_type=F32).astype(BF16)
            start = pl.multiple_of((group * UNROLL + j) * D, D)
            for q in range(16):
                wide_ref[pl.ds(start, D), 256 * q : 256 * q + 256] = section[64 * q : 64 * q + 64]
        return carry

    lax.fori_loop(0, A_BLOCK // UNROLL, sections, 0)
    second = jnp.dot(wide_ref[...], top_ref[...], preferred_element_type=F32)
    second = second.astype(BF16).astype(F32)
    base = pl.multiple_of(step_id * rows_here, rows_here)
    even_ref[pl.ds(base, rows_here), :] = second[:, :128]
    odd_ref[pl.ds(base, rows_here), :] = second[:, 128:]

    @pl.when(step_id == RANK // A_BLOCK - 1)
    def _():
        sum_ref[...] = jnp.zeros_like(sum_ref)

        def products(group, carry):
            total = sum_ref[...]
            for j in range(UNROLL):
                fill_diagonal(diag_ref, j, basis_ref[group * UNROLL + j])
            for j in range(UNROLL):
                picked = pl.ds(group * UNROLL + j, RANK, stride=D)
                rows = jnp.concatenate([even_ref[picked, :], odd_ref[picked, :]], axis=1)
                total = total + jnp.dot(
                    rows.astype(BF16), diag_ref[j], preferred_element_type=F32
                )
            sum_ref[...] = total
            return carry

        lax.fori_loop(0, D // UNROLL, products, 0)
        for u in range(4):
            out_ref[u] = sum_ref[:, 64 * u : 64 * u + 64]


def contract(bottom, first, basis, top):
    whole = lambda *dims: pl.BlockSpec(dims, lambda i: (0,) * len(dims))
    return pl.pallas_call(
        contract_kernel,
        grid=(RANK // A_BLOCK,),
        out_shape=jax.ShapeDtypeStruct((4, RANK, RANK), F32),
        in_specs=[
            whole(1024, 256),
            pl.BlockSpec((A_BLOCK, D, D), lambda i: (i, 0, 0)),
            whole(D, D, RANK),
            whole(8, 16, 32, 256),
        ],
        out_specs=whole(4, RANK, RANK),
        scratch_shapes=[
            pltpu.VMEM((D * D, 256), BF16),
            pltpu.VMEM((A_BLOCK * D, D * D), BF16),
            pltpu.VMEM((UNROLL, 256, 256), BF16),
            pltpu.VMEM((RANK * D, 128), F32),
            pltpu.VMEM((RANK * D, 128), F32),
            pltpu.VMEM((RANK, 256), F32),
        ],
        compiler_params=pltpu.CompilerParams(vmem_limit_bytes=56 << 20),
    )(bottom, first, basis, top)


def swapped_pairs(tiles):
    lane = lax.broadcasted_iota(jnp.int32, (8, 128), 1)
    stack = jnp.swapaxes(jnp.stack(tiles, axis=0), 0, 1)
    out = []
    for j in range(4):
        a, b = stack[2 * j], stack[2 * j + 1]
        low = jnp.where(lane < 64, a, pltpu.roll(b, 64, 1))
        high = jnp.where(lane < 64, pltpu.roll(a, 64, 1), b)
        out.append((low, high))
    return out


def partial_kernel(up_ref, down_ref, scale_ref, all_ref, out_ref, up_acc, down_acc):
    blocks = [all_ref[c] for c in range(4)]
    order = [(t // 4 + 2 * y, t % 4) for t in range(8) for y in range(2)]
    right = jnp.concatenate([blocks[c][:, 64 * m : 64 * m + 64] for c, m in order], axis=1)
    up_acc[...] = jnp.dot(up_ref[...], right, preferred_element_type=F32) * scale_ref[...]
    rows = []
    for c, m in order:
        part = blocks[c][:, 64 * m : 64 * m + 64]
        rows.append(jnp.concatenate([part[64 * r : 64 * r + 64] for r in range(8)], axis=1))
    down_acc[...] = lax.dot_general(
        down_ref[...],
        jnp.concatenate(rows, axis=0),
        (((1,), (1,)), ((), ())),
        preferred_element_type=F32,
    )
    for which, acc in enumerate((up_acc, down_acc)):
        for left in range(4):
            for high in range(8):
                at = 64 * left + 8 * high
                pieces = swapped_pairs(
                    [acc[at : at + 8, 128 * t : 128 * t + 128] for t in range(8)]
                )
                for j, piece in enumerate(pieces):
                    out_ref[high, which, left, 0, :, 128 * j : 128 * j + 128] = jnp.concatenate(
                        piece, axis=0
                    ).astype(BF16)


def partials(up, down, scale, by_cols):
    whole = lambda *dims: pl.BlockSpec(dims, lambda i: (0,) * len(dims))
    return pl.pallas_call(
        partial_kernel,
        grid=(4,),
        out_shape=jax.ShapeDtypeStruct((8, 2, 4, 4, 16, 512), BF16),
        in_specs=[
            whole(256, 512),
            whole(256, 512),
            whole(1, 1024),
            pl.BlockSpec((4, 512, 256), lambda i: (i, 0, 0)),
        ],
        out_specs=pl.BlockSpec((8, 2, 4, 1, 16, 512), lambda i: (0, 0, 0, i, 0, 0)),
        scratch_shapes=[pltpu.VMEM((256, 1024), F32), pltpu.VMEM((256, 1024), F32)],
        compiler_params=pltpu.CompilerParams(vmem_limit_bytes=48 << 20),
    )(up, down, scale, by_cols)


def side_kernel(own_ref, inner_ref, rows_ref, lanes_ref, all_ref, out_ref, acc_ref):
    c = pl.program_id(0)

    @pl.when(c == 0)
    def _():
        acc_ref[...] = jnp.zeros_like(acc_ref)

    own = own_ref[:, 0].reshape(256, 256).astype(F32) * inner_ref[0]
    block = all_ref[0]
    order = [s + 4 * y for s in range(4) for y in range(2)]
    right = jnp.concatenate([block[64 * s : 64 * s + 64] for s in order], axis=0)
    acc_ref[...] += lax.dot_general(
        own.astype(BF16), right, (((1,), (1,)), ((), ())), preferred_element_type=F32
    )

    @pl.when(c == 15)
    def _():
        acc_ref[...] = acc_ref[...] * rows_ref[...] * lanes_ref[...]
        for s in range(16):
            tiles = [
                acc_ref[16 * s + 8 * t : 16 * s + 8 * t + 8, 128 * q : 128 * q + 128]
                for t in range(2)
                for q in range(4)
            ]
            pieces = swapped_pairs(tiles)
            for odd in range(2):
                low = jnp.concatenate([pieces[2 * odd][0], pieces[2 * odd + 1][0]], axis=1)
                high = jnp.concatenate([pieces[2 * odd][1], pieces[2 * odd + 1][1]], axis=1)
                for t in range(2):
                    k = 4 * s + 2 * t + odd
                    out_ref[k] = jnp.concatenate(
                        [low[4 * t : 4 * t + 4], high[4 * t : 4 * t + 4]], axis=0
                    )


def side_gram(own, inner, rows, lanes, by_cols):
    whole = lambda *dims: pl.BlockSpec(dims, lambda i: (0,) * len(dims))
    return pl.pallas_call(
        side_kernel,
        grid=(16,),
        out_shape=jax.ShapeDtypeStruct((D, 8, 256), F32),
        in_specs=[
            pl.BlockSpec((8, 1, 32, 256), lambda i: (0, i, 0, 0)),
            pl.BlockSpec((1, 1, 256), lambda i: (i, 0, 0)),
            whole(256, 1),
            whole(1, 512),
            pl.BlockSpec((1, 512, 256), lambda i: (i, 0, 0)),
        ],
        out_specs=whole(D, 8, 256),
        scratch_shapes=[pltpu.VMEM((256, 512), F32)],
        compiler_params=pltpu.CompilerParams(vmem_limit_bytes=48 << 20),
    )(own, inner, rows, lanes, by_cols)


def store_gram(acc_ref, high_ref, low_ref):
    for a_high in range(2):
        for x_high in range(8):
            tiles = []
            for a_low in range(2):
                at = 64 * (2 * a_high + a_low) + 8 * x_high
                for q in range(4):
                    tiles.append(acc_ref[at : at + 8, 128 * q : 128 * q + 128])
            for j, piece in enumerate(swapped_pairs(tiles)):
                high, low = two_parts(jnp.concatenate(piece, axis=0))
                lanes = slice(512 * x_high + 128 * j, 512 * x_high + 128 * j + 128)
                high_ref[16 * a_high : 16 * a_high + 16, lanes] = high
                low_ref[16 * a_high : 16 * a_high + 16, lanes] = low


def left_gram_kernel(up_ref, down_ref, high_ref, low_ref, acc_ref):
    acc_ref[...] = lax.dot_general(
        up_ref[...],
        down_ref[...].reshape(512, 512),
        (((1,), (1,)), ((), ())),
        preferred_element_type=F32,
    )
    store_gram(acc_ref, high_ref, low_ref)


def left_gram(up, down):
    out = jax.ShapeDtypeStruct((256, D * D), BF16)
    out_spec = pl.BlockSpec((32, D * D), lambda i: (i, 0))
    return pl.pallas_call(
        left_gram_kernel,
        grid=(8,),
        out_shape=(out, out),
        in_specs=[
            pl.BlockSpec((256, 512), lambda i: (0, 0)),
            pl.BlockSpec((2, 256, 512), lambda i: (i, 0, 0)),
        ],
        out_specs=(out_spec, out_spec),
        scratch_shapes=[pltpu.VMEM((256, 512), F32)],
        compiler_params=pltpu.CompilerParams(vmem_limit_bytes=48 << 20),
    )(up, down)


def down_gram_kernel(side_ref, down_ref, high_ref, low_ref, acc_ref):
    c = pl.program_id(0)

    @pl.when(c == 0)
    def _():
        acc_ref[...] = jnp.zeros_like(acc_ref)

    side = side_ref[...].astype(F32).reshape(8, 4, 8, 256)
    side = jnp.transpose(side, (1, 0, 2, 3)).reshape(256, 256).astype(BF16)
    acc_ref[...] += lax.dot_general(
        side, down_ref[0], (((0,), (0,)), ((), ())), preferred_element_type=F32
    )

    @pl.when(c == 15)
    def _():
        store_gram(acc_ref, high_ref, low_ref)


def down_gram(side, down):
    out = jax.ShapeDtypeStruct((32, D * D), BF16)
    out_spec = pl.BlockSpec((32, D * D), lambda i: (0, 0))
    return pl.pallas_call(
        down_gram_kernel,
        grid=(16,),
        out_shape=(out, out),
        in_specs=[
            pl.BlockSpec((8, 32, 256), lambda i: (0, i, 0)),
            pl.BlockSpec((1, 256, 512), lambda i: (i, 0, 0)),
        ],
        out_specs=(out_spec, out_spec),
        scratch_shapes=[pltpu.VMEM((256, 512), F32)],
        compiler_params=pltpu.CompilerParams(vmem_limit_bytes=48 << 20),
    )(side, down)


def body(tensor, bond_weights, start_blocks):
    row_index = lax.axis_index(ROW)
    core = lax.axis_index("core")
    horizontal = bond_weights[0]
    vertical = bond_weights[1]
    horiz_rows = lax.dynamic_slice_in_dim(horizontal, row_index * 8, 8)
    grid = tensor.reshape(4, 8, D, D)
    flat = jnp.transpose(grid, (1, 2, 0, 3)).reshape(512, 256)
    by_cols = lax.all_gather(flat, COL)

    wide = grid.astype(F32)
    square = vertical * vertical
    rows_square = (horiz_rows * horiz_rows)[None, :, None, None]
    up_scale = rows_square * square[:, None] * vertical[None, :]
    own_up = jnp.transpose((wide * up_scale).astype(BF16), (0, 3, 1, 2)).reshape(256, 512)
    own_down = jnp.transpose((wide * rows_square * square).astype(BF16), (0, 2, 1, 3))
    own_down = own_down.reshape(256, 512)
    side_piece = jnp.swapaxes(flat.reshape(8, 16, 4, 256), 0, 1).reshape(16, 32, 256)
    weighted = (wide * vertical[:, None]).astype(BF16)
    top_piece = jnp.transpose(weighted.reshape(4, 8, D, 16, 4), (3, 4, 1, 0, 2))
    pieces = jnp.concatenate([side_piece, top_piece.reshape(16, 32, 256)], axis=1)
    pieces = lax.all_to_all(pieces, COL, 0, 0, tiled=True)
    side_own = from_everyone(pieces[:, :32], ROW)

    by_cols, side_own = lax.optimization_barrier((by_cols, side_own))
    lane_scale = jnp.tile(vertical, 16)[None, :]
    parts = partials(own_up, own_down, lane_scale, by_cols).reshape(8, 2, 4, D, 512)
    left_both = lax.psum_scatter(parts, ROW, scatter_dimension=0, tiled=True)

    inner = ((horizontal * horizontal)[:, None] * square[None, :]).reshape(16, 1, 256)
    lanes = jnp.repeat(jnp.transpose(horiz_rows.reshape(2, 4)).reshape(8), D)[None, :]
    side = side_gram(side_own, inner, jnp.repeat(horizontal, 4)[:, None], lanes, by_cols)
    side_all = from_everyone(side.astype(BF16).reshape(512, 256), ROW)
    left_both, side_all = lax.optimization_barrier((left_both, side_all))
    left_both = left_both.reshape(2, 256, 512)
    down_all = lax.all_gather(left_both[1], COL)

    def everywhere(y):
        mine = lax.all_to_all(
            jnp.broadcast_to(y, (64, 32, 2 * RANK)), SAME_CORE, 0, 0, tiled=True
        ).reshape(2048, 2 * RANK)
        return mine, lax.ppermute(mine, "core", [(0, 1), (1, 0)])

    slab_part = by_cols.reshape(16, 8, D, 256)[:, :, :8]
    slab_part = jnp.transpose(slab_part, (2, 0, 1, 3)).reshape(8, 128, 256)
    slab = lax.all_to_all(slab_part, ROW, split_axis=0, concat_axis=0, tiled=True)
    bottom, top_rows = vmem_call(
        fold_kernel,
        (
            jax.ShapeDtypeStruct((16, D, 256), BF16),
            jax.ShapeDtypeStruct((16, 32, 256), BF16),
        ),
        (slab, pieces[:, 32:]),
    )
    first_vectors = everywhere(start_blocks.reshape(32, 2 * RANK))
    down_all, bottom, top_rows, first_vectors = lax.optimization_barrier(
        (down_all, bottom, top_rows, first_vectors)
    )
    grams = (*left_gram(left_both[0], down_all), *down_gram(side_all, down_all))
    top_rows, grams = lax.optimization_barrier((top_rows, grams))
    top = lax.all_gather(top_rows, ROW)
    z_outs = (
        jax.ShapeDtypeStruct((8, 16, 2 * RANK), F32),
        jax.ShapeDtypeStruct((32, 2 * RANK), F32),
    )
    inv_out = jax.ShapeDtypeStruct((2 * RANK, 2 * RANK), F32)

    def local_images(z_left, z_down):
        z_left = jnp.sum(lax.all_to_all(z_left, ROW, 0, 0, tiled=True), axis=0)
        z_left = jnp.concatenate([z_left[:, :RANK], z_left[:, RANK:]], axis=0)
        z = jnp.concatenate([z_left, z_down[:, RANK:]], axis=1)
        z = jnp.transpose(z.reshape(2, 2, 2, 4, 2 * RANK), (0, 2, 3, 1, 4))
        return z.reshape(32, 2 * RANK)

    def apply(y, inverse):
        return lax.dot_general(y, inverse, (((1,), (1,)), ((), ())), precision=HIGHEST)

    where = jnp.reshape(core, (1,)).astype(jnp.int32)
    vectors = first_vectors
    for step in range(3):
        y = local_images(*vmem_call(images_kernel, z_outs, (where, *vectors, *grams), 1))
        if step:
            y = apply(y, vmem_call(factor_kernel, (inv_out,), vectors)[0])
        vectors = everywhere(y)
    basis_out = jax.ShapeDtypeStruct((D * D, RANK), BF16)
    basis, mixed, inverse = vmem_call(
        last_kernel, (basis_out, basis_out, inv_out), (where, *vectors), 1
    )
    projectors = apply(y, inverse).reshape(4, 8, 2 * RANK)
    first = jnp.transpose(mixed.reshape(16, 4, D, RANK), (3, 1, 0, 2)).reshape(RANK, D, D)
    new_tensor = contract(bottom.reshape(1024, 256), first, basis.reshape(D, D, RANK), top)
    return (projectors, new_tensor.reshape(4, 1, RANK * RANK))


def solution(mesh):
    axes = ("z", "core", "col_0", "col_1")
    torus = Mesh(mesh.devices.reshape(mesh.shape["row"] // 2, 2, 4, 4), axes)
    placed = (P(COL, ROW, None), P(), P(COL, ROW, None))
    return jax.shard_map(
        body,
        mesh=torus,
        in_specs=placed,
        out_specs=(P(COL, ROW, None), P(COL, ROW, None)),
        check_vma=False,
    )
```

```python
import jax
import jax.numpy as jnp
from jax import lax
from jax.experimental import pallas as pl
from jax.experimental.pallas import tpu as pltpu
from jax.sharding import Mesh
from jax.sharding import PartitionSpec as P

D = 64
RANK = 64
COL = ("col_0", "col_1")
ROW = ("z", "core")
SAME_CORE = ("z", "col_0", "col_1")
HIGHEST = lax.Precision.HIGHEST
F32 = jnp.float32
BF16 = jnp.bfloat16
A_BLOCK = 16
UNROLL = 4


def from_everyone(shard, axis):
    copies = jnp.broadcast_to(shard, (lax.axis_size(axis), *shard.shape))
    return lax.all_to_all(copies, axis, split_axis=0, concat_axis=0, tiled=True)


def two_parts(x):
    high = x.astype(BF16)
    return high, (x - high.astype(F32)).astype(BF16)


def by_core(core_ref, mine, other):
    first = core_ref[0] == 0
    return jnp.where(first, mine, other), jnp.where(first, other, mine)


def in_index_order(core_ref, mine_ref, other_ref):
    halves = by_core(core_ref, mine_ref[...], other_ref[...])
    y = jnp.stack([h.reshape(4, D, 8, 2 * RANK) for h in halves], axis=1)
    y = jnp.transpose(y.reshape(8, D, 8, 2 * RANK), (1, 0, 2, 3))
    return y.reshape(D * D, 2 * RANK)


def inverse_factors(mats):
    n = RANK
    rows_at = lax.broadcasted_iota(jnp.int32, (8, 2 * n), 0)
    lanes_at = lax.broadcasted_iota(jnp.int32, (8, 2 * n), 1)
    sets = []
    for c in mats:
        blocks = []
        for i in range(n // 8):
            unit = (lanes_at == rows_at + (n + 8 * i)).astype(F32)
            part = jnp.concatenate([c[8 * i : 8 * i + 8], jnp.zeros((8, n), F32)], axis=1)
            blocks.append(part + unit)
        sets.append(blocks)
    for k in range(n):
        b, s = divmod(k, 8)
        for blocks in sets:
            row = blocks[b][s : s + 1, :]
            scaled = row / row[:, k : k + 1]
            for i in range(b, n // 8):
                column = blocks[i][:, k : k + 1]
                step = column * scaled
                if i == b:
                    step = jnp.where(rows_at > s, step, 0.0)
                blocks[i] = blocks[i] - step
    out = []
    for blocks in sets:
        done = []
        for i in range(n // 8):
            own = jnp.where(lanes_at == rows_at + 8 * i, blocks[i], 0.0)
            pivot = jnp.sum(own, axis=1, keepdims=True)
            done.append(blocks[i][:, n:] / jnp.sqrt(pivot))
        out.append(jnp.concatenate(done, axis=0))
    return out


def correlation(y):
    return lax.dot_general(
        y, y, (((0,), (0,)), ((), ())), precision=HIGHEST, preferred_element_type=F32
    )


def factors_of(c):
    return inverse_factors([c[:RANK, :RANK], c[RANK:, RANK:]])


def store_inverse(inv_ref, left, down):
    zero = jnp.zeros((RANK, RANK), F32)
    inv_ref[:RANK, :] = jnp.concatenate([left, zero], axis=1)
    inv_ref[RANK:, :] = jnp.concatenate([zero, down], axis=1)


def images_of(y, gl_high, gl_low, gd_high, gd_low, zl_ref, zd_ref):
    y_high, y_low = two_parts(y)
    both = jnp.concatenate([y_high, y_low], axis=1)

    def product(high, low):
        main = jnp.dot(high[...], both, preferred_element_type=F32)
        rest = jnp.dot(low[...], y_high, preferred_element_type=F32)
        return main[:, : 2 * RANK] + main[:, 2 * RANK :] + rest

    z = product(gl_high, gl_low)[:, :RANK].reshape(8, 32, RANK)
    zl_ref[...] = jnp.concatenate([z[:, :16], z[:, 16:]], axis=2)
    zd_ref[...] = product(gd_high, gd_low)


def images_kernel(core_ref, mine_ref, other_ref, glh, gll, gdh, gdl, zl_ref, zd_ref):
    y = in_index_order(core_ref, mine_ref, other_ref)
    images_of(y, glh, gll, gdh, gdl, zl_ref, zd_ref)


def factor_kernel(mine_ref, other_ref, inv_ref):
    c = correlation(mine_ref[...]) + correlation(other_ref[...])
    store_inverse(inv_ref, *factors_of(c))


def last_kernel(core_ref, mine_ref, other_ref, basis_ref, mixed_ref, inv_ref):
    c = correlation(mine_ref[...]) + correlation(other_ref[...])
    left, down = factors_of(c)
    store_inverse(inv_ref, left, down)
    y = in_index_order(core_ref, mine_ref, other_ref)
    basis = lax.dot_general(
        y[:, :RANK], left, (((1,), (1,)), ((), ())), precision=HIGHEST, preferred_element_type=F32
    )
    basis = basis.astype(BF16)
    basis_ref[...] = basis
    to = lax.broadcasted_iota(jnp.int32, (256, 256), 0)
    at = lax.broadcasted_iota(jnp.int32, (256, 256), 1)
    source = (to // 64) * 64 + (to % 16) * 4 + (to % 64) // 16
    picks = (at == source).astype(F32).astype(BF16)
    for q in range(16):
        rows = slice(256 * q, 256 * q + 256)
        mixed_ref[rows, :] = jnp.dot(
            picks, basis[rows], preferred_element_type=F32
        ).astype(BF16)


def folded(columns):
    rows = []
    for x in range(0, 8, 2):
        turned = jnp.concatenate(columns[x : x + 2], axis=1).T
        for h in range(2):
            parts = [turned[64 * h + 16 * q : 64 * h + 16 * q + 16] for q in range(4)]
            rows.append(jnp.concatenate(parts, axis=1))
    return jnp.swapaxes(jnp.stack(rows, axis=0), 0, 1)


def fold_kernel(slab_ref, top_ref, bottom_out, top_out):
    for g in range(4):
        both = []
        for h in range(2):
            block = slab_ref[2 * g + h].astype(F32).reshape(16, 8, 256)
            by_r = jnp.swapaxes(block, 0, 1)
            both.append(
                folded(
                    [
                        jnp.concatenate(
                            [by_r[r][:, 64 * l : 64 * l + 64] for l in range(4)], axis=0
                        )
                        for r in range(8)
                    ]
                )
            )
        bottom_out[:, 16 * g : 16 * g + 16, :] = jnp.concatenate(both, axis=1).astype(BF16)
    block = top_ref[...].astype(F32)
    halves = [jnp.swapaxes(block[:, 8 * h : 8 * h + 8], 0, 1) for h in range(2)]
    for g in range(2):
        both = []
        for u in range(2 * g, 2 * g + 2):
            rows = jnp.concatenate([halves[l // 2][4 * (l % 2) + u] for l in range(4)], axis=0)
            both.append(folded([rows[:, 64 * r : 64 * r + 64] for r in range(8)]))
        top_out[:, 16 * g : 16 * g + 16, :] = jnp.concatenate(both, axis=1).astype(BF16)


def vmem_call(kernel, outs, args, scalars=0, limit=48):
    spec = pl.BlockSpec(memory_space=pltpu.VMEM)
    scalar = pl.BlockSpec(memory_space=pltpu.SMEM)
    return pl.pallas_call(
        kernel,
        out_shape=tuple(outs),
        in_specs=[scalar] * scalars + [spec] * (len(args) - scalars),
        out_specs=tuple([spec] * len(outs)),
        compiler_params=pltpu.CompilerParams(vmem_limit_bytes=limit << 20),
    )(*args)


def fill_diagonal(diag_ref, slot, block):
    for i in range(4):
        diag_ref[slot, 64 * i : 64 * i + 64, 64 * i : 64 * i + 64] = block


def contract_kernel(
    bottom_ref, first_ref, basis_ref, tops_ref, out_ref, top_ref, wide_ref, diag_ref, even_ref, odd_ref, sum_ref
):
    step_id = pl.program_id(0)
    rows_here = A_BLOCK * D

    @pl.when(step_id == 0)
    def _():
        diag_ref[...] = jnp.zeros_like(diag_ref)
        for q in range(16):
            part = tops_ref[:, q].astype(F32).reshape(8, 4, 8, 256)
            part = jnp.transpose(part, (1, 0, 2, 3)).reshape(256, 256)
            top_ref[256 * q : 256 * q + 256, :] = part.T.astype(BF16)

    bottom = bottom_ref[...]

    def sections(group, carry):
        for j in range(UNROLL):
            fill_diagonal(diag_ref, j, first_ref[group * UNROLL + j])
        for j in range(UNROLL):
            section = jnp.dot(bottom, diag_ref[j], preferred_element_type=F32).astype(BF16)
            start = pl.multiple_of((group * UNROLL + j) * D, D)
            for q in range(16):
                wide_ref[pl.ds(start, D), 256 * q : 256 * q + 256] = section[64 * q : 64 * q + 64]
        return carry

    lax.fori_loop(0, A_BLOCK // UNROLL, sections, 0)
    second = jnp.dot(wide_ref[...], top_ref[...], preferred_element_type=F32)
    second = second.astype(BF16).astype(F32)
    base = pl.multiple_of(step_id * rows_here, rows_here)
    even_ref[pl.ds(base, rows_here), :] = second[:, :128]
    odd_ref[pl.ds(base, rows_here), :] = second[:, 128:]

    @pl.when(step_id == RANK // A_BLOCK - 1)
    def _():
        sum_ref[...] = jnp.zeros_like(sum_ref)

        def products(group, carry):
            total = sum_ref[...]
            for j in range(UNROLL):
                fill_diagonal(diag_ref, j, basis_ref[group * UNROLL + j])
            for j in range(UNROLL):
                picked = pl.ds(group * UNROLL + j, RANK, stride=D)
                rows = jnp.concatenate([even_ref[picked, :], odd_ref[picked, :]], axis=1)
                total = total + jnp.dot(
                    rows.astype(BF16), diag_ref[j], preferred_element_type=F32
                )
            sum_ref[...] = total
            return carry

        lax.fori_loop(0, D // UNROLL, products, 0)
        for u in range(4):
            out_ref[u] = sum_ref[:, 64 * u : 64 * u + 64]


def contract(bottom, first, basis, top):
    whole = lambda *dims: pl.BlockSpec(dims, lambda i: (0,) * len(dims))
    return pl.pallas_call(
        contract_kernel,
        grid=(RANK // A_BLOCK,),
        out_shape=jax.ShapeDtypeStruct((4, RANK, RANK), F32),
        in_specs=[
            whole(1024, 256),
            pl.BlockSpec((A_BLOCK, D, D), lambda i: (i, 0, 0)),
            whole(D, D, RANK),
            whole(8, 16, 32, 256),
        ],
        out_specs=whole(4, RANK, RANK),
        scratch_shapes=[
            pltpu.VMEM((D * D, 256), BF16),
            pltpu.VMEM((A_BLOCK * D, D * D), BF16),
            pltpu.VMEM((UNROLL, 256, 256), BF16),
            pltpu.VMEM((RANK * D, 128), F32),
            pltpu.VMEM((RANK * D, 128), F32),
            pltpu.VMEM((RANK, 256), F32),
        ],
        compiler_params=pltpu.CompilerParams(vmem_limit_bytes=56 << 20),
    )(bottom, first, basis, top)


def swapped_pairs(tiles):
    lane = lax.broadcasted_iota(jnp.int32, (8, 128), 1)
    stack = jnp.swapaxes(jnp.stack(tiles, axis=0), 0, 1)
    out = []
    for j in range(4):
        a, b = stack[2 * j], stack[2 * j + 1]
        low = jnp.where(lane < 64, a, pltpu.roll(b, 64, 1))
        high = jnp.where(lane < 64, pltpu.roll(a, 64, 1), b)
        out.append((low, high))
    return out


def partial_kernel(up_ref, down_ref, scale_ref, all_ref, out_ref, up_acc, down_acc):
    blocks = [all_ref[c] for c in range(4)]
    order = [(t // 4 + 2 * y, t % 4) for t in range(8) for y in range(2)]
    right = jnp.concatenate([blocks[c][:, 64 * m : 64 * m + 64] for c, m in order], axis=1)
    up_acc[...] = jnp.dot(up_ref[...], right, preferred_element_type=F32) * scale_ref[...]
    rows = []
    for c, m in order:
        part = blocks[c][:, 64 * m : 64 * m + 64]
        rows.append(jnp.concatenate([part[64 * r : 64 * r + 64] for r in range(8)], axis=1))
    down_acc[...] = lax.dot_general(
        down_ref[...],
        jnp.concatenate(rows, axis=0),
        (((1,), (1,)), ((), ())),
        preferred_element_type=F32,
    )
    for which, acc in enumerate((up_acc, down_acc)):
        for left in range(4):
            for high in range(8):
                at = 64 * left + 8 * high
                pieces = swapped_pairs(
                    [acc[at : at + 8, 128 * t : 128 * t + 128] for t in range(8)]
                )
                for j, piece in enumerate(pieces):
                    out_ref[high, which, left, 0, :, 128 * j : 128 * j + 128] = jnp.concatenate(
                        piece, axis=0
                    ).astype(BF16)


def partials(up, down, scale, by_cols):
    whole = lambda *dims: pl.BlockSpec(dims, lambda i: (0,) * len(dims))
    return pl.pallas_call(
        partial_kernel,
        grid=(4,),
        out_shape=jax.ShapeDtypeStruct((8, 2, 4, 4, 16, 512), BF16),
        in_specs=[
            whole(256, 512),
            whole(256, 512),
            whole(1, 1024),
            pl.BlockSpec((4, 512, 256), lambda i: (i, 0, 0)),
        ],
        out_specs=pl.BlockSpec((8, 2, 4, 1, 16, 512), lambda i: (0, 0, 0, i, 0, 0)),
        scratch_shapes=[pltpu.VMEM((256, 1024), F32), pltpu.VMEM((256, 1024), F32)],
        compiler_params=pltpu.CompilerParams(vmem_limit_bytes=48 << 20),
    )(up, down, scale, by_cols)


def side_kernel(
    core_ref, mine_ref, other_ref, inner_ref, rows_ref, lanes_ref, all_ref, out_ref, acc_ref
):
    step = pl.program_id(0)

    @pl.when(step == 0)
    def _():
        acc_ref[...] = jnp.zeros_like(acc_ref)

    order = [s + 4 * y for s in range(4) for y in range(2)]
    left, right = [], []
    for c in range(4):
        own = jnp.concatenate(
            [mine_ref[:, c].reshape(128, 256), other_ref[:, c].reshape(128, 256)], axis=0
        )
        left.append((own.astype(F32) * inner_ref[c]).astype(BF16))
        block = all_ref[c]
        right.append(jnp.concatenate([block[64 * s : 64 * s + 64] for s in order], axis=0))
    acc_ref[...] += lax.dot_general(
        jnp.concatenate(left, axis=1),
        jnp.concatenate(right, axis=1),
        (((1,), (1,)), ((), ())),
        preferred_element_type=F32,
    )

    @pl.when(step == 3)
    def _():
        core = core_ref[0]
        for s in range(16):
            row = 2 * ((s % 8) // 2) + (core if s < 8 else 1 - core)
            first = pl.multiple_of(32 * row + 16 * (s % 2), 16)
            scaled = (
                acc_ref[16 * s : 16 * s + 16, :] * rows_ref[pl.ds(first, 16), :] * lanes_ref[...]
            )
            tiles = [
                scaled[8 * t : 8 * t + 8, 128 * q : 128 * q + 128]
                for t in range(2)
                for q in range(4)
            ]
            pieces = swapped_pairs(tiles)
            for odd in range(2):
                low = jnp.concatenate([pieces[2 * odd][0], pieces[2 * odd + 1][0]], axis=1)
                high = jnp.concatenate([pieces[2 * odd][1], pieces[2 * odd + 1][1]], axis=1)
                for t in range(2):
                    out_ref[8 * row + 4 * (s % 2) + 2 * t + odd] = jnp.concatenate(
                        [low[4 * t : 4 * t + 4], high[4 * t : 4 * t + 4]], axis=0
                    )


def side_gram(core, mine, other, inner, rows, lanes, by_cols):
    whole = lambda *dims: pl.BlockSpec(dims, lambda i: (0,) * len(dims))
    part = pl.BlockSpec((4, 4, 32, 256), lambda i: (0, i, 0, 0))
    return pl.pallas_call(
        side_kernel,
        grid=(4,),
        out_shape=jax.ShapeDtypeStruct((D, 8, 256), F32),
        in_specs=[
            pl.BlockSpec(memory_space=pltpu.SMEM),
            part,
            part,
            pl.BlockSpec((4, 1, 256), lambda i: (i, 0, 0)),
            whole(256, 1),
            whole(1, 512),
            pl.BlockSpec((4, 512, 256), lambda i: (i, 0, 0)),
        ],
        out_specs=whole(D, 8, 256),
        scratch_shapes=[pltpu.VMEM((256, 512), F32)],
        compiler_params=pltpu.CompilerParams(vmem_limit_bytes=48 << 20),
    )(core, mine, other, inner, rows, lanes, by_cols)


def store_gram(acc_ref, high_ref, low_ref):
    for a_high in range(2):
        for x_high in range(8):
            tiles = []
            for a_low in range(2):
                at = 64 * (2 * a_high + a_low) + 8 * x_high
                for q in range(4):
                    tiles.append(acc_ref[at : at + 8, 128 * q : 128 * q + 128])
            for j, piece in enumerate(swapped_pairs(tiles)):
                high, low = two_parts(jnp.concatenate(piece, axis=0))
                lanes = slice(512 * x_high + 128 * j, 512 * x_high + 128 * j + 128)
                high_ref[16 * a_high : 16 * a_high + 16, lanes] = high
                low_ref[16 * a_high : 16 * a_high + 16, lanes] = low


def left_gram_kernel(up_ref, down_ref, high_ref, low_ref, acc_ref):
    acc_ref[...] = lax.dot_general(
        up_ref[...],
        down_ref[...].reshape(512, 512),
        (((1,), (1,)), ((), ())),
        preferred_element_type=F32,
    )
    store_gram(acc_ref, high_ref, low_ref)


def left_gram(up, down):
    out = jax.ShapeDtypeStruct((256, D * D), BF16)
    out_spec = pl.BlockSpec((32, D * D), lambda i: (i, 0))
    return pl.pallas_call(
        left_gram_kernel,
        grid=(8,),
        out_shape=(out, out),
        in_specs=[
            pl.BlockSpec((256, 512), lambda i: (0, 0)),
            pl.BlockSpec((2, 256, 512), lambda i: (i, 0, 0)),
        ],
        out_specs=(out_spec, out_spec),
        scratch_shapes=[pltpu.VMEM((256, 512), F32)],
        compiler_params=pltpu.CompilerParams(vmem_limit_bytes=48 << 20),
    )(up, down)


def down_gram_kernel(core_ref, mine_ref, other_ref, down_ref, high_ref, low_ref, acc_ref):
    step = pl.program_id(0)

    @pl.when(step == 0)
    def _():
        acc_ref[...] = jnp.zeros_like(acc_ref)

    halves = by_core(core_ref, mine_ref[...].astype(F32), other_ref[...].astype(F32))
    side = jnp.stack([h.reshape(4, 16, 8, 256) for h in halves], axis=1)
    side = jnp.transpose(side.reshape(8, 16, 8, 256), (1, 0, 2, 3)).reshape(1024, 256)
    acc_ref[...] += lax.dot_general(
        side.astype(BF16),
        down_ref[...].reshape(1024, 512),
        (((0,), (0,)), ((), ())),
        preferred_element_type=F32,
    )

    @pl.when(step == 3)
    def _():
        store_gram(acc_ref, high_ref, low_ref)


def down_gram(core, mine, other, down):
    out = jax.ShapeDtypeStruct((32, D * D), BF16)
    out_spec = pl.BlockSpec((32, D * D), lambda i: (0, 0))
    part = pl.BlockSpec((4, 128, 256), lambda i: (0, i, 0))
    return pl.pallas_call(
        down_gram_kernel,
        grid=(4,),
        out_shape=(out, out),
        in_specs=[
            pl.BlockSpec(memory_space=pltpu.SMEM),
            part,
            part,
            pl.BlockSpec((4, 256, 512), lambda i: (i, 0, 0)),
        ],
        out_specs=(out_spec, out_spec),
        scratch_shapes=[pltpu.VMEM((256, 512), F32)],
        compiler_params=pltpu.CompilerParams(vmem_limit_bytes=48 << 20),
    )(core, mine, other, down)


def body(tensor, bond_weights, start_blocks):
    row_index = lax.axis_index(ROW)

    def both_cores(shard):
        mine = from_everyone(shard, "z")
        return mine, lax.ppermute(mine, "core", [(0, 1), (1, 0)])

    where = jnp.reshape(lax.axis_index("core"), (1,)).astype(jnp.int32)
    horizontal = bond_weights[0]
    vertical = bond_weights[1]
    horiz_rows = lax.dynamic_slice_in_dim(horizontal, row_index * 8, 8)
    grid = tensor.reshape(4, 8, D, D)
    flat = jnp.transpose(grid, (1, 2, 0, 3)).reshape(512, 256)
    by_cols = lax.all_gather(flat, COL)

    square = vertical * vertical
    rows_square = horiz_rows * horiz_rows
    turned = flat.T.astype(F32)
    up_scale = (rows_square[:, None] * square[None, :]).reshape(1, 512)
    own_up = (turned * up_scale * jnp.tile(vertical, 4)[:, None]).astype(BF16)
    weighted = (turned * jnp.tile(vertical, 8)[None, :]).astype(BF16)
    top_piece = jnp.swapaxes(weighted.reshape(4, 16, 4, 512), 0, 1).reshape(16, 16, 512)
    side_piece = jnp.swapaxes(flat.reshape(8, 16, 4, 256), 0, 1).reshape(16, 32, 256)
    top_piece = top_piece.reshape(16, 16, 2, 256).swapaxes(1, 2).reshape(16, 32, 256)
    pieces = jnp.concatenate([side_piece, top_piece], axis=1)
    pieces = lax.all_to_all(pieces, COL, 0, 0, tiled=True)
    top_got = pieces[:, 32:].reshape(16, 2, 16, 256).swapaxes(1, 2).reshape(16, 16, 512)
    side_own = both_cores(pieces[:, :32])
    own_down = grid.astype(F32) * rows_square[None, :, None, None] * square
    own_down = jnp.transpose(own_down.astype(BF16), (0, 2, 1, 3)).reshape(256, 512)

    by_cols, side_own = lax.optimization_barrier((by_cols, side_own))
    lane_scale = jnp.tile(vertical, 16)[None, :]
    parts = partials(own_up, own_down, lane_scale, by_cols).reshape(8, 2, 4, D, 512)
    left_both = lax.psum_scatter(parts, ROW, scatter_dimension=0, tiled=True)

    inner = ((horizontal * horizontal)[:, None] * square[None, :]).reshape(16, 1, 256)
    lanes = jnp.repeat(jnp.transpose(horiz_rows.reshape(2, 4)).reshape(8), D)[None, :]
    side = side_gram(
        where, *side_own, inner, jnp.repeat(horizontal, 4)[:, None], lanes, by_cols
    )

    def everywhere(y):
        mine = lax.all_to_all(
            jnp.broadcast_to(y, (64, 32, 2 * RANK)), SAME_CORE, 0, 0, tiled=True
        ).reshape(2048, 2 * RANK)
        return mine, lax.ppermute(mine, "core", [(0, 1), (1, 0)])

    first_vectors = everywhere(start_blocks.reshape(32, 2 * RANK))
    left_both, first_vectors, side = lax.optimization_barrier((left_both, first_vectors, side))
    left_both = left_both.reshape(2, 256, 512)
    down_all = lax.all_gather(left_both[1], COL)
    side_all = both_cores(side.astype(BF16).reshape(512, 256))

    slab_part = by_cols.reshape(16, 8, D, 256)[:, :, :8]
    slab_part = jnp.transpose(slab_part, (2, 0, 1, 3)).reshape(8, 128, 256)
    slab = lax.all_to_all(slab_part, ROW, split_axis=0, concat_axis=0, tiled=True)
    bottom, top_rows = vmem_call(
        fold_kernel,
        (
            jax.ShapeDtypeStruct((16, D, 256), BF16),
            jax.ShapeDtypeStruct((16, 32, 256), BF16),
        ),
        (slab, top_got),
    )
    down_all, bottom, top_rows, side_all = lax.optimization_barrier(
        (down_all, bottom, top_rows, side_all)
    )
    grams = (*left_gram(left_both[0], down_all), *down_gram(where, *side_all, down_all))
    top_rows, grams = lax.optimization_barrier((top_rows, grams))
    top = lax.all_gather(top_rows, ROW)
    z_outs = (
        jax.ShapeDtypeStruct((8, 16, 2 * RANK), F32),
        jax.ShapeDtypeStruct((32, 2 * RANK), F32),
    )
    inv_out = jax.ShapeDtypeStruct((2 * RANK, 2 * RANK), F32)

    def local_images(z_left, z_down):
        z_left = jnp.sum(lax.all_to_all(z_left, ROW, 0, 0, tiled=True), axis=0)
        z_left = jnp.concatenate([z_left[:, :RANK], z_left[:, RANK:]], axis=0)
        z = jnp.concatenate([z_left, z_down[:, RANK:]], axis=1)
        z = jnp.transpose(z.reshape(2, 2, 2, 4, 2 * RANK), (0, 2, 3, 1, 4))
        return z.reshape(32, 2 * RANK)

    def apply(y, inverse):
        return lax.dot_general(y, inverse, (((1,), (1,)), ((), ())), precision=HIGHEST)

    vectors = first_vectors
    for step in range(3):
        y = local_images(*vmem_call(images_kernel, z_outs, (where, *vectors, *grams), 1))
        if step:
            y = apply(y, vmem_call(factor_kernel, (inv_out,), vectors)[0])
        vectors = everywhere(y)
    basis_out = jax.ShapeDtypeStruct((D * D, RANK), BF16)
    basis, mixed, inverse = vmem_call(
        last_kernel, (basis_out, basis_out, inv_out), (where, *vectors), 1
    )
    projectors = apply(y, inverse).reshape(4, 8, 2 * RANK)
    first = jnp.transpose(mixed.reshape(16, 4, D, RANK), (3, 1, 0, 2)).reshape(RANK, D, D)
    new_tensor = contract(bottom.reshape(1024, 256), first, basis.reshape(D, D, RANK), top)
    return (projectors, new_tensor.reshape(4, 1, RANK * RANK))


def solution(mesh):
    axes = ("z", "core", "col_0", "col_1")
    torus = Mesh(mesh.devices.reshape(mesh.shape["row"] // 2, 2, 4, 4), axes)
    placed = (P(COL, ROW, None), P(), P(COL, ROW, None))
    return jax.shard_map(
        body,
        mesh=torus,
        in_specs=placed,
        out_specs=(P(COL, ROW, None), P(COL, ROW, None)),
        check_vma=False,
    )
```

```python
import jax
import jax.numpy as jnp
from jax import lax
from jax.experimental import pallas as pl
from jax.experimental.pallas import tpu as pltpu
from jax.sharding import Mesh
from jax.sharding import PartitionSpec as P

D = 64
RANK = 64
COL = ("col_0", "col_1")
ROW = ("z", "core")
SAME_CORE = ("z", "col_0", "col_1")
HIGHEST = lax.Precision.HIGHEST
F32 = jnp.float32
BF16 = jnp.bfloat16
A_BLOCK = 16
UNROLL = 8


def from_everyone(shard, axis):
    copies = jnp.broadcast_to(shard, (lax.axis_size(axis), *shard.shape))
    return lax.all_to_all(copies, axis, split_axis=0, concat_axis=0, tiled=True)


def two_parts(x):
    high = x.astype(BF16)
    return high, (x - high.astype(F32)).astype(BF16)


def by_core(core_ref, mine, other):
    first = core_ref[0] == 0
    return jnp.where(first, mine, other), jnp.where(first, other, mine)


def in_index_order(core_ref, mine_ref, other_ref):
    halves = by_core(core_ref, mine_ref[...], other_ref[...])
    y = jnp.stack([h.reshape(4, D, 8, 2 * RANK) for h in halves], axis=1)
    y = jnp.transpose(y.reshape(8, D, 8, 2 * RANK), (1, 0, 2, 3))
    return y.reshape(D * D, 2 * RANK)


def inverse_factors(mats):
    n = RANK
    count = n // 8
    rows_at = lax.broadcasted_iota(jnp.int32, (8, 2 * n), 0)
    lanes_at = lax.broadcasted_iota(jnp.int32, (8, 2 * n), 1)
    sets = []
    for c in mats:
        blocks = []
        for i in range(count):
            unit = (lanes_at == rows_at + (n + 8 * i)).astype(F32)
            part = jnp.concatenate([c[8 * i : 8 * i + 8], jnp.zeros((8, n), F32)], axis=1)
            blocks.append(part + unit)
        sets.append((blocks, []))
    for b in range(count):
        panels = []
        for blocks, _ in sets:
            columns = [
                {
                    i: jnp.broadcast_to(blocks[i][:, 8 * b + j : 8 * b + j + 1], (8, 2 * n))
                    for i in range(b, count)
                }
                for j in range(8)
            ]
            rows = [jnp.broadcast_to(blocks[b][j : j + 1], (8, 2 * n)) for j in range(8)]
            panels.append((columns, rows, []))
        for j in range(8):
            for (blocks, pivots), (columns, rows, scaled) in zip(sets, panels):
                own = columns[j][b]
                inverse = 1.0 / own[j : j + 1]
                pivots.append(own[j : j + 1])
                scaled.append(rows[j] * inverse)
                for k in range(j + 1, 8):
                    factor = columns[k][b][j : j + 1] * inverse
                    rows[k] = rows[k] - own[k : k + 1] * scaled[j]
                    for i in range(b, count):
                        columns[k][i] = columns[k][i] - columns[j][i] * factor
        for (blocks, _), (columns, rows, scaled) in zip(sets, panels):
            whole = rows[0]
            for j in range(1, 8):
                whole = jnp.where(rows_at == j, rows[j], whole)
            blocks[b] = whole
            for i in range(b + 1, count):
                for j in range(8):
                    blocks[i] = blocks[i] - columns[j][i] * scaled[j]
    out = []
    for blocks, pivots in sets:
        done = []
        for i in range(count):
            pivot = jnp.broadcast_to(pivots[8 * i], (8, 2 * n))
            for j in range(1, 8):
                pivot = jnp.where(rows_at == j, pivots[8 * i + j], pivot)
            done.append((blocks[i] / jnp.sqrt(pivot))[:, n:])
        out.append(jnp.concatenate(done, axis=0))
    return out


def correlation(y):
    return lax.dot_general(
        y, y, (((0,), (0,)), ((), ())), precision=HIGHEST, preferred_element_type=F32
    )


def factors_of(c):
    return inverse_factors([c[:RANK, :RANK], c[RANK:, RANK:]])


def store_inverse(inv_ref, left, down):
    zero = jnp.zeros((RANK, RANK), F32)
    inv_ref[:RANK, :] = jnp.concatenate([left, zero], axis=1)
    inv_ref[RANK:, :] = jnp.concatenate([zero, down], axis=1)


def images_of(y, gl_high, gl_low, gd_high, gd_low, zl_ref, zd_ref):
    y_high, y_low = two_parts(y)
    both = jnp.concatenate([y_high, y_low], axis=1)

    def product(high, low):
        main = jnp.dot(high[...], both, preferred_element_type=F32)
        rest = jnp.dot(low[...], y_high, preferred_element_type=F32)
        return main[:, : 2 * RANK] + main[:, 2 * RANK :] + rest

    z = product(gl_high, gl_low)[:, :RANK].reshape(8, 32, RANK)
    zl_ref[...] = jnp.concatenate([z[:, :16], z[:, 16:]], axis=2)
    zd_ref[...] = product(gd_high, gd_low)


def images_kernel(core_ref, mine_ref, other_ref, glh, gll, gdh, gdl, zl_ref, zd_ref):
    y = in_index_order(core_ref, mine_ref, other_ref)
    images_of(y, glh, gll, gdh, gdl, zl_ref, zd_ref)


def factor_kernel(mine_ref, other_ref, inv_ref):
    c = correlation(mine_ref[...]) + correlation(other_ref[...])
    store_inverse(inv_ref, *factors_of(c))


def last_kernel(core_ref, mine_ref, other_ref, basis_ref, mixed_ref, inv_ref):
    c = correlation(mine_ref[...]) + correlation(other_ref[...])
    left, down = factors_of(c)
    store_inverse(inv_ref, left, down)
    y = in_index_order(core_ref, mine_ref, other_ref)[:, :RANK]
    y_high, y_low = two_parts(y)
    l_high, l_low = two_parts(left.T)
    basis = jnp.dot(
        jnp.concatenate([y_high, y_low, y_high], axis=1),
        jnp.concatenate([l_high, l_high, l_low], axis=0),
        preferred_element_type=F32,
    )
    basis = basis.astype(BF16)
    basis_ref[...] = basis
    to = lax.broadcasted_iota(jnp.int32, (256, 256), 0)
    at = lax.broadcasted_iota(jnp.int32, (256, 256), 1)
    source = (to // 64) * 64 + (to % 16) * 4 + (to % 64) // 16
    picks = (at == source).astype(F32).astype(BF16)
    for q in range(16):
        rows = slice(256 * q, 256 * q + 256)
        mixed_ref[rows, :] = jnp.dot(
            picks, basis[rows], preferred_element_type=F32
        ).astype(BF16)


def folded(columns):
    rows = []
    for x in range(0, 8, 2):
        turned = jnp.concatenate(columns[x : x + 2], axis=1).T
        for h in range(2):
            parts = [turned[64 * h + 16 * q : 64 * h + 16 * q + 16] for q in range(4)]
            rows.append(jnp.concatenate(parts, axis=1))
    return jnp.swapaxes(jnp.stack(rows, axis=0), 0, 1)


def fold_kernel(slab_ref, top_ref, bottom_out, top_out):
    for g in range(4):
        both = []
        for h in range(2):
            block = slab_ref[2 * g + h].astype(F32).reshape(16, 8, 256)
            by_r = jnp.swapaxes(block, 0, 1)
            both.append(
                folded(
                    [
                        jnp.concatenate(
                            [by_r[r][:, 64 * l : 64 * l + 64] for l in range(4)], axis=0
                        )
                        for r in range(8)
                    ]
                )
            )
        bottom_out[:, 16 * g : 16 * g + 16, :] = jnp.concatenate(both, axis=1).astype(BF16)
    block = top_ref[...].astype(F32)
    halves = [jnp.swapaxes(block[:, 8 * h : 8 * h + 8], 0, 1) for h in range(2)]
    for g in range(2):
        both = []
        for u in range(2 * g, 2 * g + 2):
            rows = jnp.concatenate([halves[l // 2][4 * (l % 2) + u] for l in range(4)], axis=0)
            both.append(folded([rows[:, 64 * r : 64 * r + 64] for r in range(8)]))
        top_out[:, 16 * g : 16 * g + 16, :] = jnp.concatenate(both, axis=1).astype(BF16)


def vmem_call(kernel, outs, args, scalars=0, limit=48):
    spec = pl.BlockSpec(memory_space=pltpu.VMEM)
    scalar = pl.BlockSpec(memory_space=pltpu.SMEM)
    return pl.pallas_call(
        kernel,
        out_shape=tuple(outs),
        in_specs=[scalar] * scalars + [spec] * (len(args) - scalars),
        out_specs=tuple([spec] * len(outs)),
        compiler_params=pltpu.CompilerParams(vmem_limit_bytes=limit << 20),
    )(*args)


def fill_diagonal(diag_ref, slot, block):
    for i in range(4):
        diag_ref[slot, 64 * i : 64 * i + 64, 64 * i : 64 * i + 64] = block


def contract_kernel(
    bottom_ref, first_ref, basis_ref, tops_ref, out_ref, top_ref, wide_ref, diag_ref, even_ref, odd_ref, sum_ref
):
    step_id = pl.program_id(0)
    rows_here = A_BLOCK * D

    @pl.when(step_id == 0)
    def _():
        diag_ref[...] = jnp.zeros_like(diag_ref)
        for q in range(16):
            part = tops_ref[:, q].astype(F32).reshape(8, 4, 8, 256)
            part = jnp.transpose(part, (1, 0, 2, 3)).reshape(256, 256)
            top_ref[256 * q : 256 * q + 256, :] = part.T.astype(BF16)

    bottom = bottom_ref[...]

    def sections(group, carry):
        for j in range(UNROLL):
            fill_diagonal(diag_ref, j, first_ref[group * UNROLL + j])
        for j in range(UNROLL):
            section = jnp.dot(bottom, diag_ref[j], preferred_element_type=F32).astype(BF16)
            start = pl.multiple_of((group * UNROLL + j) * D, D)
            for q in range(16):
                wide_ref[pl.ds(start, D), 256 * q : 256 * q + 256] = section[64 * q : 64 * q + 64]
        return carry

    lax.fori_loop(0, A_BLOCK // UNROLL, sections, 0)
    second = jnp.dot(wide_ref[...], top_ref[...], preferred_element_type=F32)
    second = second.astype(BF16).astype(F32)
    base = pl.multiple_of(step_id * rows_here, rows_here)
    even_ref[pl.ds(base, rows_here), :] = second[:, :128]
    odd_ref[pl.ds(base, rows_here), :] = second[:, 128:]

    @pl.when(step_id == RANK // A_BLOCK - 1)
    def _():
        sum_ref[...] = jnp.zeros_like(sum_ref)

        def products(group, carry):
            total = sum_ref[...]
            for j in range(UNROLL):
                fill_diagonal(diag_ref, j, basis_ref[group * UNROLL + j])
            for j in range(UNROLL):
                picked = pl.ds(group * UNROLL + j, RANK, stride=D)
                rows = jnp.concatenate([even_ref[picked, :], odd_ref[picked, :]], axis=1)
                total = total + jnp.dot(
                    rows.astype(BF16), diag_ref[j], preferred_element_type=F32
                )
            sum_ref[...] = total
            return carry

        lax.fori_loop(0, D // UNROLL, products, 0)
        for u in range(4):
            out_ref[u] = sum_ref[:, 64 * u : 64 * u + 64]


def contract(bottom, first, basis, top):
    whole = lambda *dims: pl.BlockSpec(dims, lambda i: (0,) * len(dims))
    return pl.pallas_call(
        contract_kernel,
        grid=(RANK // A_BLOCK,),
        out_shape=jax.ShapeDtypeStruct((4, RANK, RANK), F32),
        in_specs=[
            whole(1024, 256),
            pl.BlockSpec((A_BLOCK, D, D), lambda i: (i, 0, 0)),
            whole(D, D, RANK),
            whole(8, 16, 32, 256),
        ],
        out_specs=whole(4, RANK, RANK),
        scratch_shapes=[
            pltpu.VMEM((D * D, 256), BF16),
            pltpu.VMEM((A_BLOCK * D, D * D), BF16),
            pltpu.VMEM((UNROLL, 256, 256), BF16),
            pltpu.VMEM((RANK * D, 128), F32),
            pltpu.VMEM((RANK * D, 128), F32),
            pltpu.VMEM((RANK, 256), F32),
        ],
        compiler_params=pltpu.CompilerParams(vmem_limit_bytes=56 << 20),
    )(bottom, first, basis, top)


def swapped_pairs(tiles):
    lane = lax.broadcasted_iota(jnp.int32, (8, 128), 1)
    stack = jnp.swapaxes(jnp.stack(tiles, axis=0), 0, 1)
    out = []
    for j in range(4):
        a, b = stack[2 * j], stack[2 * j + 1]
        low = jnp.where(lane < 64, a, pltpu.roll(b, 64, 1))
        high = jnp.where(lane < 64, pltpu.roll(a, 64, 1), b)
        out.append((low, high))
    return out


def partial_kernel(up_ref, down_ref, scale_ref, all_ref, out_ref, up_acc, down_acc):
    blocks = [all_ref[c] for c in range(4)]
    order = [(t // 4 + 2 * y, t % 4) for t in range(8) for y in range(2)]
    right = jnp.concatenate([blocks[c][:, 64 * m : 64 * m + 64] for c, m in order], axis=1)
    up_acc[...] = jnp.dot(up_ref[...], right, preferred_element_type=F32) * scale_ref[...]
    rows = []
    for c, m in order:
        part = blocks[c][:, 64 * m : 64 * m + 64]
        rows.append(jnp.concatenate([part[64 * r : 64 * r + 64] for r in range(8)], axis=1))
    down_acc[...] = lax.dot_general(
        down_ref[...],
        jnp.concatenate(rows, axis=0),
        (((1,), (1,)), ((), ())),
        preferred_element_type=F32,
    )
    for which, acc in enumerate((up_acc, down_acc)):
        for left in range(4):
            for high in range(8):
                at = 64 * left + 8 * high
                pieces = swapped_pairs(
                    [acc[at : at + 8, 128 * t : 128 * t + 128] for t in range(8)]
                )
                for j, piece in enumerate(pieces):
                    out_ref[high, which, left, 0, :, 128 * j : 128 * j + 128] = jnp.concatenate(
                        piece, axis=0
                    ).astype(BF16)


def partials(up, down, scale, by_cols):
    whole = lambda *dims: pl.BlockSpec(dims, lambda i: (0,) * len(dims))
    return pl.pallas_call(
        partial_kernel,
        grid=(4,),
        out_shape=jax.ShapeDtypeStruct((8, 2, 4, 4, 16, 512), BF16),
        in_specs=[
            whole(256, 512),
            whole(256, 512),
            whole(1, 1024),
            pl.BlockSpec((4, 512, 256), lambda i: (i, 0, 0)),
        ],
        out_specs=pl.BlockSpec((8, 2, 4, 1, 16, 512), lambda i: (0, 0, 0, i, 0, 0)),
        scratch_shapes=[pltpu.VMEM((256, 1024), F32), pltpu.VMEM((256, 1024), F32)],
        compiler_params=pltpu.CompilerParams(vmem_limit_bytes=48 << 20),
    )(up, down, scale, by_cols)


def side_kernel(
    core_ref, mine_ref, other_ref, inner_ref, rows_ref, lanes_ref, all_ref, out_ref, acc_ref
):
    step = pl.program_id(0)

    @pl.when(step == 0)
    def _():
        acc_ref[...] = jnp.zeros_like(acc_ref)

    order = [s + 4 * y for s in range(4) for y in range(2)]
    left, right = [], []
    for c in range(4):
        own = jnp.concatenate(
            [mine_ref[:, c].reshape(128, 256), other_ref[:, c].reshape(128, 256)], axis=0
        )
        left.append((own.astype(F32) * inner_ref[c]).astype(BF16))
        block = all_ref[c]
        right.append(jnp.concatenate([block[64 * s : 64 * s + 64] for s in order], axis=0))
    acc_ref[...] += lax.dot_general(
        jnp.concatenate(left, axis=1),
        jnp.concatenate(right, axis=1),
        (((1,), (1,)), ((), ())),
        preferred_element_type=F32,
    )

    @pl.when(step == 3)
    def _():
        core = core_ref[0]
        for s in range(16):
            row = 2 * ((s % 8) // 2) + (core if s < 8 else 1 - core)
            first = pl.multiple_of(32 * row + 16 * (s % 2), 16)
            scaled = (
                acc_ref[16 * s : 16 * s + 16, :] * rows_ref[pl.ds(first, 16), :] * lanes_ref[...]
            )
            tiles = [
                scaled[8 * t : 8 * t + 8, 128 * q : 128 * q + 128]
                for t in range(2)
                for q in range(4)
            ]
            pieces = swapped_pairs(tiles)
            for odd in range(2):
                low = jnp.concatenate([pieces[2 * odd][0], pieces[2 * odd + 1][0]], axis=1)
                high = jnp.concatenate([pieces[2 * odd][1], pieces[2 * odd + 1][1]], axis=1)
                for t in range(2):
                    out_ref[8 * row + 4 * (s % 2) + 2 * t + odd] = jnp.concatenate(
                        [low[4 * t : 4 * t + 4], high[4 * t : 4 * t + 4]], axis=0
                    )


def side_gram(core, mine, other, inner, rows, lanes, by_cols):
    whole = lambda *dims: pl.BlockSpec(dims, lambda i: (0,) * len(dims))
    part = pl.BlockSpec((4, 4, 32, 256), lambda i: (0, i, 0, 0))
    return pl.pallas_call(
        side_kernel,
        grid=(4,),
        out_shape=jax.ShapeDtypeStruct((D, 8, 256), F32),
        in_specs=[
            pl.BlockSpec(memory_space=pltpu.SMEM),
            part,
            part,
            pl.BlockSpec((4, 1, 256), lambda i: (i, 0, 0)),
            whole(256, 1),
            whole(1, 512),
            pl.BlockSpec((4, 512, 256), lambda i: (i, 0, 0)),
        ],
        out_specs=whole(D, 8, 256),
        scratch_shapes=[pltpu.VMEM((256, 512), F32)],
        compiler_params=pltpu.CompilerParams(vmem_limit_bytes=48 << 20),
    )(core, mine, other, inner, rows, lanes, by_cols)


def store_gram(acc_ref, high_ref, low_ref):
    for a_high in range(2):
        for x_high in range(8):
            tiles = []
            for a_low in range(2):
                at = 64 * (2 * a_high + a_low) + 8 * x_high
                for q in range(4):
                    tiles.append(acc_ref[at : at + 8, 128 * q : 128 * q + 128])
            for j, piece in enumerate(swapped_pairs(tiles)):
                high, low = two_parts(jnp.concatenate(piece, axis=0))
                lanes = slice(512 * x_high + 128 * j, 512 * x_high + 128 * j + 128)
                high_ref[16 * a_high : 16 * a_high + 16, lanes] = high
                low_ref[16 * a_high : 16 * a_high + 16, lanes] = low


def left_gram_kernel(up_ref, down_ref, high_ref, low_ref, acc_ref):
    acc_ref[...] = lax.dot_general(
        up_ref[...],
        down_ref[...].reshape(512, 512),
        (((1,), (1,)), ((), ())),
        preferred_element_type=F32,
    )
    store_gram(acc_ref, high_ref, low_ref)


def left_gram(up, down):
    out = jax.ShapeDtypeStruct((256, D * D), BF16)
    out_spec = pl.BlockSpec((32, D * D), lambda i: (i, 0))
    return pl.pallas_call(
        left_gram_kernel,
        grid=(8,),
        out_shape=(out, out),
        in_specs=[
            pl.BlockSpec((256, 512), lambda i: (0, 0)),
            pl.BlockSpec((2, 256, 512), lambda i: (i, 0, 0)),
        ],
        out_specs=(out_spec, out_spec),
        scratch_shapes=[pltpu.VMEM((256, 512), F32)],
        compiler_params=pltpu.CompilerParams(vmem_limit_bytes=48 << 20),
    )(up, down)


def down_gram_kernel(core_ref, mine_ref, other_ref, down_ref, high_ref, low_ref, acc_ref):
    step = pl.program_id(0)

    @pl.when(step == 0)
    def _():
        acc_ref[...] = jnp.zeros_like(acc_ref)

    halves = by_core(core_ref, mine_ref[...].astype(F32), other_ref[...].astype(F32))
    side = jnp.stack([h.reshape(4, 16, 8, 256) for h in halves], axis=1)
    side = jnp.transpose(side.reshape(8, 16, 8, 256), (1, 0, 2, 3)).reshape(1024, 256)
    acc_ref[...] += lax.dot_general(
        side.astype(BF16),
        down_ref[...].reshape(1024, 512),
        (((0,), (0,)), ((), ())),
        preferred_element_type=F32,
    )

    @pl.when(step == 3)
    def _():
        store_gram(acc_ref, high_ref, low_ref)


def down_gram(core, mine, other, down):
    out = jax.ShapeDtypeStruct((32, D * D), BF16)
    out_spec = pl.BlockSpec((32, D * D), lambda i: (0, 0))
    part = pl.BlockSpec((4, 128, 256), lambda i: (0, i, 0))
    return pl.pallas_call(
        down_gram_kernel,
        grid=(4,),
        out_shape=(out, out),
        in_specs=[
            pl.BlockSpec(memory_space=pltpu.SMEM),
            part,
            part,
            pl.BlockSpec((4, 256, 512), lambda i: (i, 0, 0)),
        ],
        out_specs=(out_spec, out_spec),
        scratch_shapes=[pltpu.VMEM((256, 512), F32)],
        compiler_params=pltpu.CompilerParams(vmem_limit_bytes=48 << 20),
    )(core, mine, other, down)


def body(tensor, bond_weights, start_blocks):
    row_index = lax.axis_index(ROW)

    def both_cores(shard):
        mine = from_everyone(shard, "z")
        return mine, lax.ppermute(mine, "core", [(0, 1), (1, 0)])

    where = jnp.reshape(lax.axis_index("core"), (1,)).astype(jnp.int32)
    horizontal = bond_weights[0]
    vertical = bond_weights[1]
    horiz_rows = lax.dynamic_slice_in_dim(horizontal, row_index * 8, 8)
    grid = tensor.reshape(4, 8, D, D)
    flat = jnp.transpose(grid, (1, 2, 0, 3)).reshape(512, 256)
    by_cols = lax.all_gather(flat, COL)

    square = vertical * vertical
    rows_square = horiz_rows * horiz_rows
    turned = flat.T.astype(F32)
    up_scale = (rows_square[:, None] * square[None, :]).reshape(1, 512)
    own_up = (turned * up_scale * jnp.tile(vertical, 4)[:, None]).astype(BF16)
    weighted = (turned * jnp.tile(vertical, 8)[None, :]).astype(BF16)
    top_piece = jnp.swapaxes(weighted.reshape(4, 16, 4, 512), 0, 1).reshape(16, 16, 512)
    side_piece = jnp.swapaxes(flat.reshape(8, 16, 4, 256), 0, 1).reshape(16, 32, 256)
    top_piece = top_piece.reshape(16, 16, 2, 256).swapaxes(1, 2).reshape(16, 32, 256)
    pieces = jnp.concatenate([side_piece, top_piece], axis=1)
    pieces = lax.all_to_all(pieces, COL, 0, 0, tiled=True)
    top_got = pieces[:, 32:].reshape(16, 2, 16, 256).swapaxes(1, 2).reshape(16, 16, 512)
    side_own = both_cores(pieces[:, :32])
    own_down = grid.astype(F32) * rows_square[None, :, None, None] * square
    own_down = jnp.transpose(own_down.astype(BF16), (0, 2, 1, 3)).reshape(256, 512)

    by_cols, side_own = lax.optimization_barrier((by_cols, side_own))
    lane_scale = jnp.tile(vertical, 16)[None, :]
    parts = partials(own_up, own_down, lane_scale, by_cols).reshape(8, 2, 4, D, 512)
    left_both = lax.psum_scatter(parts, ROW, scatter_dimension=0, tiled=True)

    inner = ((horizontal * horizontal)[:, None] * square[None, :]).reshape(16, 1, 256)
    lanes = jnp.repeat(jnp.transpose(horiz_rows.reshape(2, 4)).reshape(8), D)[None, :]
    side = side_gram(
        where, *side_own, inner, jnp.repeat(horizontal, 4)[:, None], lanes, by_cols
    )

    def everywhere(y):
        mine = lax.all_to_all(
            jnp.broadcast_to(y, (64, 32, 2 * RANK)), SAME_CORE, 0, 0, tiled=True
        ).reshape(2048, 2 * RANK)
        return mine, lax.ppermute(mine, "core", [(0, 1), (1, 0)])

    first_vectors = everywhere(start_blocks.reshape(32, 2 * RANK))
    left_both, first_vectors, side = lax.optimization_barrier((left_both, first_vectors, side))
    left_both = left_both.reshape(2, 256, 512)
    down_all = lax.all_gather(left_both[1], COL)
    side_all = both_cores(side.astype(BF16).reshape(512, 256))

    slab_part = by_cols.reshape(16, 8, D, 256)[:, :, :8]
    slab_part = jnp.transpose(slab_part, (2, 0, 1, 3)).reshape(8, 128, 256)
    slab = lax.all_to_all(slab_part, ROW, split_axis=0, concat_axis=0, tiled=True)
    bottom, top_rows = vmem_call(
        fold_kernel,
        (
            jax.ShapeDtypeStruct((16, D, 256), BF16),
            jax.ShapeDtypeStruct((16, 32, 256), BF16),
        ),
        (slab, top_got),
    )
    down_all, bottom, top_rows, side_all = lax.optimization_barrier(
        (down_all, bottom, top_rows, side_all)
    )
    grams = (*left_gram(left_both[0], down_all), *down_gram(where, *side_all, down_all))
    top_rows, grams = lax.optimization_barrier((top_rows, grams))
    top = lax.all_gather(top_rows, ROW)
    z_outs = (
        jax.ShapeDtypeStruct((8, 16, 2 * RANK), F32),
        jax.ShapeDtypeStruct((32, 2 * RANK), F32),
    )
    inv_out = jax.ShapeDtypeStruct((2 * RANK, 2 * RANK), F32)

    def local_images(z_left, z_down):
        z_left = jnp.sum(lax.all_to_all(z_left, ROW, 0, 0, tiled=True), axis=0)
        z_left = jnp.concatenate([z_left[:, :RANK], z_left[:, RANK:]], axis=0)
        z = jnp.concatenate([z_left, z_down[:, RANK:]], axis=1)
        z = jnp.transpose(z.reshape(2, 2, 2, 4, 2 * RANK), (0, 2, 3, 1, 4))
        return z.reshape(32, 2 * RANK)

    def apply(y, inverse):
        return lax.dot_general(y, inverse, (((1,), (1,)), ((), ())), precision=HIGHEST)

    vectors = first_vectors
    for step in range(3):
        y = local_images(*vmem_call(images_kernel, z_outs, (where, *vectors, *grams), 1))
        if step:
            y = apply(y, vmem_call(factor_kernel, (inv_out,), vectors)[0])
        vectors = everywhere(y)
    basis_out = jax.ShapeDtypeStruct((D * D, RANK), BF16)
    basis, mixed, inverse = vmem_call(
        last_kernel, (basis_out, basis_out, inv_out), (where, *vectors), 1
    )
    projectors = apply(y, inverse).reshape(4, 8, 2 * RANK)
    first = jnp.transpose(mixed.reshape(16, 4, D, RANK), (3, 1, 0, 2)).reshape(RANK, D, D)
    new_tensor = contract(bottom.reshape(1024, 256), first, basis.reshape(D, D, RANK), top)
    return (projectors, new_tensor.reshape(4, 1, RANK * RANK))


def solution(mesh):
    axes = ("z", "core", "col_0", "col_1")
    torus = Mesh(mesh.devices.reshape(mesh.shape["row"] // 2, 2, 4, 4), axes)
    placed = (P(COL, ROW, None), P(), P(COL, ROW, None))
    return jax.shard_map(
        body,
        mesh=torus,
        in_specs=placed,
        out_specs=(P(COL, ROW, None), P(COL, ROW, None)),
        check_vma=False,
    )
```

```python
import jax
import jax.numpy as jnp
from jax import lax
from jax.experimental import pallas as pl
from jax.experimental.pallas import tpu as pltpu
from jax.sharding import Mesh
from jax.sharding import PartitionSpec as P

D = 64
RANK = 64
COL = ("col_0", "col_1")
ROW = ("z", "core")
SAME_CORE = ("z", "col_0", "col_1")
HIGHEST = lax.Precision.HIGHEST
F32 = jnp.float32
BF16 = jnp.bfloat16
A_BLOCK = 16
UNROLL = 8


def from_everyone(shard, axis):
    copies = jnp.broadcast_to(shard, (lax.axis_size(axis), *shard.shape))
    return lax.all_to_all(copies, axis, split_axis=0, concat_axis=0, tiled=True)


def two_parts(x):
    high = x.astype(BF16)
    return high, (x - high.astype(F32)).astype(BF16)


def by_core(core_ref, mine, other):
    first = core_ref[0] == 0
    return jnp.where(first, mine, other), jnp.where(first, other, mine)


def in_index_order(core_ref, mine_ref, other_ref):
    halves = by_core(core_ref, mine_ref[...], other_ref[...])
    y = jnp.stack([h.reshape(4, D, 8, 2 * RANK) for h in halves], axis=1)
    y = jnp.transpose(y.reshape(8, D, 8, 2 * RANK), (1, 0, 2, 3))
    return y.reshape(D * D, 2 * RANK)


def inverse_factors(mats):
    n = RANK
    count = n // 8
    rows_at = lax.broadcasted_iota(jnp.int32, (8, 2 * n), 0)
    lanes_at = lax.broadcasted_iota(jnp.int32, (8, 2 * n), 1)
    sets = []
    for c in mats:
        blocks = []
        for i in range(count):
            unit = (lanes_at == rows_at + (n + 8 * i)).astype(F32)
            part = jnp.concatenate([c[8 * i : 8 * i + 8], jnp.zeros((8, n), F32)], axis=1)
            blocks.append(part + unit)
        sets.append((blocks, []))
    for b in range(count):
        panels = []
        for blocks, _ in sets:
            columns = [
                {
                    i: jnp.broadcast_to(blocks[i][:, 8 * b + j : 8 * b + j + 1], (8, 2 * n))
                    for i in range(b, count)
                }
                for j in range(8)
            ]
            rows = [jnp.broadcast_to(blocks[b][j : j + 1], (8, 2 * n)) for j in range(8)]
            panels.append((columns, rows, []))
        for j in range(8):
            for (blocks, pivots), (columns, rows, scaled) in zip(sets, panels):
                own = columns[j][b]
                inverse = 1.0 / own[j : j + 1]
                pivots.append(own[j : j + 1])
                scaled.append(rows[j] * inverse)
                for k in range(j + 1, 8):
                    factor = columns[k][b][j : j + 1] * inverse
                    rows[k] = rows[k] - own[k : k + 1] * scaled[j]
                    for i in range(b, count):
                        columns[k][i] = columns[k][i] - columns[j][i] * factor
        for (blocks, _), (columns, rows, scaled) in zip(sets, panels):
            whole = rows[0]
            for j in range(1, 8):
                whole = jnp.where(rows_at == j, rows[j], whole)
            blocks[b] = whole
            for i in range(b + 1, count):
                for j in range(8):
                    blocks[i] = blocks[i] - columns[j][i] * scaled[j]
    out = []
    for blocks, pivots in sets:
        done = []
        for i in range(count):
            pivot = jnp.broadcast_to(pivots[8 * i], (8, 2 * n))
            for j in range(1, 8):
                pivot = jnp.where(rows_at == j, pivots[8 * i + j], pivot)
            done.append((blocks[i] / jnp.sqrt(pivot))[:, n:])
        out.append(jnp.concatenate(done, axis=0))
    return out


def correlation(y):
    return lax.dot_general(
        y, y, (((0,), (0,)), ((), ())), precision=HIGHEST, preferred_element_type=F32
    )


def factors_of(c):
    return inverse_factors([c[:RANK, :RANK], c[RANK:, RANK:]])


def store_inverse(inv_ref, left, down):
    zero = jnp.zeros((RANK, RANK), F32)
    inv_ref[:RANK, :] = jnp.concatenate([left, zero], axis=1)
    inv_ref[RANK:, :] = jnp.concatenate([zero, down], axis=1)


def images_of(y, gl_high, gl_low, gd_high, gd_low, zl_ref, zd_ref):
    y_high, y_low = two_parts(y)
    both = jnp.concatenate([y_high, y_low], axis=1)

    def product(high, low):
        main = jnp.dot(high[...], both, preferred_element_type=F32)
        rest = jnp.dot(low[...], y_high, preferred_element_type=F32)
        return main[:, : 2 * RANK] + main[:, 2 * RANK :] + rest

    z = product(gl_high, gl_low)[:, :RANK].reshape(8, 32, RANK)
    zl_ref[...] = jnp.concatenate([z[:, :16], z[:, 16:]], axis=2)
    zd_ref[...] = product(gd_high, gd_low)


def images_kernel(core_ref, mine_ref, other_ref, glh, gll, gdh, gdl, zl_ref, zd_ref):
    y = in_index_order(core_ref, mine_ref, other_ref)
    images_of(y, glh, gll, gdh, gdl, zl_ref, zd_ref)


def factor_kernel(mine_ref, other_ref, inv_ref):
    c = correlation(mine_ref[...]) + correlation(other_ref[...])
    store_inverse(inv_ref, *factors_of(c))


def last_kernel(core_ref, mine_ref, other_ref, basis_ref, mixed_ref, inv_ref):
    c = correlation(mine_ref[...]) + correlation(other_ref[...])
    left, down = factors_of(c)
    store_inverse(inv_ref, left, down)
    y = in_index_order(core_ref, mine_ref, other_ref)[:, :RANK]
    y_high, y_low = two_parts(y)
    l_high, l_low = two_parts(left.T)
    basis = jnp.dot(
        jnp.concatenate([y_high, y_low, y_high], axis=1),
        jnp.concatenate([l_high, l_high, l_low], axis=0),
        preferred_element_type=F32,
    )
    basis = basis.astype(BF16)
    basis_ref[...] = basis
    to = lax.broadcasted_iota(jnp.int32, (256, 256), 0)
    at = lax.broadcasted_iota(jnp.int32, (256, 256), 1)
    source = (to // 64) * 64 + (to % 16) * 4 + (to % 64) // 16
    picks = (at == source).astype(F32).astype(BF16)
    for q in range(16):
        rows = slice(256 * q, 256 * q + 256)
        mixed_ref[rows, :] = jnp.dot(
            picks, basis[rows], preferred_element_type=F32
        ).astype(BF16)


def folded(columns):
    rows = []
    for x in range(0, 8, 2):
        turned = jnp.concatenate(columns[x : x + 2], axis=1).T
        for h in range(2):
            parts = [turned[64 * h + 16 * q : 64 * h + 16 * q + 16] for q in range(4)]
            rows.append(jnp.concatenate(parts, axis=1))
    return jnp.swapaxes(jnp.stack(rows, axis=0), 0, 1)


def fold_kernel(slab_ref, top_ref, bottom_out, top_out):
    for g in range(4):
        both = []
        for h in range(2):
            block = slab_ref[2 * g + h].astype(F32).reshape(16, 8, 256)
            by_r = jnp.swapaxes(block, 0, 1)
            both.append(
                folded(
                    [
                        jnp.concatenate(
                            [by_r[r][:, 64 * l : 64 * l + 64] for l in range(4)], axis=0
                        )
                        for r in range(8)
                    ]
                )
            )
        bottom_out[:, 16 * g : 16 * g + 16, :] = jnp.concatenate(both, axis=1).astype(BF16)
    block = top_ref[...].astype(F32)
    halves = [jnp.swapaxes(block[:, 8 * h : 8 * h + 8], 0, 1) for h in range(2)]
    for g in range(2):
        both = []
        for u in range(2 * g, 2 * g + 2):
            rows = jnp.concatenate([halves[l // 2][4 * (l % 2) + u] for l in range(4)], axis=0)
            both.append(folded([rows[:, 64 * r : 64 * r + 64] for r in range(8)]))
        top_out[:, 16 * g : 16 * g + 16, :] = jnp.concatenate(both, axis=1).astype(BF16)


def vmem_call(kernel, outs, args, scalars=0, limit=48):
    spec = pl.BlockSpec(memory_space=pltpu.VMEM)
    scalar = pl.BlockSpec(memory_space=pltpu.SMEM)
    return pl.pallas_call(
        kernel,
        out_shape=tuple(outs),
        in_specs=[scalar] * scalars + [spec] * (len(args) - scalars),
        out_specs=tuple([spec] * len(outs)),
        compiler_params=pltpu.CompilerParams(vmem_limit_bytes=limit << 20),
    )(*args)


def fill_diagonal(diag_ref, slot, block):
    for i in range(4):
        diag_ref[slot, 64 * i : 64 * i + 64, 64 * i : 64 * i + 64] = block


def contract_kernel(
    bottom_ref, first_ref, basis_ref, tops_ref, out_ref, top_ref, wide_ref, diag_ref, even_ref, odd_ref, low_ref, high_ref
):
    step_id = pl.program_id(0)
    rows_here = A_BLOCK * D

    @pl.when(step_id == 0)
    def _():
        diag_ref[...] = jnp.zeros_like(diag_ref)
        for q in range(16):
            part = tops_ref[:, q].astype(F32).reshape(8, 4, 8, 256)
            part = jnp.transpose(part, (1, 0, 2, 3)).reshape(256, 256)
            top_ref[256 * q : 256 * q + 256, :] = part.T.astype(BF16)

    bottom = bottom_ref[...]

    def sections(group, carry):
        for j in range(UNROLL):
            fill_diagonal(diag_ref, j, first_ref[group * UNROLL + j])
        for j in range(UNROLL):
            section = jnp.dot(bottom, diag_ref[j], preferred_element_type=F32).astype(BF16)
            start = pl.multiple_of((group * UNROLL + j) * D, D)
            for q in range(16):
                wide_ref[pl.ds(start, D), 256 * q : 256 * q + 256] = section[64 * q : 64 * q + 64]
        return carry

    lax.fori_loop(0, A_BLOCK // UNROLL, sections, 0)
    second = jnp.dot(wide_ref[...], top_ref[...], preferred_element_type=F32)
    base = pl.multiple_of(step_id * rows_here, rows_here)
    even_ref[pl.ds(base, rows_here), :] = second[:, :128]
    odd_ref[pl.ds(base, rows_here), :] = second[:, 128:]

    @pl.when(step_id == RANK // A_BLOCK - 1)
    def _():
        low_ref[...] = jnp.zeros_like(low_ref)
        high_ref[...] = jnp.zeros_like(high_ref)

        def products(group, carry):
            total = jnp.zeros((RANK, 256), F32)
            for j in range(UNROLL):
                fill_diagonal(diag_ref, j, basis_ref[group * UNROLL + j])
            for j in range(UNROLL):
                picked = pl.ds(group * UNROLL + j, RANK, stride=D)
                rows = jnp.concatenate([even_ref[picked, :], odd_ref[picked, :]], axis=1)
                total = total + jnp.dot(
                    rows.astype(BF16), diag_ref[j], preferred_element_type=F32
                )
            low_ref[...] += total[:, :128]
            high_ref[...] += total[:, 128:]
            return carry

        lax.fori_loop(0, D // UNROLL, products, 0)
        for u in range(4):
            ref = high_ref if u // 2 else low_ref
            lanes = slice(64 * (u % 2), 64 * (u % 2) + 64)
            pair = [ref[pl.ds(odd, RANK // 2, stride=2), :][:, lanes] for odd in range(2)]
            out_ref[u] = jnp.concatenate(pair, axis=1)


def contract(bottom, first, basis, top):
    whole = lambda *dims: pl.BlockSpec(dims, lambda i: (0,) * len(dims))
    return pl.pallas_call(
        contract_kernel,
        grid=(RANK // A_BLOCK,),
        out_shape=jax.ShapeDtypeStruct((4, RANK // 2, 2 * RANK), F32),
        in_specs=[
            whole(1024, 256),
            pl.BlockSpec((A_BLOCK, D, D), lambda i: (i, 0, 0)),
            whole(D, D, RANK),
            whole(8, 16, 32, 256),
        ],
        out_specs=whole(4, RANK // 2, 2 * RANK),
        scratch_shapes=[
            pltpu.VMEM((D * D, 256), BF16),
            pltpu.VMEM((A_BLOCK * D, D * D), BF16),
            pltpu.VMEM((UNROLL, 256, 256), BF16),
            pltpu.VMEM((RANK * D, 128), F32),
            pltpu.VMEM((RANK * D, 128), F32),
            pltpu.VMEM((RANK, 128), F32),
            pltpu.VMEM((RANK, 128), F32),
        ],
        compiler_params=pltpu.CompilerParams(vmem_limit_bytes=56 << 20),
    )(bottom, first, basis, top)


def swapped_pairs(tiles):
    lane = lax.broadcasted_iota(jnp.int32, (8, 128), 1)
    stack = jnp.swapaxes(jnp.stack(tiles, axis=0), 0, 1)
    out = []
    for j in range(4):
        a, b = stack[2 * j], stack[2 * j + 1]
        low = jnp.where(lane < 64, a, pltpu.roll(b, 64, 1))
        high = jnp.where(lane < 64, pltpu.roll(a, 64, 1), b)
        out.append((low, high))
    return out


def partial_kernel(
    core_ref, up_ref, down_ref, scale_ref, all_ref, up_out, down_out, up_acc, down_acc
):
    blocks = [all_ref[c] for c in range(4)]
    order = [(t // 4 + 2 * y, t % 4) for t in range(8) for y in range(2)]
    right = jnp.concatenate([blocks[c][:, 64 * m : 64 * m + 64] for c, m in order], axis=1)
    up_acc[...] = jnp.dot(up_ref[...], right, preferred_element_type=F32) * scale_ref[...]
    rows = []
    for c, m in order:
        part = blocks[c][:, 64 * m : 64 * m + 64]
        rows.append(jnp.concatenate([part[64 * r : 64 * r + 64] for r in range(8)], axis=1))
    down_acc[...] = lax.dot_general(
        down_ref[...],
        jnp.concatenate(rows, axis=0),
        (((1,), (1,)), ((), ())),
        preferred_element_type=F32,
    )
    core = core_ref[0]
    for left in range(4):
        for high in range(8):
            at = 64 * left + 8 * high
            slot = 1 - core if high % 2 else core
            for which, acc in enumerate((down_acc, up_acc)):
                pieces = swapped_pairs(
                    [acc[at : at + 8, 128 * t : 128 * t + 128] for t in range(8)]
                )
                for j, piece in enumerate(pieces):
                    value = jnp.concatenate(piece, axis=0).astype(BF16)
                    lanes = slice(128 * j, 128 * j + 128)
                    if which == 0:
                        down_out[high, left, 0, :, lanes] = value
                    else:
                        up_out[slot, high // 2, left, 0, :, lanes] = value


def partials(core, up, down, scale, by_cols):
    whole = lambda *dims: pl.BlockSpec(dims, lambda i: (0,) * len(dims))
    return pl.pallas_call(
        partial_kernel,
        grid=(4,),
        out_shape=(
            jax.ShapeDtypeStruct((2, 4, 4, 4, 16, 512), BF16),
            jax.ShapeDtypeStruct((8, 4, 4, 16, 512), BF16),
        ),
        in_specs=[
            pl.BlockSpec(memory_space=pltpu.SMEM),
            whole(256, 512),
            whole(256, 512),
            whole(1, 1024),
            pl.BlockSpec((4, 512, 256), lambda i: (i, 0, 0)),
        ],
        out_specs=(
            pl.BlockSpec((2, 4, 4, 1, 16, 512), lambda i: (0, 0, 0, i, 0, 0)),
            pl.BlockSpec((8, 4, 1, 16, 512), lambda i: (0, 0, i, 0, 0)),
        ),
        scratch_shapes=[pltpu.VMEM((256, 1024), F32), pltpu.VMEM((256, 1024), F32)],
        compiler_params=pltpu.CompilerParams(vmem_limit_bytes=48 << 20),
    )(core, up, down, scale, by_cols)


def side_kernel(
    core_ref, mine_ref, other_ref, inner_ref, rows_ref, lanes_ref, all_ref, out_ref, acc_ref
):
    step = pl.program_id(0)

    @pl.when(step == 0)
    def _():
        acc_ref[...] = jnp.zeros_like(acc_ref)

    order = [s + 4 * y for s in range(4) for y in range(2)]
    left, right = [], []
    for c in range(4):
        own = jnp.concatenate(
            [mine_ref[:, c].reshape(128, 256), other_ref[:, c].reshape(128, 256)], axis=0
        )
        left.append((own.astype(F32) * inner_ref[c]).astype(BF16))
        block = all_ref[c]
        right.append(jnp.concatenate([block[64 * s : 64 * s + 64] for s in order], axis=0))
    acc_ref[...] += lax.dot_general(
        jnp.concatenate(left, axis=1),
        jnp.concatenate(right, axis=1),
        (((1,), (1,)), ((), ())),
        preferred_element_type=F32,
    )

    @pl.when(step == 3)
    def _():
        core = core_ref[0]
        for s in range(16):
            row = 2 * ((s % 8) // 2) + (core if s < 8 else 1 - core)
            first = pl.multiple_of(32 * row + 16 * (s % 2), 16)
            scaled = (
                acc_ref[16 * s : 16 * s + 16, :] * rows_ref[pl.ds(first, 16), :] * lanes_ref[...]
            )
            tiles = [
                scaled[8 * t : 8 * t + 8, 128 * q : 128 * q + 128]
                for t in range(2)
                for q in range(4)
            ]
            pieces = swapped_pairs(tiles)
            for odd in range(2):
                low = jnp.concatenate([pieces[2 * odd][0], pieces[2 * odd + 1][0]], axis=1)
                high = jnp.concatenate([pieces[2 * odd][1], pieces[2 * odd + 1][1]], axis=1)
                for t in range(2):
                    out_ref[8 * row + 4 * (s % 2) + 2 * t + odd] = jnp.concatenate(
                        [low[4 * t : 4 * t + 4], high[4 * t : 4 * t + 4]], axis=0
                    )


def side_gram(core, mine, other, inner, rows, lanes, by_cols):
    whole = lambda *dims: pl.BlockSpec(dims, lambda i: (0,) * len(dims))
    part = pl.BlockSpec((4, 4, 32, 256), lambda i: (0, i, 0, 0))
    return pl.pallas_call(
        side_kernel,
        grid=(4,),
        out_shape=jax.ShapeDtypeStruct((D, 8, 256), F32),
        in_specs=[
            pl.BlockSpec(memory_space=pltpu.SMEM),
            part,
            part,
            pl.BlockSpec((4, 1, 256), lambda i: (i, 0, 0)),
            whole(256, 1),
            whole(1, 512),
            pl.BlockSpec((4, 512, 256), lambda i: (i, 0, 0)),
        ],
        out_specs=whole(D, 8, 256),
        scratch_shapes=[pltpu.VMEM((256, 512), F32)],
        compiler_params=pltpu.CompilerParams(vmem_limit_bytes=48 << 20),
    )(core, mine, other, inner, rows, lanes, by_cols)


def store_gram(acc_ref, high_ref, low_ref):
    for a_high in range(2):
        for x_high in range(8):
            tiles = []
            for a_low in range(2):
                at = 64 * (2 * a_high + a_low) + 8 * x_high
                for q in range(4):
                    tiles.append(acc_ref[at : at + 8, 128 * q : 128 * q + 128])
            for j, piece in enumerate(swapped_pairs(tiles)):
                high, low = two_parts(jnp.concatenate(piece, axis=0))
                lanes = slice(512 * x_high + 128 * j, 512 * x_high + 128 * j + 128)
                high_ref[16 * a_high : 16 * a_high + 16, lanes] = high
                low_ref[16 * a_high : 16 * a_high + 16, lanes] = low


def left_gram_kernel(parts_ref, down_ref, high_ref, low_ref, up_ref, acc_ref):
    @pl.when(pl.program_id(0) == 0)
    def _():
        total = parts_ref[0].astype(F32)
        for z in range(1, 4):
            total = total + parts_ref[z].astype(F32)
        up_ref[...] = total.astype(BF16)

    acc_ref[...] = lax.dot_general(
        up_ref[...],
        down_ref[...].reshape(512, 512),
        (((1,), (1,)), ((), ())),
        preferred_element_type=F32,
    )
    store_gram(acc_ref, high_ref, low_ref)


def left_gram(up, down):
    out = jax.ShapeDtypeStruct((256, D * D), BF16)
    out_spec = pl.BlockSpec((32, D * D), lambda i: (i, 0))
    return pl.pallas_call(
        left_gram_kernel,
        grid=(8,),
        out_shape=(out, out),
        in_specs=[
            pl.BlockSpec((4, 256, 512), lambda i: (0, 0, 0)),
            pl.BlockSpec((2, 256, 512), lambda i: (i, 0, 0)),
        ],
        out_specs=(out_spec, out_spec),
        scratch_shapes=[pltpu.VMEM((256, 512), BF16), pltpu.VMEM((256, 512), F32)],
        compiler_params=pltpu.CompilerParams(vmem_limit_bytes=48 << 20),
    )(up, down)


def down_gram_kernel(core_ref, mine_ref, other_ref, down_ref, high_ref, low_ref, acc_ref):
    step = pl.program_id(0)

    @pl.when(step == 0)
    def _():
        acc_ref[...] = jnp.zeros_like(acc_ref)

    halves = by_core(core_ref, mine_ref[...].astype(F32), other_ref[...].astype(F32))
    side = jnp.stack([h.reshape(4, 16, 8, 256) for h in halves], axis=1)
    side = jnp.transpose(side.reshape(8, 16, 8, 256), (1, 0, 2, 3)).reshape(1024, 256)
    acc_ref[...] += lax.dot_general(
        side.astype(BF16),
        down_ref[...].reshape(1024, 512),
        (((0,), (0,)), ((), ())),
        preferred_element_type=F32,
    )

    @pl.when(step == 3)
    def _():
        store_gram(acc_ref, high_ref, low_ref)


def down_gram(core, mine, other, down):
    out = jax.ShapeDtypeStruct((32, D * D), BF16)
    out_spec = pl.BlockSpec((32, D * D), lambda i: (0, 0))
    part = pl.BlockSpec((4, 128, 256), lambda i: (0, i, 0))
    return pl.pallas_call(
        down_gram_kernel,
        grid=(4,),
        out_shape=(out, out),
        in_specs=[
            pl.BlockSpec(memory_space=pltpu.SMEM),
            part,
            part,
            pl.BlockSpec((4, 256, 512), lambda i: (i, 0, 0)),
        ],
        out_specs=(out_spec, out_spec),
        scratch_shapes=[pltpu.VMEM((256, 512), F32)],
        compiler_params=pltpu.CompilerParams(vmem_limit_bytes=48 << 20),
    )(core, mine, other, down)


def body(tensor, bond_weights, start_blocks):
    row_index = lax.axis_index(ROW)

    def both_cores(shard):
        mine = from_everyone(shard, "z")
        return mine, lax.ppermute(mine, "core", [(0, 1), (1, 0)])

    where = jnp.reshape(lax.axis_index("core"), (1,)).astype(jnp.int32)
    horizontal = bond_weights[0]
    vertical = bond_weights[1]
    horiz_rows = lax.dynamic_slice_in_dim(horizontal, row_index * 8, 8)
    grid = tensor.reshape(4, 8, D, D)
    flat = jnp.transpose(grid, (1, 2, 0, 3)).reshape(512, 256)
    by_cols = lax.all_gather(flat, COL)

    square = vertical * vertical
    rows_square = horiz_rows * horiz_rows
    turned = flat.T.astype(F32)
    up_scale = (rows_square[:, None] * square[None, :]).reshape(1, 512)
    own_up = (turned * up_scale * jnp.tile(vertical, 4)[:, None]).astype(BF16)
    weighted = (turned * jnp.tile(vertical, 8)[None, :]).astype(BF16)
    top_piece = jnp.swapaxes(weighted.reshape(4, 16, 4, 512), 0, 1).reshape(16, 16, 512)
    top_got = lax.all_to_all(top_piece, COL, 0, 0, tiled=True)

    def everywhere(y):
        mine = lax.all_to_all(
            jnp.broadcast_to(y, (64, 32, 2 * RANK)), SAME_CORE, 0, 0, tiled=True
        ).reshape(2048, 2 * RANK)
        return mine, lax.ppermute(mine, "core", [(0, 1), (1, 0)])

    first_vectors = everywhere(start_blocks.reshape(32, 2 * RANK))
    own_down = grid.astype(F32) * rows_square[None, :, None, None] * square
    own_down = jnp.transpose(own_down.astype(BF16), (0, 2, 1, 3)).reshape(256, 512)

    by_cols, first_vectors, top_got = lax.optimization_barrier((by_cols, first_vectors, top_got))
    lane_scale = jnp.tile(vertical, 16)[None, :]
    part_up, part_down = partials(where, own_up, own_down, lane_scale, by_cols)
    left_down = lax.psum_scatter(
        part_down.reshape(8, 4, D, 512), ROW, scatter_dimension=0, tiled=True
    )
    received = lax.ppermute(part_up[1], "core", [(0, 1), (1, 0)])
    side_piece = lax.dynamic_index_in_dim(
        by_cols.reshape(16, 8, 16, 4, 256), lax.axis_index(COL), 2, keepdims=False
    )
    side_own = both_cores(side_piece.reshape(16, 32, 256))

    inner = ((horizontal * horizontal)[:, None] * square[None, :]).reshape(16, 1, 256)
    lanes = jnp.repeat(jnp.transpose(horiz_rows.reshape(2, 4)).reshape(8), D)[None, :]
    side = side_gram(
        where, *side_own, inner, jnp.repeat(horizontal, 4)[:, None], lanes, by_cols
    )

    slab_part = by_cols.reshape(16, 8, D, 256)[:, :, :8]
    slab_part = jnp.transpose(slab_part, (2, 0, 1, 3)).reshape(8, 128, 256)
    slab = lax.all_to_all(slab_part, ROW, split_axis=0, concat_axis=0, tiled=True)
    left_down, slab, side = lax.optimization_barrier((left_down, slab, side))
    down_all = lax.all_gather(left_down.reshape(256, 512), COL)
    pair_up = (part_up[0].astype(F32) + received.astype(F32)).astype(BF16)
    left_up = lax.all_to_all(pair_up.reshape(4, 256, 512), "z", 0, 0, tiled=True)
    side_all = both_cores(side.astype(BF16).reshape(512, 256))
    bottom, top_rows = vmem_call(
        fold_kernel,
        (
            jax.ShapeDtypeStruct((16, D, 256), BF16),
            jax.ShapeDtypeStruct((16, 32, 256), BF16),
        ),
        (slab, top_got),
    )
    down_all, bottom, top_rows, side_all, left_up = lax.optimization_barrier(
        (down_all, bottom, top_rows, side_all, left_up)
    )
    grams = (*left_gram(left_up, down_all), *down_gram(where, *side_all, down_all))
    top_rows, grams = lax.optimization_barrier((top_rows, grams))
    top = lax.all_gather(top_rows, ROW)
    z_outs = (
        jax.ShapeDtypeStruct((8, 16, 2 * RANK), F32),
        jax.ShapeDtypeStruct((32, 2 * RANK), F32),
    )
    inv_out = jax.ShapeDtypeStruct((2 * RANK, 2 * RANK), F32)

    def local_images(z_left, z_down):
        z_left = jnp.sum(lax.all_to_all(z_left, ROW, 0, 0, tiled=True), axis=0)
        z_left = jnp.concatenate([z_left[:, :RANK], z_left[:, RANK:]], axis=0)
        z = jnp.concatenate([z_left, z_down[:, RANK:]], axis=1)
        z = jnp.transpose(z.reshape(2, 2, 2, 4, 2 * RANK), (0, 2, 3, 1, 4))
        return z.reshape(32, 2 * RANK)

    def apply(y, inverse):
        return lax.dot_general(y, inverse, (((1,), (1,)), ((), ())), precision=HIGHEST)

    vectors = first_vectors
    for step in range(3):
        y = local_images(*vmem_call(images_kernel, z_outs, (where, *vectors, *grams), 1))
        if step:
            y = apply(y, vmem_call(factor_kernel, (inv_out,), vectors)[0])
        vectors = everywhere(y)
    basis_out = jax.ShapeDtypeStruct((D * D, RANK), BF16)
    basis, mixed, inverse = vmem_call(
        last_kernel, (basis_out, basis_out, inv_out), (where, *vectors), 1
    )
    projectors = apply(y, inverse).reshape(4, 8, 2 * RANK)
    first = jnp.transpose(mixed.reshape(16, 4, D, RANK), (3, 1, 0, 2)).reshape(RANK, D, D)
    new_tensor = contract(bottom.reshape(1024, 256), first, basis.reshape(D, D, RANK), top)
    return (projectors, new_tensor.reshape(4, 1, RANK * RANK))


def solution(mesh):
    axes = ("z", "core", "col_0", "col_1")
    torus = Mesh(mesh.devices.reshape(mesh.shape["row"] // 2, 2, 4, 4), axes)
    placed = (P(COL, ROW, None), P(), P(COL, ROW, None))
    return jax.shard_map(
        body,
        mesh=torus,
        in_specs=placed,
        out_specs=(P(COL, ROW, None), P(COL, ROW, None)),
        check_vma=False,
    )
```

```python
import jax
import jax.numpy as jnp
from jax import lax
from jax.experimental import pallas as pl
from jax.experimental.pallas import tpu as pltpu
from jax.sharding import Mesh
from jax.sharding import PartitionSpec as P

D = 64
RANK = 64
COL = ("col_0", "col_1")
ROW = ("z", "core")
SAME_CORE = ("z", "col_0", "col_1")
HIGHEST = lax.Precision.HIGHEST
F32 = jnp.float32
BF16 = jnp.bfloat16
A_BLOCK = 16
UNROLL = 8


def from_everyone(shard, axis):
    copies = jnp.broadcast_to(shard, (lax.axis_size(axis), *shard.shape))
    return lax.all_to_all(copies, axis, split_axis=0, concat_axis=0, tiled=True)


def two_parts(x):
    high = x.astype(BF16)
    return high, (x - high.astype(F32)).astype(BF16)


def by_core(core_ref, mine, other):
    first = core_ref[0] == 0
    return jnp.where(first, mine, other), jnp.where(first, other, mine)


def in_index_order(core_ref, mine_ref, other_ref):
    halves = by_core(core_ref, mine_ref[...], other_ref[...])
    y = jnp.stack([h.reshape(4, D, 8, 2 * RANK) for h in halves], axis=1)
    y = jnp.transpose(y.reshape(8, D, 8, 2 * RANK), (1, 0, 2, 3))
    return y.reshape(D * D, 2 * RANK)


def inverse_factors(mats):
    n = RANK
    count = n // 8
    rows_at = lax.broadcasted_iota(jnp.int32, (8, 2 * n), 0)
    lanes_at = lax.broadcasted_iota(jnp.int32, (8, 2 * n), 1)
    sets = []
    for c in mats:
        blocks = []
        for i in range(count):
            unit = (lanes_at == rows_at + (n + 8 * i)).astype(F32)
            part = jnp.concatenate([c[8 * i : 8 * i + 8], jnp.zeros((8, n), F32)], axis=1)
            blocks.append(part + unit)
        sets.append((blocks, []))
    for b in range(count):
        panels = []
        for blocks, _ in sets:
            columns = [
                {
                    i: jnp.broadcast_to(blocks[i][:, 8 * b + j : 8 * b + j + 1], (8, 2 * n))
                    for i in range(b, count)
                }
                for j in range(8)
            ]
            rows = [jnp.broadcast_to(blocks[b][j : j + 1], (8, 2 * n)) for j in range(8)]
            panels.append((columns, rows, []))
        for j in range(8):
            for (blocks, pivots), (columns, rows, scaled) in zip(sets, panels):
                own = columns[j][b]
                inverse = 1.0 / own[j : j + 1]
                pivots.append(own[j : j + 1])
                scaled.append(rows[j] * inverse)
                for k in range(j + 1, 8):
                    factor = columns[k][b][j : j + 1] * inverse
                    rows[k] = rows[k] - own[k : k + 1] * scaled[j]
                    for i in range(b, count):
                        columns[k][i] = columns[k][i] - columns[j][i] * factor
        for (blocks, _), (columns, rows, scaled) in zip(sets, panels):
            whole = rows[0]
            for j in range(1, 8):
                whole = jnp.where(rows_at == j, rows[j], whole)
            blocks[b] = whole
            for i in range(b + 1, count):
                for j in range(8):
                    blocks[i] = blocks[i] - columns[j][i] * scaled[j]
    out = []
    for blocks, pivots in sets:
        done = []
        for i in range(count):
            pivot = jnp.broadcast_to(pivots[8 * i], (8, 2 * n))
            for j in range(1, 8):
                pivot = jnp.where(rows_at == j, pivots[8 * i + j], pivot)
            done.append((blocks[i] / jnp.sqrt(pivot))[:, n:])
        out.append(jnp.concatenate(done, axis=0))
    return out


def correlation(y):
    return lax.dot_general(
        y, y, (((0,), (0,)), ((), ())), precision=HIGHEST, preferred_element_type=F32
    )


def factors_of(c):
    return inverse_factors([c[:RANK, :RANK], c[RANK:, RANK:]])


def store_inverse(inv_ref, left, down):
    zero = jnp.zeros((RANK, RANK), F32)
    inv_ref[:RANK, :] = jnp.concatenate([left, zero], axis=1)
    inv_ref[RANK:, :] = jnp.concatenate([zero, down], axis=1)


def images_of(y, gl_high, gl_low, gd_high, gd_low, zl_ref, zd_ref):
    y_high, y_low = two_parts(y)
    both = jnp.concatenate([y_high, y_low], axis=1)

    def product(high, low):
        main = jnp.dot(high[...], both, preferred_element_type=F32)
        rest = jnp.dot(low[...], y_high, preferred_element_type=F32)
        return main[:, : 2 * RANK] + main[:, 2 * RANK :] + rest

    z = product(gl_high, gl_low)[:, :RANK].reshape(8, 32, RANK)
    zl_ref[...] = jnp.concatenate([z[:, :16], z[:, 16:]], axis=2)
    zd_ref[...] = product(gd_high, gd_low)


def images_kernel(core_ref, mine_ref, other_ref, glh, gll, gdh, gdl, zl_ref, zd_ref):
    y = in_index_order(core_ref, mine_ref, other_ref)
    images_of(y, glh, gll, gdh, gdl, zl_ref, zd_ref)


def factor_kernel(mine_ref, other_ref, inv_ref):
    c = correlation(mine_ref[...]) + correlation(other_ref[...])
    store_inverse(inv_ref, *factors_of(c))


def last_kernel(core_ref, mine_ref, other_ref, basis_ref, mixed_ref, inv_ref):
    c = correlation(mine_ref[...]) + correlation(other_ref[...])
    left, down = factors_of(c)
    store_inverse(inv_ref, left, down)
    y = in_index_order(core_ref, mine_ref, other_ref)[:, :RANK]
    y_high, y_low = two_parts(y)
    l_high, l_low = two_parts(left.T)
    basis = jnp.dot(
        jnp.concatenate([y_high, y_low, y_high], axis=1),
        jnp.concatenate([l_high, l_high, l_low], axis=0),
        preferred_element_type=F32,
    )
    basis = basis.astype(BF16)
    basis_ref[...] = basis
    to = lax.broadcasted_iota(jnp.int32, (256, 256), 0)
    at = lax.broadcasted_iota(jnp.int32, (256, 256), 1)
    source = (to // 64) * 64 + (to % 16) * 4 + (to % 64) // 16
    picks = (at == source).astype(F32).astype(BF16)
    for q in range(16):
        rows = slice(256 * q, 256 * q + 256)
        mixed_ref[rows, :] = jnp.dot(
            picks, basis[rows], preferred_element_type=F32
        ).astype(BF16)


def folded(columns):
    rows = []
    for x in range(0, 8, 2):
        turned = jnp.concatenate(columns[x : x + 2], axis=1).T
        for h in range(2):
            parts = [turned[64 * h + 16 * q : 64 * h + 16 * q + 16] for q in range(4)]
            rows.append(jnp.concatenate(parts, axis=1))
    return jnp.swapaxes(jnp.stack(rows, axis=0), 0, 1)


def fold_kernel(slab_ref, top_ref, bottom_out, top_out):
    for g in range(4):
        both = []
        for h in range(2):
            block = slab_ref[2 * g + h].astype(F32).reshape(16, 8, 256)
            by_r = jnp.swapaxes(block, 0, 1)
            both.append(
                folded(
                    [
                        jnp.concatenate(
                            [by_r[r][:, 64 * l : 64 * l + 64] for l in range(4)], axis=0
                        )
                        for r in range(8)
                    ]
                )
            )
        bottom_out[:, 16 * g : 16 * g + 16, :] = jnp.concatenate(both, axis=1).astype(BF16)
    block = top_ref[...].astype(F32)
    halves = [jnp.swapaxes(block[:, 8 * h : 8 * h + 8], 0, 1) for h in range(2)]
    for g in range(2):
        both = []
        for u in range(2 * g, 2 * g + 2):
            rows = jnp.concatenate([halves[l // 2][4 * (l % 2) + u] for l in range(4)], axis=0)
            both.append(folded([rows[:, 64 * r : 64 * r + 64] for r in range(8)]))
        top_out[:, 16 * g : 16 * g + 16, :] = jnp.concatenate(both, axis=1).astype(BF16)


def vmem_call(kernel, outs, args, scalars=0, limit=48):
    spec = pl.BlockSpec(memory_space=pltpu.VMEM)
    scalar = pl.BlockSpec(memory_space=pltpu.SMEM)
    return pl.pallas_call(
        kernel,
        out_shape=tuple(outs),
        in_specs=[scalar] * scalars + [spec] * (len(args) - scalars),
        out_specs=tuple([spec] * len(outs)),
        compiler_params=pltpu.CompilerParams(vmem_limit_bytes=limit << 20),
    )(*args)


def fill_diagonal(diag_ref, slot, block):
    for i in range(4):
        diag_ref[slot, 64 * i : 64 * i + 64, 64 * i : 64 * i + 64] = block


def contract_kernel(
    bottom_ref, first_ref, basis_ref, tops_ref, out_ref, top_ref, wide_ref, diag_ref, even_ref, odd_ref, low_ref, high_ref
):
    step_id = pl.program_id(0)
    rows_here = A_BLOCK * D

    @pl.when(step_id == 0)
    def _():
        diag_ref[...] = jnp.zeros_like(diag_ref)
        for q in range(16):
            part = tops_ref[:, q].astype(F32).reshape(8, 4, 8, 256)
            part = jnp.transpose(part, (1, 0, 2, 3)).reshape(256, 256)
            top_ref[256 * q : 256 * q + 256, :] = part.T.astype(BF16)

    bottom = bottom_ref[...]

    def sections(group, carry):
        for j in range(UNROLL):
            fill_diagonal(diag_ref, j, first_ref[group * UNROLL + j])
        for j in range(UNROLL):
            section = jnp.dot(bottom, diag_ref[j], preferred_element_type=F32).astype(BF16)
            start = pl.multiple_of((group * UNROLL + j) * D, D)
            for q in range(16):
                wide_ref[pl.ds(start, D), 256 * q : 256 * q + 256] = section[64 * q : 64 * q + 64]
        return carry

    lax.fori_loop(0, A_BLOCK // UNROLL, sections, 0)
    second = jnp.dot(wide_ref[...], top_ref[...], preferred_element_type=F32)
    base = pl.multiple_of(step_id * rows_here, rows_here)
    even_ref[pl.ds(base, rows_here), :] = second[:, :128]
    odd_ref[pl.ds(base, rows_here), :] = second[:, 128:]

    @pl.when(step_id == RANK // A_BLOCK - 1)
    def _():
        low_ref[...] = jnp.zeros_like(low_ref)
        high_ref[...] = jnp.zeros_like(high_ref)

        def products(group, carry):
            total = jnp.zeros((RANK, 256), F32)
            for j in range(UNROLL):
                fill_diagonal(diag_ref, j, basis_ref[group * UNROLL + j])
            for j in range(UNROLL):
                picked = pl.ds(group * UNROLL + j, RANK, stride=D)
                rows = jnp.concatenate([even_ref[picked, :], odd_ref[picked, :]], axis=1)
                total = total + jnp.dot(
                    rows.astype(BF16), diag_ref[j], preferred_element_type=F32
                )
            low_ref[...] += total[:, :128]
            high_ref[...] += total[:, 128:]
            return carry

        lax.fori_loop(0, D // UNROLL, products, 0)
        for u in range(4):
            ref = high_ref if u // 2 else low_ref
            lanes = slice(64 * (u % 2), 64 * (u % 2) + 64)
            pair = [ref[pl.ds(odd, RANK // 2, stride=2), :][:, lanes] for odd in range(2)]
            out_ref[u] = jnp.concatenate(pair, axis=1)


def contract(bottom, first, basis, top):
    whole = lambda *dims: pl.BlockSpec(dims, lambda i: (0,) * len(dims))
    return pl.pallas_call(
        contract_kernel,
        grid=(RANK // A_BLOCK,),
        out_shape=jax.ShapeDtypeStruct((4, RANK // 2, 2 * RANK), F32),
        in_specs=[
            whole(1024, 256),
            pl.BlockSpec((A_BLOCK, D, D), lambda i: (i, 0, 0)),
            whole(D, D, RANK),
            whole(8, 16, 32, 256),
        ],
        out_specs=whole(4, RANK // 2, 2 * RANK),
        scratch_shapes=[
            pltpu.VMEM((D * D, 256), BF16),
            pltpu.VMEM((A_BLOCK * D, D * D), BF16),
            pltpu.VMEM((UNROLL, 256, 256), BF16),
            pltpu.VMEM((RANK * D, 128), F32),
            pltpu.VMEM((RANK * D, 128), F32),
            pltpu.VMEM((RANK, 128), F32),
            pltpu.VMEM((RANK, 128), F32),
        ],
        compiler_params=pltpu.CompilerParams(vmem_limit_bytes=56 << 20),
    )(bottom, first, basis, top)


def swapped_pairs(tiles):
    lane = lax.broadcasted_iota(jnp.int32, (8, 128), 1)
    stack = jnp.swapaxes(jnp.stack(tiles, axis=0), 0, 1)
    out = []
    for j in range(4):
        a, b = stack[2 * j], stack[2 * j + 1]
        low = jnp.where(lane < 64, a, pltpu.roll(b, 64, 1))
        high = jnp.where(lane < 64, pltpu.roll(a, 64, 1), b)
        out.append((low, high))
    return out


def partial_kernel(
    core_ref, up_ref, down_ref, scale_ref, all_ref, up_out, down_out, up_acc, down_acc
):
    blocks = [all_ref[c] for c in range(4)]
    order = [(t // 4 + 2 * y, t % 4) for t in range(8) for y in range(2)]
    right = jnp.concatenate([blocks[c][:, 64 * m : 64 * m + 64] for c, m in order], axis=1)
    up_acc[...] = jnp.dot(up_ref[...], right, preferred_element_type=F32) * scale_ref[...]
    rows = []
    for c, m in order:
        part = blocks[c][:, 64 * m : 64 * m + 64]
        rows.append(jnp.concatenate([part[64 * r : 64 * r + 64] for r in range(8)], axis=1))
    down_acc[...] = lax.dot_general(
        down_ref[...],
        jnp.concatenate(rows, axis=0),
        (((1,), (1,)), ((), ())),
        preferred_element_type=F32,
    )
    core = core_ref[0]
    for left in range(4):
        for high in range(8):
            at = 64 * left + 8 * high
            slot = 1 - core if high % 2 else core
            for which, acc in enumerate((down_acc, up_acc)):
                pieces = swapped_pairs(
                    [acc[at : at + 8, 128 * t : 128 * t + 128] for t in range(8)]
                )
                for j, piece in enumerate(pieces):
                    value = jnp.concatenate(piece, axis=0).astype(BF16)
                    lanes = slice(128 * j, 128 * j + 128)
                    if which == 0:
                        down_out[high, left, 0, :, lanes] = value
                    else:
                        up_out[slot, high // 2, left, 0, :, lanes] = value


def partials(core, up, down, scale, by_cols):
    whole = lambda *dims: pl.BlockSpec(dims, lambda i: (0,) * len(dims))
    return pl.pallas_call(
        partial_kernel,
        grid=(4,),
        out_shape=(
            jax.ShapeDtypeStruct((2, 4, 4, 4, 16, 512), BF16),
            jax.ShapeDtypeStruct((8, 4, 4, 16, 512), BF16),
        ),
        in_specs=[
            pl.BlockSpec(memory_space=pltpu.SMEM),
            whole(256, 512),
            whole(256, 512),
            whole(1, 1024),
            pl.BlockSpec((4, 512, 256), lambda i: (i, 0, 0)),
        ],
        out_specs=(
            pl.BlockSpec((2, 4, 4, 1, 16, 512), lambda i: (0, 0, 0, i, 0, 0)),
            pl.BlockSpec((8, 4, 1, 16, 512), lambda i: (0, 0, i, 0, 0)),
        ),
        scratch_shapes=[pltpu.VMEM((256, 1024), F32), pltpu.VMEM((256, 1024), F32)],
        compiler_params=pltpu.CompilerParams(vmem_limit_bytes=48 << 20),
    )(core, up, down, scale, by_cols)


def side_kernel(
    core_ref, mine_ref, other_ref, inner_ref, rows_ref, lanes_ref, all_ref, out_ref, acc_ref
):
    step = pl.program_id(0)

    @pl.when(step == 0)
    def _():
        acc_ref[...] = jnp.zeros_like(acc_ref)

    order = [s + 4 * y for s in range(4) for y in range(2)]
    left, right = [], []
    for c in range(4):
        own = jnp.concatenate(
            [mine_ref[:, c].reshape(128, 256), other_ref[:, c].reshape(128, 256)], axis=0
        )
        left.append((own.astype(F32) * inner_ref[c]).astype(BF16))
        block = all_ref[c]
        right.append(jnp.concatenate([block[64 * s : 64 * s + 64] for s in order], axis=0))
    acc_ref[...] += lax.dot_general(
        jnp.concatenate(left, axis=1),
        jnp.concatenate(right, axis=1),
        (((1,), (1,)), ((), ())),
        preferred_element_type=F32,
    )

    @pl.when(step == 3)
    def _():
        core = core_ref[0]
        for s in range(16):
            row = 2 * ((s % 8) // 2) + (core if s < 8 else 1 - core)
            first = pl.multiple_of(32 * row + 16 * (s % 2), 16)
            scaled = (
                acc_ref[16 * s : 16 * s + 16, :] * rows_ref[pl.ds(first, 16), :] * lanes_ref[...]
            )
            tiles = [
                scaled[8 * t : 8 * t + 8, 128 * q : 128 * q + 128]
                for t in range(2)
                for q in range(4)
            ]
            pieces = swapped_pairs(tiles)
            for odd in range(2):
                low = jnp.concatenate([pieces[2 * odd][0], pieces[2 * odd + 1][0]], axis=1)
                high = jnp.concatenate([pieces[2 * odd][1], pieces[2 * odd + 1][1]], axis=1)
                for t in range(2):
                    out_ref[8 * row + 4 * (s % 2) + 2 * t + odd] = jnp.concatenate(
                        [low[4 * t : 4 * t + 4], high[4 * t : 4 * t + 4]], axis=0
                    )


def side_gram(core, mine, other, inner, rows, lanes, by_cols):
    whole = lambda *dims: pl.BlockSpec(dims, lambda i: (0,) * len(dims))
    part = pl.BlockSpec((4, 4, 32, 256), lambda i: (0, i, 0, 0))
    return pl.pallas_call(
        side_kernel,
        grid=(4,),
        out_shape=jax.ShapeDtypeStruct((D, 8, 256), F32),
        in_specs=[
            pl.BlockSpec(memory_space=pltpu.SMEM),
            part,
            part,
            pl.BlockSpec((4, 1, 256), lambda i: (i, 0, 0)),
            whole(256, 1),
            whole(1, 512),
            pl.BlockSpec((4, 512, 256), lambda i: (i, 0, 0)),
        ],
        out_specs=whole(D, 8, 256),
        scratch_shapes=[pltpu.VMEM((256, 512), F32)],
        compiler_params=pltpu.CompilerParams(vmem_limit_bytes=48 << 20),
    )(core, mine, other, inner, rows, lanes, by_cols)


def store_gram(acc_ref, high_ref, low_ref):
    for a_high in range(2):
        for x_high in range(8):
            tiles = []
            for a_low in range(2):
                at = 64 * (2 * a_high + a_low) + 8 * x_high
                for q in range(4):
                    tiles.append(acc_ref[at : at + 8, 128 * q : 128 * q + 128])
            for j, piece in enumerate(swapped_pairs(tiles)):
                high, low = two_parts(jnp.concatenate(piece, axis=0))
                lanes = slice(512 * x_high + 128 * j, 512 * x_high + 128 * j + 128)
                high_ref[16 * a_high : 16 * a_high + 16, lanes] = high
                low_ref[16 * a_high : 16 * a_high + 16, lanes] = low


def left_gram_kernel(parts_ref, down_ref, high_ref, low_ref, up_ref, acc_ref):
    @pl.when(pl.program_id(0) == 0)
    def _():
        total = parts_ref[0].astype(F32)
        for z in range(1, 4):
            total = total + parts_ref[z].astype(F32)
        up_ref[...] = total.astype(BF16)

    acc_ref[...] = lax.dot_general(
        up_ref[...],
        down_ref[...].reshape(512, 512),
        (((1,), (1,)), ((), ())),
        preferred_element_type=F32,
    )
    store_gram(acc_ref, high_ref, low_ref)


def left_gram(up, down):
    out = jax.ShapeDtypeStruct((256, D * D), BF16)
    out_spec = pl.BlockSpec((32, D * D), lambda i: (i, 0))
    return pl.pallas_call(
        left_gram_kernel,
        grid=(8,),
        out_shape=(out, out),
        in_specs=[
            pl.BlockSpec((4, 256, 512), lambda i: (0, 0, 0)),
            pl.BlockSpec((2, 256, 512), lambda i: (i, 0, 0)),
        ],
        out_specs=(out_spec, out_spec),
        scratch_shapes=[pltpu.VMEM((256, 512), BF16), pltpu.VMEM((256, 512), F32)],
        compiler_params=pltpu.CompilerParams(vmem_limit_bytes=48 << 20),
    )(up, down)


def down_gram_kernel(core_ref, mine_ref, other_ref, down_ref, high_ref, low_ref, acc_ref):
    step = pl.program_id(0)

    @pl.when(step == 0)
    def _():
        acc_ref[...] = jnp.zeros_like(acc_ref)

    halves = by_core(core_ref, mine_ref[...].astype(F32), other_ref[...].astype(F32))
    side = jnp.stack([h.reshape(4, 16, 8, 256) for h in halves], axis=1)
    side = jnp.transpose(side.reshape(8, 16, 8, 256), (1, 0, 2, 3)).reshape(1024, 256)
    acc_ref[...] += lax.dot_general(
        side.astype(BF16),
        down_ref[...].reshape(1024, 512),
        (((0,), (0,)), ((), ())),
        preferred_element_type=F32,
    )

    @pl.when(step == 3)
    def _():
        store_gram(acc_ref, high_ref, low_ref)


def down_gram(core, mine, other, down):
    out = jax.ShapeDtypeStruct((32, D * D), BF16)
    out_spec = pl.BlockSpec((32, D * D), lambda i: (0, 0))
    part = pl.BlockSpec((4, 128, 256), lambda i: (0, i, 0))
    return pl.pallas_call(
        down_gram_kernel,
        grid=(4,),
        out_shape=(out, out),
        in_specs=[
            pl.BlockSpec(memory_space=pltpu.SMEM),
            part,
            part,
            pl.BlockSpec((4, 256, 512), lambda i: (i, 0, 0)),
        ],
        out_specs=(out_spec, out_spec),
        scratch_shapes=[pltpu.VMEM((256, 512), F32)],
        compiler_params=pltpu.CompilerParams(vmem_limit_bytes=48 << 20),
    )(core, mine, other, down)


def body(tensor, bond_weights, start_blocks):
    row_index = lax.axis_index(ROW)

    def both_cores(shard):
        mine = from_everyone(shard, "z")
        return mine, lax.ppermute(mine, "core", [(0, 1), (1, 0)])

    where = jnp.reshape(lax.axis_index("core"), (1,)).astype(jnp.int32)
    horizontal = bond_weights[0]
    vertical = bond_weights[1]
    horiz_rows = lax.dynamic_slice_in_dim(horizontal, row_index * 8, 8)
    grid = tensor.reshape(4, 8, D, D)
    flat = jnp.transpose(grid, (1, 2, 0, 3)).reshape(512, 256)
    by_cols = lax.all_gather(flat, COL)

    square = vertical * vertical
    rows_square = horiz_rows * horiz_rows
    turned = flat.T.astype(F32)
    up_scale = (rows_square[:, None] * square[None, :]).reshape(1, 512)
    own_up = (turned * up_scale * jnp.tile(vertical, 4)[:, None]).astype(BF16)
    weighted = (turned * jnp.tile(vertical, 8)[None, :]).astype(BF16)
    top_piece = jnp.swapaxes(weighted.reshape(4, 16, 4, 512), 0, 1).reshape(16, 16, 512)
    side_piece = jnp.swapaxes(flat.reshape(8, 16, 4, 256), 0, 1).reshape(16, 32, 256)
    top_piece = top_piece.reshape(16, 16, 2, 256).swapaxes(1, 2).reshape(16, 32, 256)
    pieces = jnp.concatenate([side_piece, top_piece], axis=1)
    pieces = lax.all_to_all(pieces, COL, 0, 0, tiled=True)
    top_got = pieces[:, 32:].reshape(16, 2, 16, 256).swapaxes(1, 2).reshape(16, 16, 512)
    side_own = both_cores(pieces[:, :32])

    def everywhere(y):
        mine = lax.all_to_all(
            jnp.broadcast_to(y, (64, 32, 2 * RANK)), SAME_CORE, 0, 0, tiled=True
        ).reshape(2048, 2 * RANK)
        return mine, lax.ppermute(mine, "core", [(0, 1), (1, 0)])

    own_down = grid.astype(F32) * rows_square[None, :, None, None] * square
    own_down = jnp.transpose(own_down.astype(BF16), (0, 2, 1, 3)).reshape(256, 512)

    by_cols, side_own = lax.optimization_barrier((by_cols, side_own))
    lane_scale = jnp.tile(vertical, 16)[None, :]
    part_up, part_down = partials(where, own_up, own_down, lane_scale, by_cols)
    left_down = lax.psum_scatter(
        part_down.reshape(8, 4, D, 512), ROW, scatter_dimension=0, tiled=True
    )
    received = lax.ppermute(part_up[1], "core", [(0, 1), (1, 0)])
    first_vectors = everywhere(start_blocks.reshape(32, 2 * RANK))

    inner = ((horizontal * horizontal)[:, None] * square[None, :]).reshape(16, 1, 256)
    lanes = jnp.repeat(jnp.transpose(horiz_rows.reshape(2, 4)).reshape(8), D)[None, :]
    side = side_gram(
        where, *side_own, inner, jnp.repeat(horizontal, 4)[:, None], lanes, by_cols
    )

    left_down, first_vectors, side = lax.optimization_barrier((left_down, first_vectors, side))
    down_all = lax.all_gather(left_down.reshape(256, 512), COL)
    pair_up = (part_up[0].astype(F32) + received.astype(F32)).astype(BF16)
    left_up = lax.all_to_all(pair_up.reshape(4, 256, 512), "z", 0, 0, tiled=True)
    side_all = both_cores(side.astype(BF16).reshape(512, 256))
    slab_part = by_cols.reshape(16, 8, D, 256)[:, :, :8]
    slab_part = jnp.transpose(slab_part, (2, 0, 1, 3)).reshape(8, 128, 256)
    slab = lax.all_to_all(slab_part, ROW, split_axis=0, concat_axis=0, tiled=True)
    bottom, top_rows = vmem_call(
        fold_kernel,
        (
            jax.ShapeDtypeStruct((16, D, 256), BF16),
            jax.ShapeDtypeStruct((16, 32, 256), BF16),
        ),
        (slab, top_got),
    )
    down_all, bottom, top_rows, side_all, left_up = lax.optimization_barrier(
        (down_all, bottom, top_rows, side_all, left_up)
    )
    grams = (*left_gram(left_up, down_all), *down_gram(where, *side_all, down_all))
    top_rows, grams = lax.optimization_barrier((top_rows, grams))
    top = lax.all_gather(top_rows, ROW)
    z_outs = (
        jax.ShapeDtypeStruct((8, 16, 2 * RANK), F32),
        jax.ShapeDtypeStruct((32, 2 * RANK), F32),
    )
    inv_out = jax.ShapeDtypeStruct((2 * RANK, 2 * RANK), F32)

    def local_images(z_left, z_down):
        z_left = jnp.sum(lax.all_to_all(z_left, ROW, 0, 0, tiled=True), axis=0)
        z_left = jnp.concatenate([z_left[:, :RANK], z_left[:, RANK:]], axis=0)
        z = jnp.concatenate([z_left, z_down[:, RANK:]], axis=1)
        z = jnp.transpose(z.reshape(2, 2, 2, 4, 2 * RANK), (0, 2, 3, 1, 4))
        return z.reshape(32, 2 * RANK)

    def apply(y, inverse):
        return lax.dot_general(y, inverse, (((1,), (1,)), ((), ())), precision=HIGHEST)

    vectors = first_vectors
    for step in range(3):
        y = local_images(*vmem_call(images_kernel, z_outs, (where, *vectors, *grams), 1))
        if step:
            y = apply(y, vmem_call(factor_kernel, (inv_out,), vectors)[0])
        vectors = everywhere(y)
    basis_out = jax.ShapeDtypeStruct((D * D, RANK), BF16)
    basis, mixed, inverse = vmem_call(
        last_kernel, (basis_out, basis_out, inv_out), (where, *vectors), 1
    )
    projectors = apply(y, inverse).reshape(4, 8, 2 * RANK)
    first = jnp.transpose(mixed.reshape(16, 4, D, RANK), (3, 1, 0, 2)).reshape(RANK, D, D)
    new_tensor = contract(bottom.reshape(1024, 256), first, basis.reshape(D, D, RANK), top)
    return (projectors, new_tensor.reshape(4, 1, RANK * RANK))


def solution(mesh):
    axes = ("z", "core", "col_0", "col_1")
    torus = Mesh(mesh.devices.reshape(mesh.shape["row"] // 2, 2, 4, 4), axes)
    placed = (P(COL, ROW, None), P(), P(COL, ROW, None))
    return jax.shard_map(
        body,
        mesh=torus,
        in_specs=placed,
        out_specs=(P(COL, ROW, None), P(COL, ROW, None)),
        check_vma=False,
    )
```

```python
import jax
import jax.numpy as jnp
from jax import lax
from jax.experimental import pallas as pl
from jax.experimental.pallas import tpu as pltpu
from jax.sharding import Mesh
from jax.sharding import PartitionSpec as P

D = 64
RANK = 64
COL = ("col_0", "col_1")
ROW = ("z", "core")
SAME_CORE = ("z", "col_0", "col_1")
HIGHEST = lax.Precision.HIGHEST
F32 = jnp.float32
BF16 = jnp.bfloat16
A_BLOCK = 16
UNROLL = 8


def from_everyone(shard, axis):
    copies = jnp.broadcast_to(shard, (lax.axis_size(axis), *shard.shape))
    return lax.all_to_all(copies, axis, split_axis=0, concat_axis=0, tiled=True)


def two_parts(x):
    high = x.astype(BF16)
    return high, (x - high.astype(F32)).astype(BF16)


def by_core(core_ref, mine, other):
    first = core_ref[0] == 0
    return jnp.where(first, mine, other), jnp.where(first, other, mine)


def in_index_order(core_ref, mine_ref, other_ref):
    halves = by_core(core_ref, mine_ref[...], other_ref[...])
    y = jnp.stack([h.reshape(4, D, 8, 2 * RANK) for h in halves], axis=1)
    y = jnp.transpose(y.reshape(8, D, 8, 2 * RANK), (1, 0, 2, 3))
    return y.reshape(D * D, 2 * RANK)


def inverse_factors(mats):
    n = RANK
    count = n // 8
    rows_at = lax.broadcasted_iota(jnp.int32, (8, 2 * n), 0)
    lanes_at = lax.broadcasted_iota(jnp.int32, (8, 2 * n), 1)
    sets = []
    for c in mats:
        blocks = []
        for i in range(count):
            unit = (lanes_at == rows_at + (n + 8 * i)).astype(F32)
            part = jnp.concatenate([c[8 * i : 8 * i + 8], jnp.zeros((8, n), F32)], axis=1)
            blocks.append(part + unit)
        sets.append((blocks, []))
    for b in range(count):
        panels = []
        for blocks, _ in sets:
            columns = [
                {
                    i: jnp.broadcast_to(blocks[i][:, 8 * b + j : 8 * b + j + 1], (8, 2 * n))
                    for i in range(b, count)
                }
                for j in range(8)
            ]
            rows = [jnp.broadcast_to(blocks[b][j : j + 1], (8, 2 * n)) for j in range(8)]
            panels.append((columns, rows, []))
        for j in range(8):
            for (blocks, pivots), (columns, rows, scaled) in zip(sets, panels):
                own = columns[j][b]
                inverse = 1.0 / own[j : j + 1]
                pivots.append(own[j : j + 1])
                scaled.append(rows[j] * inverse)
                for k in range(j + 1, 8):
                    factor = columns[k][b][j : j + 1] * inverse
                    rows[k] = rows[k] - own[k : k + 1] * scaled[j]
                    for i in range(b, count):
                        columns[k][i] = columns[k][i] - columns[j][i] * factor
        for (blocks, _), (columns, rows, scaled) in zip(sets, panels):
            whole = rows[0]
            for j in range(1, 8):
                whole = jnp.where(rows_at == j, rows[j], whole)
            blocks[b] = whole
            for i in range(b + 1, count):
                for j in range(8):
                    blocks[i] = blocks[i] - columns[j][i] * scaled[j]
    out = []
    for blocks, pivots in sets:
        done = []
        for i in range(count):
            pivot = jnp.broadcast_to(pivots[8 * i], (8, 2 * n))
            for j in range(1, 8):
                pivot = jnp.where(rows_at == j, pivots[8 * i + j], pivot)
            done.append((blocks[i] / jnp.sqrt(pivot))[:, n:])
        out.append(jnp.concatenate(done, axis=0))
    return out


def correlation(y):
    return lax.dot_general(
        y, y, (((0,), (0,)), ((), ())), precision=HIGHEST, preferred_element_type=F32
    )


def factors_of(c):
    return inverse_factors([c[:RANK, :RANK], c[RANK:, RANK:]])


def store_inverse(inv_ref, left, down):
    zero = jnp.zeros((RANK, RANK), F32)
    inv_ref[:RANK, :] = jnp.concatenate([left, zero], axis=1)
    inv_ref[RANK:, :] = jnp.concatenate([zero, down], axis=1)


def images_of(y, gl_high, gl_low, gd_high, gd_low, zl_ref, zd_ref):
    y_high, y_low = two_parts(y)
    both = jnp.concatenate([y_high, y_low], axis=1)

    def product(high, low):
        main = jnp.dot(high[...], both, preferred_element_type=F32)
        rest = jnp.dot(low[...], y_high, preferred_element_type=F32)
        return main[:, : 2 * RANK] + main[:, 2 * RANK :] + rest

    z = product(gl_high, gl_low)[:, :RANK].reshape(8, 32, RANK)
    zl_ref[...] = jnp.concatenate([z[:, :16], z[:, 16:]], axis=2)
    zd_ref[...] = product(gd_high, gd_low)


def images_kernel(core_ref, mine_ref, other_ref, glh, gll, gdh, gdl, zl_ref, zd_ref):
    y = in_index_order(core_ref, mine_ref, other_ref)
    images_of(y, glh, gll, gdh, gdl, zl_ref, zd_ref)


def factor_kernel(mine_ref, other_ref, inv_ref):
    c = correlation(mine_ref[...]) + correlation(other_ref[...])
    store_inverse(inv_ref, *factors_of(c))


def last_kernel(core_ref, mine_ref, other_ref, basis_ref, mixed_ref, inv_ref):
    c = correlation(mine_ref[...]) + correlation(other_ref[...])
    left, down = factors_of(c)
    store_inverse(inv_ref, left, down)
    y = in_index_order(core_ref, mine_ref, other_ref)[:, :RANK]
    y_high, y_low = two_parts(y)
    l_high, l_low = two_parts(left.T)
    basis = jnp.dot(
        jnp.concatenate([y_high, y_low, y_high], axis=1),
        jnp.concatenate([l_high, l_high, l_low], axis=0),
        preferred_element_type=F32,
    )
    basis = basis.astype(BF16)
    basis_ref[...] = basis
    to = lax.broadcasted_iota(jnp.int32, (256, 256), 0)
    at = lax.broadcasted_iota(jnp.int32, (256, 256), 1)
    source = (to // 64) * 64 + (to % 16) * 4 + (to % 64) // 16
    picks = (at == source).astype(F32).astype(BF16)
    for q in range(16):
        rows = slice(256 * q, 256 * q + 256)
        mixed_ref[rows, :] = jnp.dot(
            picks, basis[rows], preferred_element_type=F32
        ).astype(BF16)


def folded(columns):
    rows = []
    for x in range(0, 8, 2):
        turned = jnp.concatenate(columns[x : x + 2], axis=1).T
        for h in range(2):
            parts = [turned[64 * h + 16 * q : 64 * h + 16 * q + 16] for q in range(4)]
            rows.append(jnp.concatenate(parts, axis=1))
    return jnp.swapaxes(jnp.stack(rows, axis=0), 0, 1)


def fold_kernel(slab_ref, top_ref, bottom_out, top_out):
    for g in range(4):
        both = []
        for h in range(2):
            block = slab_ref[2 * g + h].astype(F32).reshape(16, 8, 256)
            by_r = jnp.swapaxes(block, 0, 1)
            both.append(
                folded(
                    [
                        jnp.concatenate(
                            [by_r[r][:, 64 * l : 64 * l + 64] for l in range(4)], axis=0
                        )
                        for r in range(8)
                    ]
                )
            )
        bottom_out[:, 16 * g : 16 * g + 16, :] = jnp.concatenate(both, axis=1).astype(BF16)
    block = top_ref[...].astype(F32)
    halves = [jnp.swapaxes(block[:, 8 * h : 8 * h + 8], 0, 1) for h in range(2)]
    for g in range(2):
        both = []
        for u in range(2 * g, 2 * g + 2):
            rows = jnp.concatenate([halves[l // 2][4 * (l % 2) + u] for l in range(4)], axis=0)
            both.append(folded([rows[:, 64 * r : 64 * r + 64] for r in range(8)]))
        top_out[:, 16 * g : 16 * g + 16, :] = jnp.concatenate(both, axis=1).astype(BF16)


def vmem_call(kernel, outs, args, scalars=0, limit=48):
    spec = pl.BlockSpec(memory_space=pltpu.VMEM)
    scalar = pl.BlockSpec(memory_space=pltpu.SMEM)
    return pl.pallas_call(
        kernel,
        out_shape=tuple(outs),
        in_specs=[scalar] * scalars + [spec] * (len(args) - scalars),
        out_specs=tuple([spec] * len(outs)),
        compiler_params=pltpu.CompilerParams(vmem_limit_bytes=limit << 20),
    )(*args)


def fill_diagonal(diag_ref, slot, block):
    for i in range(4):
        diag_ref[slot, 64 * i : 64 * i + 64, 64 * i : 64 * i + 64] = block


def contract_kernel(
    bottom_ref, first_ref, basis_ref, tops_ref, out_ref, top_ref, wide_ref, diag_ref, even_ref, odd_ref, sum_ref
):
    step_id = pl.program_id(0)
    rows_here = A_BLOCK * D

    @pl.when(step_id == 0)
    def _():
        diag_ref[...] = jnp.zeros_like(diag_ref)
        for q in range(16):
            part = tops_ref[:, q].astype(F32).reshape(8, 4, 8, 256)
            part = jnp.transpose(part, (1, 0, 2, 3)).reshape(256, 256)
            top_ref[256 * q : 256 * q + 256, :] = part.T.astype(BF16)

    bottom = bottom_ref[...]

    def sections(group, carry):
        for j in range(UNROLL):
            fill_diagonal(diag_ref, j, first_ref[group * UNROLL + j])
        for j in range(UNROLL):
            section = jnp.dot(bottom, diag_ref[j], preferred_element_type=F32).astype(BF16)
            start = pl.multiple_of((group * UNROLL + j) * D, D)
            for q in range(16):
                wide_ref[pl.ds(start, D), 256 * q : 256 * q + 256] = section[64 * q : 64 * q + 64]
        return carry

    lax.fori_loop(0, A_BLOCK // UNROLL, sections, 0)
    second = jnp.dot(wide_ref[...], top_ref[...], preferred_element_type=F32)
    base = pl.multiple_of(step_id * rows_here, rows_here)
    even_ref[pl.ds(base, rows_here), :] = second[:, :128]
    odd_ref[pl.ds(base, rows_here), :] = second[:, 128:]

    @pl.when(step_id == RANK // A_BLOCK - 1)
    def _():
        sum_ref[...] = jnp.zeros_like(sum_ref)

        def products(group, carry):
            total = jnp.zeros((4 * RANK, RANK), F32)
            for j in range(4):
                at = 16 * group + 4 * j
                parts = []
                for ref in (even_ref, odd_ref):
                    rows = [ref[pl.ds(at + r, RANK, stride=D), :] for r in range(4)]
                    for h in range(2):
                        parts.append(
                            jnp.concatenate([r[:, 64 * h : 64 * h + 64] for r in rows], axis=1)
                        )
                total = total + jnp.dot(
                    jnp.concatenate(parts, axis=0).astype(BF16),
                    basis_ref[pl.ds(at, 4)].reshape(4 * D, RANK),
                    preferred_element_type=F32,
                )
            sum_ref[:, :RANK] += total
            return carry

        lax.fori_loop(0, 4, products, 0)
        for u in range(4):
            pair = [
                sum_ref[pl.ds(RANK * u + odd, RANK // 2, stride=2), :][:, :RANK] for odd in range(2)
            ]
            out_ref[u] = jnp.concatenate(pair, axis=1)


def contract(bottom, first, basis, top):
    whole = lambda *dims: pl.BlockSpec(dims, lambda i: (0,) * len(dims))
    return pl.pallas_call(
        contract_kernel,
        grid=(RANK // A_BLOCK,),
        out_shape=jax.ShapeDtypeStruct((4, RANK // 2, 2 * RANK), F32),
        in_specs=[
            whole(1024, 256),
            pl.BlockSpec((A_BLOCK, D, D), lambda i: (i, 0, 0)),
            whole(D, D, RANK),
            whole(8, 16, 32, 256),
        ],
        out_specs=whole(4, RANK // 2, 2 * RANK),
        scratch_shapes=[
            pltpu.VMEM((D * D, 256), BF16),
            pltpu.VMEM((A_BLOCK * D, D * D), BF16),
            pltpu.VMEM((UNROLL, 256, 256), BF16),
            pltpu.VMEM((RANK * D, 128), F32),
            pltpu.VMEM((RANK * D, 128), F32),
            pltpu.VMEM((4 * RANK, 2 * RANK), F32),
        ],
        compiler_params=pltpu.CompilerParams(vmem_limit_bytes=56 << 20),
    )(bottom, first, basis, top)


def swapped_pairs(tiles):
    lane = lax.broadcasted_iota(jnp.int32, (8, 128), 1)
    stack = jnp.swapaxes(jnp.stack(tiles, axis=0), 0, 1)
    out = []
    for j in range(4):
        a, b = stack[2 * j], stack[2 * j + 1]
        low = jnp.where(lane < 64, a, pltpu.roll(b, 64, 1))
        high = jnp.where(lane < 64, pltpu.roll(a, 64, 1), b)
        out.append((low, high))
    return out


def partial_kernel(
    core_ref, up_ref, down_ref, scale_ref, all_ref, up_out, down_out, up_acc, down_acc
):
    blocks = [all_ref[c] for c in range(4)]
    order = [(t // 4 + 2 * y, t % 4) for t in range(8) for y in range(2)]
    right = jnp.concatenate([blocks[c][:, 64 * m : 64 * m + 64] for c, m in order], axis=1)
    up_acc[...] = jnp.dot(up_ref[...], right, preferred_element_type=F32) * scale_ref[...]
    rows = []
    for c, m in order:
        part = blocks[c][:, 64 * m : 64 * m + 64]
        rows.append(jnp.concatenate([part[64 * r : 64 * r + 64] for r in range(8)], axis=1))
    down_acc[...] = lax.dot_general(
        down_ref[...],
        jnp.concatenate(rows, axis=0),
        (((1,), (1,)), ((), ())),
        preferred_element_type=F32,
    )
    core = core_ref[0]
    for left in range(4):
        for high in range(8):
            at = 64 * left + 8 * high
            slot = 1 - core if high % 2 else core
            for which, acc in enumerate((down_acc, up_acc)):
                pieces = swapped_pairs(
                    [acc[at : at + 8, 128 * t : 128 * t + 128] for t in range(8)]
                )
                for j, piece in enumerate(pieces):
                    value = jnp.concatenate(piece, axis=0).astype(BF16)
                    lanes = slice(128 * j, 128 * j + 128)
                    if which == 0:
                        down_out[slot, high // 2, left, 0, :, lanes] = value
                    else:
                        up_out[high, left, 0, :, lanes] = value


def partials(core, up, down, scale, by_cols):
    whole = lambda *dims: pl.BlockSpec(dims, lambda i: (0,) * len(dims))
    return pl.pallas_call(
        partial_kernel,
        grid=(4,),
        out_shape=(
            jax.ShapeDtypeStruct((8, 4, 4, 16, 512), BF16),
            jax.ShapeDtypeStruct((2, 4, 4, 4, 16, 512), BF16),
        ),
        in_specs=[
            pl.BlockSpec(memory_space=pltpu.SMEM),
            whole(256, 512),
            whole(256, 512),
            whole(1, 1024),
            pl.BlockSpec((4, 512, 256), lambda i: (i, 0, 0)),
        ],
        out_specs=(
            pl.BlockSpec((8, 4, 1, 16, 512), lambda i: (0, 0, i, 0, 0)),
            pl.BlockSpec((2, 4, 4, 1, 16, 512), lambda i: (0, 0, 0, i, 0, 0)),
        ),
        scratch_shapes=[pltpu.VMEM((256, 1024), F32), pltpu.VMEM((256, 1024), F32)],
        compiler_params=pltpu.CompilerParams(vmem_limit_bytes=48 << 20),
    )(core, up, down, scale, by_cols)


def side_kernel(
    core_ref, mine_ref, other_ref, inner_ref, rows_ref, lanes_ref, all_ref, out_ref, acc_ref
):
    step = pl.program_id(0)

    @pl.when(step == 0)
    def _():
        acc_ref[...] = jnp.zeros_like(acc_ref)

    order = [s + 4 * y for s in range(4) for y in range(2)]
    left, right = [], []
    for c in range(4):
        own = jnp.concatenate(
            [mine_ref[:, c].reshape(128, 256), other_ref[:, c].reshape(128, 256)], axis=0
        )
        left.append((own.astype(F32) * inner_ref[c]).astype(BF16))
        block = all_ref[c]
        right.append(jnp.concatenate([block[64 * s : 64 * s + 64] for s in order], axis=0))
    acc_ref[...] += lax.dot_general(
        jnp.concatenate(left, axis=1),
        jnp.concatenate(right, axis=1),
        (((1,), (1,)), ((), ())),
        preferred_element_type=F32,
    )

    @pl.when(step == 3)
    def _():
        core = core_ref[0]
        for s in range(16):
            row = 2 * ((s % 8) // 2) + (core if s < 8 else 1 - core)
            first = pl.multiple_of(32 * row + 16 * (s % 2), 16)
            scaled = (
                acc_ref[16 * s : 16 * s + 16, :] * rows_ref[pl.ds(first, 16), :] * lanes_ref[...]
            )
            tiles = [
                scaled[8 * t : 8 * t + 8, 128 * q : 128 * q + 128]
                for t in range(2)
                for q in range(4)
            ]
            pieces = swapped_pairs(tiles)
            for odd in range(2):
                low = jnp.concatenate([pieces[2 * odd][0], pieces[2 * odd + 1][0]], axis=1)
                high = jnp.concatenate([pieces[2 * odd][1], pieces[2 * odd + 1][1]], axis=1)
                for t in range(2):
                    out_ref[8 * row + 4 * (s % 2) + 2 * t + odd] = jnp.concatenate(
                        [low[4 * t : 4 * t + 4], high[4 * t : 4 * t + 4]], axis=0
                    )


def side_gram(core, mine, other, inner, rows, lanes, by_cols):
    whole = lambda *dims: pl.BlockSpec(dims, lambda i: (0,) * len(dims))
    part = pl.BlockSpec((4, 4, 32, 256), lambda i: (0, i, 0, 0))
    return pl.pallas_call(
        side_kernel,
        grid=(4,),
        out_shape=jax.ShapeDtypeStruct((D, 8, 256), F32),
        in_specs=[
            pl.BlockSpec(memory_space=pltpu.SMEM),
            part,
            part,
            pl.BlockSpec((4, 1, 256), lambda i: (i, 0, 0)),
            whole(256, 1),
            whole(1, 512),
            pl.BlockSpec((4, 512, 256), lambda i: (i, 0, 0)),
        ],
        out_specs=whole(D, 8, 256),
        scratch_shapes=[pltpu.VMEM((256, 512), F32)],
        compiler_params=pltpu.CompilerParams(vmem_limit_bytes=48 << 20),
    )(core, mine, other, inner, rows, lanes, by_cols)


def store_gram(acc_ref, high_ref, low_ref):
    for a_high in range(2):
        for x_high in range(8):
            tiles = []
            for a_low in range(2):
                at = 64 * (2 * a_high + a_low) + 8 * x_high
                for q in range(4):
                    tiles.append(acc_ref[at : at + 8, 128 * q : 128 * q + 128])
            for j, piece in enumerate(swapped_pairs(tiles)):
                high, low = two_parts(jnp.concatenate(piece, axis=0))
                lanes = slice(512 * x_high + 128 * j, 512 * x_high + 128 * j + 128)
                high_ref[16 * a_high : 16 * a_high + 16, lanes] = high
                low_ref[16 * a_high : 16 * a_high + 16, lanes] = low


def left_gram_kernel(up_ref, down_ref, high_ref, low_ref, acc_ref):
    acc_ref[...] = lax.dot_general(
        up_ref[...],
        down_ref[...].reshape(512, 512),
        (((1,), (1,)), ((), ())),
        preferred_element_type=F32,
    )
    store_gram(acc_ref, high_ref, low_ref)


def left_gram(up, down):
    out = jax.ShapeDtypeStruct((256, D * D), BF16)
    out_spec = pl.BlockSpec((32, D * D), lambda i: (i, 0))
    return pl.pallas_call(
        left_gram_kernel,
        grid=(8,),
        out_shape=(out, out),
        in_specs=[
            pl.BlockSpec((256, 512), lambda i: (0, 0)),
            pl.BlockSpec((2, 256, 512), lambda i: (i, 0, 0)),
        ],
        out_specs=(out_spec, out_spec),
        scratch_shapes=[pltpu.VMEM((256, 512), F32)],
        compiler_params=pltpu.CompilerParams(vmem_limit_bytes=48 << 20),
    )(up, down)


def down_gram_kernel(core_ref, mine_ref, other_ref, down_ref, high_ref, low_ref, acc_ref):
    step = pl.program_id(0)

    @pl.when(step == 0)
    def _():
        acc_ref[...] = jnp.zeros_like(acc_ref)

    halves = by_core(core_ref, mine_ref[...].astype(F32), other_ref[...].astype(F32))
    side = jnp.stack([h.reshape(4, 16, 8, 256) for h in halves], axis=1)
    side = jnp.transpose(side.reshape(8, 16, 8, 256), (1, 0, 2, 3)).reshape(1024, 256)
    acc_ref[...] += lax.dot_general(
        side.astype(BF16),
        down_ref[...].reshape(1024, 512),
        (((0,), (0,)), ((), ())),
        preferred_element_type=F32,
    )

    @pl.when(step == 3)
    def _():
        store_gram(acc_ref, high_ref, low_ref)


def down_gram(core, mine, other, down):
    out = jax.ShapeDtypeStruct((32, D * D), BF16)
    out_spec = pl.BlockSpec((32, D * D), lambda i: (0, 0))
    part = pl.BlockSpec((4, 128, 256), lambda i: (0, i, 0))
    return pl.pallas_call(
        down_gram_kernel,
        grid=(4,),
        out_shape=(out, out),
        in_specs=[
            pl.BlockSpec(memory_space=pltpu.SMEM),
            part,
            part,
            pl.BlockSpec((4, 256, 512), lambda i: (i, 0, 0)),
        ],
        out_specs=(out_spec, out_spec),
        scratch_shapes=[pltpu.VMEM((256, 512), F32)],
        compiler_params=pltpu.CompilerParams(vmem_limit_bytes=48 << 20),
    )(core, mine, other, down)


def body(tensor, bond_weights, start_blocks):
    row_index = lax.axis_index(ROW)

    def both_cores(shard):
        mine = from_everyone(shard, "z")
        return mine, lax.ppermute(mine, "core", [(0, 1), (1, 0)])

    where = jnp.reshape(lax.axis_index("core"), (1,)).astype(jnp.int32)
    horizontal = bond_weights[0]
    vertical = bond_weights[1]
    horiz_rows = lax.dynamic_slice_in_dim(horizontal, row_index * 8, 8)
    grid = tensor.reshape(4, 8, D, D)
    flat = jnp.transpose(grid, (1, 2, 0, 3)).reshape(512, 256)
    by_cols = lax.all_gather(flat, COL)

    square = vertical * vertical
    rows_square = horiz_rows * horiz_rows
    turned = flat.T.astype(F32)
    up_scale = (rows_square[:, None] * square[None, :]).reshape(1, 512)
    own_up = (turned * up_scale * jnp.tile(vertical, 4)[:, None]).astype(BF16)
    weighted = (turned * jnp.tile(vertical, 8)[None, :]).astype(BF16)
    top_piece = jnp.swapaxes(weighted.reshape(4, 16, 4, 512), 0, 1).reshape(16, 16, 512)
    side_piece = jnp.swapaxes(flat.reshape(8, 16, 4, 256), 0, 1).reshape(16, 32, 256)
    top_piece = top_piece.reshape(16, 16, 2, 256).swapaxes(1, 2).reshape(16, 32, 256)
    pieces = jnp.concatenate([side_piece, top_piece], axis=1)
    pieces = lax.all_to_all(pieces, COL, 0, 0, tiled=True)
    top_got = pieces[:, 32:].reshape(16, 2, 16, 256).swapaxes(1, 2).reshape(16, 16, 512)
    side_own = both_cores(pieces[:, :32])
    own_down = grid.astype(F32) * rows_square[None, :, None, None] * square
    own_down = jnp.transpose(own_down.astype(BF16), (0, 2, 1, 3)).reshape(256, 512)

    by_cols, side_own = lax.optimization_barrier((by_cols, side_own))
    lane_scale = jnp.tile(vertical, 16)[None, :]
    part_up, part_down = partials(where, own_up, own_down, lane_scale, by_cols)
    left_up = lax.psum_scatter(
        part_up.reshape(8, 4, D, 512), ROW, scatter_dimension=0, tiled=True
    )
    received = lax.ppermute(part_down[1], "core", [(0, 1), (1, 0)])
    pair_down = (part_down[0].astype(F32) + received.astype(F32)).astype(BF16)
    left_down = lax.all_to_all(pair_down.reshape(4, 256, 512), "z", 0, 0, tiled=True)
    left_down = jnp.sum(left_down.astype(F32), axis=0).astype(BF16)
    start_blocks, left_down = lax.optimization_barrier((start_blocks, left_down))

    inner = ((horizontal * horizontal)[:, None] * square[None, :]).reshape(16, 1, 256)
    lanes = jnp.repeat(jnp.transpose(horiz_rows.reshape(2, 4)).reshape(8), D)[None, :]
    side = side_gram(
        where, *side_own, inner, jnp.repeat(horizontal, 4)[:, None], lanes, by_cols
    )

    def everywhere(y):
        mine = lax.all_to_all(
            jnp.broadcast_to(y, (64, 32, 2 * RANK)), SAME_CORE, 0, 0, tiled=True
        ).reshape(2048, 2 * RANK)
        return mine, lax.ppermute(mine, "core", [(0, 1), (1, 0)])

    first_vectors = everywhere(start_blocks.reshape(32, 2 * RANK))
    left_up, left_down, first_vectors = lax.optimization_barrier(
        (left_up, left_down, first_vectors)
    )
    down_all = lax.all_gather(left_down, COL)
    side_all = both_cores(side.astype(BF16).reshape(512, 256))

    slab_part = by_cols.reshape(16, 8, D, 256)[:, :, :8]
    slab_part = jnp.transpose(slab_part, (2, 0, 1, 3)).reshape(8, 128, 256)
    slab = lax.all_to_all(slab_part, ROW, split_axis=0, concat_axis=0, tiled=True)
    bottom, top_rows = vmem_call(
        fold_kernel,
        (
            jax.ShapeDtypeStruct((16, D, 256), BF16),
            jax.ShapeDtypeStruct((16, 32, 256), BF16),
        ),
        (slab, top_got),
    )
    down_all, bottom, top_rows, side_all = lax.optimization_barrier(
        (down_all, bottom, top_rows, side_all)
    )
    grams = (*left_gram(left_up.reshape(256, 512), down_all), *down_gram(where, *side_all, down_all))
    top_rows, grams = lax.optimization_barrier((top_rows, grams))
    top = lax.all_gather(top_rows, ROW)
    z_outs = (
        jax.ShapeDtypeStruct((8, 16, 2 * RANK), F32),
        jax.ShapeDtypeStruct((32, 2 * RANK), F32),
    )
    inv_out = jax.ShapeDtypeStruct((2 * RANK, 2 * RANK), F32)

    def local_images(z_left, z_down):
        z_left = jnp.sum(lax.all_to_all(z_left, ROW, 0, 0, tiled=True), axis=0)
        z_left = jnp.concatenate([z_left[:, :RANK], z_left[:, RANK:]], axis=0)
        z = jnp.concatenate([z_left, z_down[:, RANK:]], axis=1)
        z = jnp.transpose(z.reshape(2, 2, 2, 4, 2 * RANK), (0, 2, 3, 1, 4))
        return z.reshape(32, 2 * RANK)

    def apply(y, inverse):
        return lax.dot_general(y, inverse, (((1,), (1,)), ((), ())), precision=HIGHEST)

    vectors = first_vectors
    for step in range(3):
        y = local_images(*vmem_call(images_kernel, z_outs, (where, *vectors, *grams), 1))
        if step:
            y = apply(y, vmem_call(factor_kernel, (inv_out,), vectors)[0])
        vectors = everywhere(y)
    basis_out = jax.ShapeDtypeStruct((D * D, RANK), BF16)
    basis, mixed, inverse = vmem_call(
        last_kernel, (basis_out, basis_out, inv_out), (where, *vectors), 1
    )
    projectors = apply(y, inverse).reshape(4, 8, 2 * RANK)
    first = jnp.transpose(mixed.reshape(16, 4, D, RANK), (3, 1, 0, 2)).reshape(RANK, D, D)
    new_tensor = contract(bottom.reshape(1024, 256), first, basis.reshape(D, D, RANK), top)
    return (projectors, new_tensor.reshape(4, 1, RANK * RANK))


def solution(mesh):
    axes = ("z", "core", "col_0", "col_1")
    torus = Mesh(mesh.devices.reshape(mesh.shape["row"] // 2, 2, 4, 4), axes)
    placed = (P(COL, ROW, None), P(), P(COL, ROW, None))
    return jax.shard_map(
        body,
        mesh=torus,
        in_specs=placed,
        out_specs=(P(COL, ROW, None), P(COL, ROW, None)),
        check_vma=False,
    )
```

```python
import jax
import jax.numpy as jnp
from jax import lax
from jax.experimental import pallas as pl
from jax.experimental.pallas import tpu as pltpu
from jax.sharding import Mesh
from jax.sharding import PartitionSpec as P

D = 64
RANK = 64
COL = ("col_0", "col_1")
ROW = ("z", "core")
SAME_CORE = ("z", "col_0", "col_1")
HIGHEST = lax.Precision.HIGHEST
F32 = jnp.float32
BF16 = jnp.bfloat16
A_BLOCK = 16
UNROLL = 8


def from_everyone(shard, axis):
    copies = jnp.broadcast_to(shard, (lax.axis_size(axis), *shard.shape))
    return lax.all_to_all(copies, axis, split_axis=0, concat_axis=0, tiled=True)


def two_parts(x):
    high = x.astype(BF16)
    return high, (x - high.astype(F32)).astype(BF16)


def by_core(core_ref, mine, other):
    first = core_ref[0] == 0
    return jnp.where(first, mine, other), jnp.where(first, other, mine)


def in_index_order(core_ref, mine_ref, other_ref):
    halves = by_core(core_ref, mine_ref[...], other_ref[...])
    y = jnp.stack([h.reshape(4, D, 8, 2 * RANK) for h in halves], axis=1)
    y = jnp.transpose(y.reshape(8, D, 8, 2 * RANK), (1, 0, 2, 3))
    return y.reshape(D * D, 2 * RANK)


def inverse_factors(mats):
    n = RANK
    count = n // 8
    rows_at = lax.broadcasted_iota(jnp.int32, (8, 2 * n), 0)
    lanes_at = lax.broadcasted_iota(jnp.int32, (8, 2 * n), 1)
    sets = []
    for c in mats:
        blocks = []
        for i in range(count):
            unit = (lanes_at == rows_at + (n + 8 * i)).astype(F32)
            part = jnp.concatenate([c[8 * i : 8 * i + 8], jnp.zeros((8, n), F32)], axis=1)
            blocks.append(part + unit)
        sets.append((blocks, []))
    for b in range(count):
        panels = []
        for blocks, _ in sets:
            columns = [
                {
                    i: jnp.broadcast_to(blocks[i][:, 8 * b + j : 8 * b + j + 1], (8, 2 * n))
                    for i in range(b, count)
                }
                for j in range(8)
            ]
            rows = [jnp.broadcast_to(blocks[b][j : j + 1], (8, 2 * n)) for j in range(8)]
            panels.append((columns, rows, []))
        for j in range(8):
            for (blocks, pivots), (columns, rows, scaled) in zip(sets, panels):
                own = columns[j][b]
                inverse = 1.0 / own[j : j + 1]
                pivots.append(own[j : j + 1])
                scaled.append(rows[j] * inverse)
                for k in range(j + 1, 8):
                    factor = columns[k][b][j : j + 1] * inverse
                    rows[k] = rows[k] - own[k : k + 1] * scaled[j]
                    for i in range(b, count):
                        columns[k][i] = columns[k][i] - columns[j][i] * factor
        for (blocks, _), (columns, rows, scaled) in zip(sets, panels):
            whole = rows[0]
            for j in range(1, 8):
                whole = jnp.where(rows_at == j, rows[j], whole)
            blocks[b] = whole
            for i in range(b + 1, count):
                for j in range(8):
                    blocks[i] = blocks[i] - columns[j][i] * scaled[j]
    out = []
    for blocks, pivots in sets:
        done = []
        for i in range(count):
            pivot = jnp.broadcast_to(pivots[8 * i], (8, 2 * n))
            for j in range(1, 8):
                pivot = jnp.where(rows_at == j, pivots[8 * i + j], pivot)
            done.append((blocks[i] / jnp.sqrt(pivot))[:, n:])
        out.append(jnp.concatenate(done, axis=0))
    return out


def correlation(y):
    return lax.dot_general(
        y, y, (((0,), (0,)), ((), ())), precision=HIGHEST, preferred_element_type=F32
    )


def factors_of(c):
    return inverse_factors([c[:RANK, :RANK], c[RANK:, RANK:]])


def store_inverse(inv_ref, left, down):
    zero = jnp.zeros((RANK, RANK), F32)
    inv_ref[:RANK, :] = jnp.concatenate([left, zero], axis=1)
    inv_ref[RANK:, :] = jnp.concatenate([zero, down], axis=1)


def images_of(y, gl_high, gl_low, gd_high, gd_low, zl_ref, zd_ref):
    y_high, y_low = two_parts(y)
    both = jnp.concatenate([y_high, y_low], axis=1)

    def product(high, low):
        main = jnp.dot(high[...], both, preferred_element_type=F32)
        rest = jnp.dot(low[...], y_high, preferred_element_type=F32)
        return main[:, : 2 * RANK] + main[:, 2 * RANK :] + rest

    z = product(gl_high, gl_low)[:, :RANK].reshape(8, 32, RANK)
    zl_ref[...] = jnp.concatenate([z[:, :16], z[:, 16:]], axis=2)
    zd_ref[...] = product(gd_high, gd_low)


def images_kernel(core_ref, mine_ref, other_ref, glh, gll, gdh, gdl, zl_ref, zd_ref):
    y = in_index_order(core_ref, mine_ref, other_ref)
    images_of(y, glh, gll, gdh, gdl, zl_ref, zd_ref)


def factor_kernel(mine_ref, other_ref, inv_ref):
    c = correlation(mine_ref[...]) + correlation(other_ref[...])
    store_inverse(inv_ref, *factors_of(c))


def last_kernel(core_ref, mine_ref, other_ref, basis_ref, mixed_ref, inv_ref):
    c = correlation(mine_ref[...]) + correlation(other_ref[...])
    left, down = factors_of(c)
    store_inverse(inv_ref, left, down)
    y = in_index_order(core_ref, mine_ref, other_ref)[:, :RANK]
    y_high, y_low = two_parts(y)
    l_high, l_low = two_parts(left.T)
    basis = jnp.dot(
        jnp.concatenate([y_high, y_low, y_high], axis=1),
        jnp.concatenate([l_high, l_high, l_low], axis=0),
        preferred_element_type=F32,
    )
    basis = basis.astype(BF16)
    basis_ref[...] = basis
    to = lax.broadcasted_iota(jnp.int32, (256, 256), 0)
    at = lax.broadcasted_iota(jnp.int32, (256, 256), 1)
    source = (to // 64) * 64 + (to % 16) * 4 + (to % 64) // 16
    picks = (at == source).astype(F32).astype(BF16)
    for q in range(16):
        rows = slice(256 * q, 256 * q + 256)
        mixed_ref[rows, :] = jnp.dot(
            picks, basis[rows], preferred_element_type=F32
        ).astype(BF16)


def folded(columns):
    rows = []
    for x in range(0, 8, 2):
        turned = jnp.concatenate(columns[x : x + 2], axis=1).T
        for h in range(2):
            parts = [turned[64 * h + 16 * q : 64 * h + 16 * q + 16] for q in range(4)]
            rows.append(jnp.concatenate(parts, axis=1))
    return jnp.swapaxes(jnp.stack(rows, axis=0), 0, 1)


def fold_kernel(slab_ref, top_ref, bottom_out, top_out):
    for g in range(4):
        both = []
        for h in range(2):
            block = slab_ref[2 * g + h].astype(F32).reshape(16, 8, 256)
            by_r = jnp.swapaxes(block, 0, 1)
            both.append(
                folded(
                    [
                        jnp.concatenate(
                            [by_r[r][:, 64 * l : 64 * l + 64] for l in range(4)], axis=0
                        )
                        for r in range(8)
                    ]
                )
            )
        bottom_out[:, 16 * g : 16 * g + 16, :] = jnp.concatenate(both, axis=1).astype(BF16)
    block = top_ref[...].astype(F32)
    halves = [jnp.swapaxes(block[:, 8 * h : 8 * h + 8], 0, 1) for h in range(2)]
    for g in range(2):
        both = []
        for u in range(2 * g, 2 * g + 2):
            rows = jnp.concatenate([halves[l // 2][4 * (l % 2) + u] for l in range(4)], axis=0)
            both.append(folded([rows[:, 64 * r : 64 * r + 64] for r in range(8)]))
        top_out[:, 16 * g : 16 * g + 16, :] = jnp.concatenate(both, axis=1).astype(BF16)


def vmem_call(kernel, outs, args, scalars=0, limit=48):
    spec = pl.BlockSpec(memory_space=pltpu.VMEM)
    scalar = pl.BlockSpec(memory_space=pltpu.SMEM)
    return pl.pallas_call(
        kernel,
        out_shape=tuple(outs),
        in_specs=[scalar] * scalars + [spec] * (len(args) - scalars),
        out_specs=tuple([spec] * len(outs)),
        compiler_params=pltpu.CompilerParams(vmem_limit_bytes=limit << 20),
    )(*args)


def fill_diagonal(diag_ref, slot, block):
    for i in range(4):
        diag_ref[slot, 64 * i : 64 * i + 64, 64 * i : 64 * i + 64] = block


def contract_kernel(
    bottom_ref, first_ref, basis_ref, tops_ref, out_ref, top_ref, wide_ref, diag_ref, even_ref, odd_ref, sum_ref
):
    step_id = pl.program_id(0)
    rows_here = A_BLOCK * D

    @pl.when(step_id == 0)
    def _():
        diag_ref[...] = jnp.zeros_like(diag_ref)
        for q in range(16):
            part = tops_ref[:, q].astype(F32).reshape(8, 4, 8, 256)
            part = jnp.transpose(part, (1, 0, 2, 3)).reshape(256, 256)
            top_ref[256 * q : 256 * q + 256, :] = part.T.astype(BF16)

    bottom = bottom_ref[...]

    def sections(group, carry):
        for j in range(UNROLL):
            fill_diagonal(diag_ref, j, first_ref[group * UNROLL + j])
        for j in range(UNROLL):
            section = jnp.dot(bottom, diag_ref[j], preferred_element_type=F32).astype(BF16)
            start = pl.multiple_of((group * UNROLL + j) * D, D)
            for q in range(16):
                wide_ref[pl.ds(start, D), 256 * q : 256 * q + 256] = section[64 * q : 64 * q + 64]
        return carry

    lax.fori_loop(0, A_BLOCK // UNROLL, sections, 0)
    second = jnp.dot(wide_ref[...], top_ref[...], preferred_element_type=F32)
    base = pl.multiple_of(step_id * rows_here, rows_here)
    even_ref[pl.ds(base, rows_here), :] = second[:, :128]
    odd_ref[pl.ds(base, rows_here), :] = second[:, 128:]

    @pl.when(step_id == RANK // A_BLOCK - 1)
    def _():
        sum_ref[...] = jnp.zeros_like(sum_ref)

        def products(group, carry):
            total = jnp.zeros((4 * RANK, RANK), F32)
            for j in range(4):
                at = 16 * group + 4 * j
                parts = []
                for ref in (even_ref, odd_ref):
                    rows = [ref[pl.ds(at + r, RANK, stride=D), :] for r in range(4)]
                    for h in range(2):
                        parts.append(
                            jnp.concatenate([r[:, 64 * h : 64 * h + 64] for r in rows], axis=1)
                        )
                total = total + jnp.dot(
                    jnp.concatenate(parts, axis=0).astype(BF16),
                    basis_ref[pl.ds(at, 4)].reshape(4 * D, RANK),
                    preferred_element_type=F32,
                )
            sum_ref[:, :RANK] += total
            return carry

        lax.fori_loop(0, 4, products, 0)
        for u in range(4):
            pair = [
                sum_ref[pl.ds(RANK * u + odd, RANK // 2, stride=2), :][:, :RANK] for odd in range(2)
            ]
            out_ref[u] = jnp.concatenate(pair, axis=1)


def contract(bottom, first, basis, top):
    whole = lambda *dims: pl.BlockSpec(dims, lambda i: (0,) * len(dims))
    return pl.pallas_call(
        contract_kernel,
        grid=(RANK // A_BLOCK,),
        out_shape=jax.ShapeDtypeStruct((4, RANK // 2, 2 * RANK), F32),
        in_specs=[
            whole(1024, 256),
            pl.BlockSpec((A_BLOCK, D, D), lambda i: (i, 0, 0)),
            whole(D, D, RANK),
            whole(8, 16, 32, 256),
        ],
        out_specs=whole(4, RANK // 2, 2 * RANK),
        scratch_shapes=[
            pltpu.VMEM((D * D, 256), BF16),
            pltpu.VMEM((A_BLOCK * D, D * D), BF16),
            pltpu.VMEM((UNROLL, 256, 256), BF16),
            pltpu.VMEM((RANK * D, 128), F32),
            pltpu.VMEM((RANK * D, 128), F32),
            pltpu.VMEM((4 * RANK, 2 * RANK), F32),
        ],
        compiler_params=pltpu.CompilerParams(vmem_limit_bytes=56 << 20),
    )(bottom, first, basis, top)


def swapped_pairs(tiles):
    lane = lax.broadcasted_iota(jnp.int32, (8, 128), 1)
    stack = jnp.swapaxes(jnp.stack(tiles, axis=0), 0, 1)
    out = []
    for j in range(4):
        a, b = stack[2 * j], stack[2 * j + 1]
        low = jnp.where(lane < 64, a, pltpu.roll(b, 64, 1))
        high = jnp.where(lane < 64, pltpu.roll(a, 64, 1), b)
        out.append((low, high))
    return out


def partial_kernel(up_ref, down_ref, scale_ref, all_ref, out_ref, up_acc, down_acc):
    blocks = [all_ref[c] for c in range(4)]
    order = [(t // 4 + 2 * y, t % 4) for t in range(8) for y in range(2)]
    right = jnp.concatenate([blocks[c][:, 64 * m : 64 * m + 64] for c, m in order], axis=1)
    up_acc[...] = jnp.dot(up_ref[...], right, preferred_element_type=F32) * scale_ref[...]
    rows = []
    for c, m in order:
        part = blocks[c][:, 64 * m : 64 * m + 64]
        rows.append(jnp.concatenate([part[64 * r : 64 * r + 64] for r in range(8)], axis=1))
    down_acc[...] = lax.dot_general(
        down_ref[...],
        jnp.concatenate(rows, axis=0),
        (((1,), (1,)), ((), ())),
        preferred_element_type=F32,
    )
    for which, acc in enumerate((up_acc, down_acc)):
        for left in range(4):
            for high in range(8):
                at = 64 * left + 8 * high
                pieces = swapped_pairs(
                    [acc[at : at + 8, 128 * t : 128 * t + 128] for t in range(8)]
                )
                for j, piece in enumerate(pieces):
                    out_ref[high, which, left, 0, :, 128 * j : 128 * j + 128] = jnp.concatenate(
                        piece, axis=0
                    ).astype(BF16)


def partials(up, down, scale, by_cols):
    whole = lambda *dims: pl.BlockSpec(dims, lambda i: (0,) * len(dims))
    return pl.pallas_call(
        partial_kernel,
        grid=(4,),
        out_shape=jax.ShapeDtypeStruct((8, 2, 4, 4, 16, 512), BF16),
        in_specs=[
            whole(256, 512),
            whole(256, 512),
            whole(1, 1024),
            pl.BlockSpec((4, 512, 256), lambda i: (i, 0, 0)),
        ],
        out_specs=pl.BlockSpec((8, 2, 4, 1, 16, 512), lambda i: (0, 0, 0, i, 0, 0)),
        scratch_shapes=[pltpu.VMEM((256, 1024), F32), pltpu.VMEM((256, 1024), F32)],
        compiler_params=pltpu.CompilerParams(vmem_limit_bytes=48 << 20),
    )(up, down, scale, by_cols)


def side_kernel(
    core_ref, mine_ref, other_ref, inner_ref, rows_ref, lanes_ref, all_ref, out_ref, acc_ref
):
    step = pl.program_id(0)

    @pl.when(step == 0)
    def _():
        acc_ref[...] = jnp.zeros_like(acc_ref)

    order = [s + 4 * y for s in range(4) for y in range(2)]
    left, right = [], []
    for c in range(4):
        own = jnp.concatenate(
            [mine_ref[:, c].reshape(128, 256), other_ref[:, c].reshape(128, 256)], axis=0
        )
        left.append((own.astype(F32) * inner_ref[c]).astype(BF16))
        block = all_ref[c]
        right.append(jnp.concatenate([block[64 * s : 64 * s + 64] for s in order], axis=0))
    acc_ref[...] += lax.dot_general(
        jnp.concatenate(left, axis=1),
        jnp.concatenate(right, axis=1),
        (((1,), (1,)), ((), ())),
        preferred_element_type=F32,
    )

    @pl.when(step == 3)
    def _():
        core = core_ref[0]
        for s in range(16):
            row = 2 * ((s % 8) // 2) + (core if s < 8 else 1 - core)
            first = pl.multiple_of(32 * row + 16 * (s % 2), 16)
            scaled = (
                acc_ref[16 * s : 16 * s + 16, :] * rows_ref[pl.ds(first, 16), :] * lanes_ref[...]
            )
            tiles = [
                scaled[8 * t : 8 * t + 8, 128 * q : 128 * q + 128]
                for t in range(2)
                for q in range(4)
            ]
            pieces = swapped_pairs(tiles)
            for odd in range(2):
                low = jnp.concatenate([pieces[2 * odd][0], pieces[2 * odd + 1][0]], axis=1)
                high = jnp.concatenate([pieces[2 * odd][1], pieces[2 * odd + 1][1]], axis=1)
                for t in range(2):
                    out_ref[8 * row + 4 * (s % 2) + 2 * t + odd] = jnp.concatenate(
                        [low[4 * t : 4 * t + 4], high[4 * t : 4 * t + 4]], axis=0
                    )


def side_gram(core, mine, other, inner, rows, lanes, by_cols):
    whole = lambda *dims: pl.BlockSpec(dims, lambda i: (0,) * len(dims))
    part = pl.BlockSpec((4, 4, 32, 256), lambda i: (0, i, 0, 0))
    return pl.pallas_call(
        side_kernel,
        grid=(4,),
        out_shape=jax.ShapeDtypeStruct((D, 8, 256), F32),
        in_specs=[
            pl.BlockSpec(memory_space=pltpu.SMEM),
            part,
            part,
            pl.BlockSpec((4, 1, 256), lambda i: (i, 0, 0)),
            whole(256, 1),
            whole(1, 512),
            pl.BlockSpec((4, 512, 256), lambda i: (i, 0, 0)),
        ],
        out_specs=whole(D, 8, 256),
        scratch_shapes=[pltpu.VMEM((256, 512), F32)],
        compiler_params=pltpu.CompilerParams(vmem_limit_bytes=48 << 20),
    )(core, mine, other, inner, rows, lanes, by_cols)


def store_gram(acc_ref, high_ref, low_ref):
    for a_high in range(2):
        for x_high in range(8):
            tiles = []
            for a_low in range(2):
                at = 64 * (2 * a_high + a_low) + 8 * x_high
                for q in range(4):
                    tiles.append(acc_ref[at : at + 8, 128 * q : 128 * q + 128])
            for j, piece in enumerate(swapped_pairs(tiles)):
                high, low = two_parts(jnp.concatenate(piece, axis=0))
                lanes = slice(512 * x_high + 128 * j, 512 * x_high + 128 * j + 128)
                high_ref[16 * a_high : 16 * a_high + 16, lanes] = high
                low_ref[16 * a_high : 16 * a_high + 16, lanes] = low


def left_gram_kernel(up_ref, down_ref, high_ref, low_ref, acc_ref):
    acc_ref[...] = lax.dot_general(
        up_ref[...],
        down_ref[...].reshape(512, 512),
        (((1,), (1,)), ((), ())),
        preferred_element_type=F32,
    )
    store_gram(acc_ref, high_ref, low_ref)


def left_gram(up, down):
    out = jax.ShapeDtypeStruct((256, D * D), BF16)
    out_spec = pl.BlockSpec((32, D * D), lambda i: (i, 0))
    return pl.pallas_call(
        left_gram_kernel,
        grid=(8,),
        out_shape=(out, out),
        in_specs=[
            pl.BlockSpec((256, 512), lambda i: (0, 0)),
            pl.BlockSpec((2, 256, 512), lambda i: (i, 0, 0)),
        ],
        out_specs=(out_spec, out_spec),
        scratch_shapes=[pltpu.VMEM((256, 512), F32)],
        compiler_params=pltpu.CompilerParams(vmem_limit_bytes=48 << 20),
    )(up, down)


def down_gram_kernel(core_ref, mine_ref, other_ref, down_ref, high_ref, low_ref, acc_ref):
    step = pl.program_id(0)

    @pl.when(step == 0)
    def _():
        acc_ref[...] = jnp.zeros_like(acc_ref)

    halves = by_core(core_ref, mine_ref[...].astype(F32), other_ref[...].astype(F32))
    side = jnp.stack([h.reshape(4, 16, 8, 256) for h in halves], axis=1)
    side = jnp.transpose(side.reshape(8, 16, 8, 256), (1, 0, 2, 3)).reshape(1024, 256)
    acc_ref[...] += lax.dot_general(
        side.astype(BF16),
        down_ref[...].reshape(1024, 512),
        (((0,), (0,)), ((), ())),
        preferred_element_type=F32,
    )

    @pl.when(step == 3)
    def _():
        store_gram(acc_ref, high_ref, low_ref)


def down_gram(core, mine, other, down):
    out = jax.ShapeDtypeStruct((32, D * D), BF16)
    out_spec = pl.BlockSpec((32, D * D), lambda i: (0, 0))
    part = pl.BlockSpec((4, 128, 256), lambda i: (0, i, 0))
    return pl.pallas_call(
        down_gram_kernel,
        grid=(4,),
        out_shape=(out, out),
        in_specs=[
            pl.BlockSpec(memory_space=pltpu.SMEM),
            part,
            part,
            pl.BlockSpec((4, 256, 512), lambda i: (i, 0, 0)),
        ],
        out_specs=(out_spec, out_spec),
        scratch_shapes=[pltpu.VMEM((256, 512), F32)],
        compiler_params=pltpu.CompilerParams(vmem_limit_bytes=48 << 20),
    )(core, mine, other, down)


def body(tensor, bond_weights, start_blocks):
    row_index = lax.axis_index(ROW)

    def both_cores(shard):
        mine = from_everyone(shard, "z")
        return mine, lax.ppermute(mine, "core", [(0, 1), (1, 0)])

    where = jnp.reshape(lax.axis_index("core"), (1,)).astype(jnp.int32)
    horizontal = bond_weights[0]
    vertical = bond_weights[1]
    horiz_rows = lax.dynamic_slice_in_dim(horizontal, row_index * 8, 8)
    grid = tensor.reshape(4, 8, D, D)
    flat = jnp.transpose(grid, (1, 2, 0, 3)).reshape(512, 256)
    by_cols = lax.all_gather(flat, COL)

    square = vertical * vertical
    rows_square = horiz_rows * horiz_rows
    turned = flat.T.astype(F32)
    up_scale = (rows_square[:, None] * square[None, :]).reshape(1, 512)
    own_up = (turned * up_scale * jnp.tile(vertical, 4)[:, None]).astype(BF16)
    weighted = (turned * jnp.tile(vertical, 8)[None, :]).astype(BF16)
    top_piece = jnp.swapaxes(weighted.reshape(4, 16, 4, 512), 0, 1).reshape(16, 16, 512)
    side_piece = jnp.swapaxes(flat.reshape(8, 16, 4, 256), 0, 1).reshape(16, 32, 256)
    top_piece = top_piece.reshape(16, 16, 2, 256).swapaxes(1, 2).reshape(16, 32, 256)
    pieces = jnp.concatenate([side_piece, top_piece], axis=1)
    pieces = lax.all_to_all(pieces, COL, 0, 0, tiled=True)
    top_got = pieces[:, 32:].reshape(16, 2, 16, 256).swapaxes(1, 2).reshape(16, 16, 512)
    side_own = both_cores(pieces[:, :32])
    own_down = grid.astype(F32) * rows_square[None, :, None, None] * square
    own_down = jnp.transpose(own_down.astype(BF16), (0, 2, 1, 3)).reshape(256, 512)

    by_cols, side_own = lax.optimization_barrier((by_cols, side_own))
    lane_scale = jnp.tile(vertical, 16)[None, :]
    parts = partials(own_up, own_down, lane_scale, by_cols).reshape(8, 2, 4, D, 512)
    left_both = lax.psum_scatter(parts, ROW, scatter_dimension=0, tiled=True)

    inner = ((horizontal * horizontal)[:, None] * square[None, :]).reshape(16, 1, 256)
    lanes = jnp.repeat(jnp.transpose(horiz_rows.reshape(2, 4)).reshape(8), D)[None, :]
    side = side_gram(
        where, *side_own, inner, jnp.repeat(horizontal, 4)[:, None], lanes, by_cols
    )

    def everywhere(y):
        mine = lax.all_to_all(
            jnp.broadcast_to(y, (64, 32, 2 * RANK)), SAME_CORE, 0, 0, tiled=True
        ).reshape(2048, 2 * RANK)
        return mine, lax.ppermute(mine, "core", [(0, 1), (1, 0)])

    first_vectors = everywhere(start_blocks.reshape(32, 2 * RANK))
    left_both, first_vectors, side = lax.optimization_barrier((left_both, first_vectors, side))
    left_both = left_both.reshape(2, 256, 512)
    down_all = lax.all_gather(left_both[1], COL)
    side_all = both_cores(side.astype(BF16).reshape(512, 256))

    slab_part = by_cols.reshape(16, 8, D, 256)[:, :, :8]
    slab_part = jnp.transpose(slab_part, (2, 0, 1, 3)).reshape(8, 128, 256)
    slab = lax.all_to_all(slab_part, ROW, split_axis=0, concat_axis=0, tiled=True)
    bottom, top_rows = vmem_call(
        fold_kernel,
        (
            jax.ShapeDtypeStruct((16, D, 256), BF16),
            jax.ShapeDtypeStruct((16, 32, 256), BF16),
        ),
        (slab, top_got),
    )
    down_all, bottom, top_rows, side_all = lax.optimization_barrier(
        (down_all, bottom, top_rows, side_all)
    )
    grams = (*left_gram(left_both[0], down_all), *down_gram(where, *side_all, down_all))
    top_rows, grams = lax.optimization_barrier((top_rows, grams))
    top = lax.all_gather(top_rows, ROW)
    z_outs = (
        jax.ShapeDtypeStruct((8, 16, 2 * RANK), F32),
        jax.ShapeDtypeStruct((32, 2 * RANK), F32),
    )
    inv_out = jax.ShapeDtypeStruct((2 * RANK, 2 * RANK), F32)

    def local_images(z_left, z_down):
        z_left = jnp.sum(lax.all_to_all(z_left, ROW, 0, 0, tiled=True), axis=0)
        z_left = jnp.concatenate([z_left[:, :RANK], z_left[:, RANK:]], axis=0)
        z = jnp.concatenate([z_left, z_down[:, RANK:]], axis=1)
        z = jnp.transpose(z.reshape(2, 2, 2, 4, 2 * RANK), (0, 2, 3, 1, 4))
        return z.reshape(32, 2 * RANK)

    def apply(y, inverse):
        return lax.dot_general(y, inverse, (((1,), (1,)), ((), ())), precision=HIGHEST)

    vectors = first_vectors
    for step in range(3):
        y = local_images(*vmem_call(images_kernel, z_outs, (where, *vectors, *grams), 1))
        if step:
            y = apply(y, vmem_call(factor_kernel, (inv_out,), vectors)[0])
        vectors = everywhere(y)
    basis_out = jax.ShapeDtypeStruct((D * D, RANK), BF16)
    basis, mixed, inverse = vmem_call(
        last_kernel, (basis_out, basis_out, inv_out), (where, *vectors), 1
    )
    projectors = apply(y, inverse).reshape(4, 8, 2 * RANK)
    first = jnp.transpose(mixed.reshape(16, 4, D, RANK), (3, 1, 0, 2)).reshape(RANK, D, D)
    new_tensor = contract(bottom.reshape(1024, 256), first, basis.reshape(D, D, RANK), top)
    return (projectors, new_tensor.reshape(4, 1, RANK * RANK))


def solution(mesh):
    axes = ("z", "core", "col_0", "col_1")
    torus = Mesh(mesh.devices.reshape(mesh.shape["row"] // 2, 2, 4, 4), axes)
    placed = (P(COL, ROW, None), P(), P(COL, ROW, None))
    return jax.shard_map(
        body,
        mesh=torus,
        in_specs=placed,
        out_specs=(P(COL, ROW, None), P(COL, ROW, None)),
        check_vma=False,
    )
```

```python
import jax
import jax.numpy as jnp
from jax import lax
from jax.experimental import pallas as pl
from jax.experimental.pallas import tpu as pltpu
from jax.sharding import Mesh
from jax.sharding import PartitionSpec as P

D = 64
RANK = 64
COL = ("col_0", "col_1")
ROW = ("z", "core")
SAME_CORE = ("z", "col_0", "col_1")
HIGHEST = lax.Precision.HIGHEST
F32 = jnp.float32
BF16 = jnp.bfloat16
A_BLOCK = 32
UNROLL = 16


def from_everyone(shard, axis):
    copies = jnp.broadcast_to(shard, (lax.axis_size(axis), *shard.shape))
    return lax.all_to_all(copies, axis, split_axis=0, concat_axis=0, tiled=True)


def two_parts(x):
    high = x.astype(BF16)
    return high, (x - high.astype(F32)).astype(BF16)


def by_core(core_ref, mine, other):
    first = core_ref[0] == 0
    return jnp.where(first, mine, other), jnp.where(first, other, mine)


def in_index_order(core_ref, mine_ref, other_ref):
    halves = by_core(core_ref, mine_ref[...], other_ref[...])
    y = jnp.stack([h.reshape(4, D, 8, 2 * RANK) for h in halves], axis=1)
    y = jnp.transpose(y.reshape(8, D, 8, 2 * RANK), (1, 0, 2, 3))
    return y.reshape(D * D, 2 * RANK)


def inverse_factors(mats):
    n = RANK
    count = n // 8
    rows_at = lax.broadcasted_iota(jnp.int32, (8, 2 * n), 0)
    lanes_at = lax.broadcasted_iota(jnp.int32, (8, 2 * n), 1)
    sets = []
    for c in mats:
        blocks = []
        for i in range(count):
            unit = (lanes_at == rows_at + (n + 8 * i)).astype(F32)
            part = jnp.concatenate([c[8 * i : 8 * i + 8], jnp.zeros((8, n), F32)], axis=1)
            blocks.append(part + unit)
        sets.append((blocks, []))
    for b in range(count):
        panels = []
        for blocks, _ in sets:
            columns = [
                {
                    i: jnp.broadcast_to(blocks[i][:, 8 * b + j : 8 * b + j + 1], (8, 2 * n))
                    for i in range(b, count)
                }
                for j in range(8)
            ]
            rows = [jnp.broadcast_to(blocks[b][j : j + 1], (8, 2 * n)) for j in range(8)]
            panels.append((columns, rows, []))
        for j in range(8):
            for (blocks, pivots), (columns, rows, scaled) in zip(sets, panels):
                own = columns[j][b]
                inverse = 1.0 / own[j : j + 1]
                pivots.append(own[j : j + 1])
                scaled.append(rows[j] * inverse)
                for k in range(j + 1, 8):
                    factor = columns[k][b][j : j + 1] * inverse
                    rows[k] = rows[k] - own[k : k + 1] * scaled[j]
                    for i in range(b, count):
                        columns[k][i] = columns[k][i] - columns[j][i] * factor
        for (blocks, _), (columns, rows, scaled) in zip(sets, panels):
            whole = rows[0]
            for j in range(1, 8):
                whole = jnp.where(rows_at == j, rows[j], whole)
            blocks[b] = whole
            for i in range(b + 1, count):
                for j in range(8):
                    blocks[i] = blocks[i] - columns[j][i] * scaled[j]
    out = []
    for blocks, pivots in sets:
        done = []
        for i in range(count):
            pivot = jnp.broadcast_to(pivots[8 * i], (8, 2 * n))
            for j in range(1, 8):
                pivot = jnp.where(rows_at == j, pivots[8 * i + j], pivot)
            done.append((blocks[i] / jnp.sqrt(pivot))[:, n:])
        out.append(jnp.concatenate(done, axis=0))
    return out


def correlation(y):
    return lax.dot_general(
        y, y, (((0,), (0,)), ((), ())), precision=HIGHEST, preferred_element_type=F32
    )


def factors_of(c):
    return inverse_factors([c[:RANK, :RANK], c[RANK:, RANK:]])


def store_inverse(inv_ref, left, down):
    zero = jnp.zeros((RANK, RANK), F32)
    inv_ref[:RANK, :] = jnp.concatenate([left, zero], axis=1)
    inv_ref[RANK:, :] = jnp.concatenate([zero, down], axis=1)


def images_of(y, gl_high, gl_low, gd_high, gd_low, zl_ref, zd_ref):
    y_high, y_low = two_parts(y)
    both = jnp.concatenate([y_high, y_low], axis=1)

    def product(high, low):
        main = jnp.dot(high[...], both, preferred_element_type=F32)
        rest = jnp.dot(low[...], y_high, preferred_element_type=F32)
        return main[:, : 2 * RANK] + main[:, 2 * RANK :] + rest

    z = product(gl_high, gl_low)[:, :RANK].reshape(8, 32, RANK)
    zl_ref[...] = jnp.concatenate([z[:, :16], z[:, 16:]], axis=2)
    zd_ref[...] = product(gd_high, gd_low)


def images_kernel(core_ref, mine_ref, other_ref, glh, gll, gdh, gdl, zl_ref, zd_ref):
    y = in_index_order(core_ref, mine_ref, other_ref)
    images_of(y, glh, gll, gdh, gdl, zl_ref, zd_ref)


def factor_kernel(mine_ref, other_ref, inv_ref):
    c = correlation(mine_ref[...]) + correlation(other_ref[...])
    store_inverse(inv_ref, *factors_of(c))


def last_kernel(core_ref, mine_ref, other_ref, basis_ref, mixed_ref, inv_ref):
    c = correlation(mine_ref[...]) + correlation(other_ref[...])
    left, down = factors_of(c)
    store_inverse(inv_ref, left, down)
    y = in_index_order(core_ref, mine_ref, other_ref)[:, :RANK]
    y_high, y_low = two_parts(y)
    l_high, l_low = two_parts(left.T)
    basis = jnp.dot(
        jnp.concatenate([y_high, y_low, y_high], axis=1),
        jnp.concatenate([l_high, l_high, l_low], axis=0),
        preferred_element_type=F32,
    )
    basis = basis.astype(BF16)
    basis_ref[...] = basis
    to = lax.broadcasted_iota(jnp.int32, (256, 256), 0)
    at = lax.broadcasted_iota(jnp.int32, (256, 256), 1)
    source = (to // 64) * 64 + (to % 16) * 4 + (to % 64) // 16
    picks = (at == source).astype(F32).astype(BF16)
    for q in range(16):
        rows = slice(256 * q, 256 * q + 256)
        mixed_ref[rows, :] = jnp.dot(
            picks, basis[rows], preferred_element_type=F32
        ).astype(BF16)


def folded(columns):
    rows = []
    for x in range(0, 8, 2):
        turned = jnp.concatenate(columns[x : x + 2], axis=1).T
        for h in range(2):
            parts = [turned[64 * h + 16 * q : 64 * h + 16 * q + 16] for q in range(4)]
            rows.append(jnp.concatenate(parts, axis=1))
    return jnp.swapaxes(jnp.stack(rows, axis=0), 0, 1)


def fold_kernel(slab_ref, top_ref, bottom_out, top_out):
    for g in range(4):
        both = []
        for h in range(2):
            block = slab_ref[2 * g + h].astype(F32).reshape(16, 8, 256)
            by_r = jnp.swapaxes(block, 0, 1)
            both.append(
                folded(
                    [
                        jnp.concatenate(
                            [by_r[r][:, 64 * l : 64 * l + 64] for l in range(4)], axis=0
                        )
                        for r in range(8)
                    ]
                )
            )
        bottom_out[:, 16 * g : 16 * g + 16, :] = jnp.concatenate(both, axis=1).astype(BF16)
    block = top_ref[...].astype(F32)
    halves = [jnp.swapaxes(block[:, 8 * h : 8 * h + 8], 0, 1) for h in range(2)]
    for g in range(2):
        both = []
        for u in range(2 * g, 2 * g + 2):
            rows = jnp.concatenate([halves[l // 2][4 * (l % 2) + u] for l in range(4)], axis=0)
            both.append(folded([rows[:, 64 * r : 64 * r + 64] for r in range(8)]))
        top_out[:, 16 * g : 16 * g + 16, :] = jnp.concatenate(both, axis=1).astype(BF16)


def vmem_call(kernel, outs, args, scalars=0, limit=48):
    spec = pl.BlockSpec(memory_space=pltpu.VMEM)
    scalar = pl.BlockSpec(memory_space=pltpu.SMEM)
    return pl.pallas_call(
        kernel,
        out_shape=tuple(outs),
        in_specs=[scalar] * scalars + [spec] * (len(args) - scalars),
        out_specs=tuple([spec] * len(outs)),
        compiler_params=pltpu.CompilerParams(vmem_limit_bytes=limit << 20),
    )(*args)


def fill_diagonal(diag_ref, slot, block):
    for i in range(4):
        diag_ref[slot, 64 * i : 64 * i + 64, 64 * i : 64 * i + 64] = block


def contract_kernel(
    bottom_ref, first_ref, basis_ref, tops_ref, out_ref, top_ref, wide_ref, diag_ref, even_ref, odd_ref, sum_ref
):
    step_id = pl.program_id(0)
    rows_here = A_BLOCK * D

    @pl.when(step_id == 0)
    def _():
        diag_ref[...] = jnp.zeros_like(diag_ref)
        for q in range(16):
            part = tops_ref[:, q].astype(F32).reshape(8, 4, 8, 256)
            part = jnp.transpose(part, (1, 0, 2, 3)).reshape(256, 256)
            top_ref[256 * q : 256 * q + 256, :] = part.T.astype(BF16)

    bottom = bottom_ref[...]

    def sections(group, carry):
        for j in range(UNROLL):
            fill_diagonal(diag_ref, j, first_ref[group * UNROLL + j])
        for j in range(UNROLL):
            section = jnp.dot(bottom, diag_ref[j], preferred_element_type=F32).astype(BF16)
            start = pl.multiple_of((group * UNROLL + j) * D, D)
            for q in range(16):
                wide_ref[pl.ds(start, D), 256 * q : 256 * q + 256] = section[64 * q : 64 * q + 64]
        return carry

    lax.fori_loop(0, A_BLOCK // UNROLL, sections, 0)
    second = jnp.dot(wide_ref[...], top_ref[...], preferred_element_type=F32)
    base = pl.multiple_of(step_id * rows_here, rows_here)
    even_ref[pl.ds(base, rows_here), :] = second[:, :128]
    odd_ref[pl.ds(base, rows_here), :] = second[:, 128:]

    @pl.when(step_id == RANK // A_BLOCK - 1)
    def _():
        sum_ref[...] = jnp.zeros_like(sum_ref)

        def products(group, carry):
            total = jnp.zeros((4 * RANK, RANK), F32)
            for j in range(4):
                at = 16 * group + 4 * j
                parts = []
                for ref in (even_ref, odd_ref):
                    rows = [ref[pl.ds(at + r, RANK, stride=D), :] for r in range(4)]
                    for h in range(2):
                        parts.append(
                            jnp.concatenate([r[:, 64 * h : 64 * h + 64] for r in rows], axis=1)
                        )
                total = total + jnp.dot(
                    jnp.concatenate(parts, axis=0).astype(BF16),
                    basis_ref[pl.ds(at, 4)].reshape(4 * D, RANK),
                    preferred_element_type=F32,
                )
            sum_ref[:, :RANK] += total
            return carry

        lax.fori_loop(0, 4, products, 0)
        for u in range(4):
            pair = [
                sum_ref[pl.ds(RANK * u + odd, RANK // 2, stride=2), :][:, :RANK] for odd in range(2)
            ]
            out_ref[u] = jnp.concatenate(pair, axis=1)


def contract(bottom, first, basis, top):
    whole = lambda *dims: pl.BlockSpec(dims, lambda i: (0,) * len(dims))
    return pl.pallas_call(
        contract_kernel,
        grid=(RANK // A_BLOCK,),
        out_shape=jax.ShapeDtypeStruct((4, RANK // 2, 2 * RANK), F32),
        in_specs=[
            whole(1024, 256),
            pl.BlockSpec((A_BLOCK, D, D), lambda i: (i, 0, 0)),
            whole(D, D, RANK),
            whole(8, 16, 32, 256),
        ],
        out_specs=whole(4, RANK // 2, 2 * RANK),
        scratch_shapes=[
            pltpu.VMEM((D * D, 256), BF16),
            pltpu.VMEM((A_BLOCK * D, D * D), BF16),
            pltpu.VMEM((UNROLL, 256, 256), BF16),
            pltpu.VMEM((RANK * D, 128), F32),
            pltpu.VMEM((RANK * D, 128), F32),
            pltpu.VMEM((4 * RANK, 2 * RANK), F32),
        ],
        compiler_params=pltpu.CompilerParams(vmem_limit_bytes=56 << 20),
    )(bottom, first, basis, top)


def swapped_pairs(tiles):
    lane = lax.broadcasted_iota(jnp.int32, (8, 128), 1)
    stack = jnp.swapaxes(jnp.stack(tiles, axis=0), 0, 1)
    out = []
    for j in range(4):
        a, b = stack[2 * j], stack[2 * j + 1]
        low = jnp.where(lane < 64, a, pltpu.roll(b, 64, 1))
        high = jnp.where(lane < 64, pltpu.roll(a, 64, 1), b)
        out.append((low, high))
    return out


def partial_kernel(up_ref, down_ref, scale_ref, all_ref, out_ref, up_acc, down_acc):
    blocks = [all_ref[c] for c in range(4)]
    order = [(t // 4 + 2 * y, t % 4) for t in range(8) for y in range(2)]
    right = jnp.concatenate([blocks[c][:, 64 * m : 64 * m + 64] for c, m in order], axis=1)
    up_acc[...] = jnp.dot(up_ref[...], right, preferred_element_type=F32) * scale_ref[...]
    rows = []
    for c, m in order:
        part = blocks[c][:, 64 * m : 64 * m + 64]
        rows.append(jnp.concatenate([part[64 * r : 64 * r + 64] for r in range(8)], axis=1))
    down_acc[...] = lax.dot_general(
        down_ref[...],
        jnp.concatenate(rows, axis=0),
        (((1,), (1,)), ((), ())),
        preferred_element_type=F32,
    )
    for which, acc in enumerate((up_acc, down_acc)):
        for left in range(4):
            for high in range(8):
                at = 64 * left + 8 * high
                pieces = swapped_pairs(
                    [acc[at : at + 8, 128 * t : 128 * t + 128] for t in range(8)]
                )
                for j, piece in enumerate(pieces):
                    out_ref[high, which, left, 0, :, 128 * j : 128 * j + 128] = jnp.concatenate(
                        piece, axis=0
                    ).astype(BF16)


def partials(up, down, scale, by_cols):
    whole = lambda *dims: pl.BlockSpec(dims, lambda i: (0,) * len(dims))
    return pl.pallas_call(
        partial_kernel,
        grid=(4,),
        out_shape=jax.ShapeDtypeStruct((8, 2, 4, 4, 16, 512), BF16),
        in_specs=[
            whole(256, 512),
            whole(256, 512),
            whole(1, 1024),
            pl.BlockSpec((4, 512, 256), lambda i: (i, 0, 0)),
        ],
        out_specs=pl.BlockSpec((8, 2, 4, 1, 16, 512), lambda i: (0, 0, 0, i, 0, 0)),
        scratch_shapes=[pltpu.VMEM((256, 1024), F32), pltpu.VMEM((256, 1024), F32)],
        compiler_params=pltpu.CompilerParams(vmem_limit_bytes=48 << 20),
    )(up, down, scale, by_cols)


def side_kernel(
    core_ref, mine_ref, other_ref, inner_ref, rows_ref, lanes_ref, all_ref, out_ref, acc_ref
):
    step = pl.program_id(0)

    @pl.when(step == 0)
    def _():
        acc_ref[...] = jnp.zeros_like(acc_ref)

    order = [s + 4 * y for s in range(4) for y in range(2)]
    left, right = [], []
    for c in range(4):
        own = jnp.concatenate(
            [mine_ref[:, c].reshape(128, 256), other_ref[:, c].reshape(128, 256)], axis=0
        )
        left.append((own.astype(F32) * inner_ref[c]).astype(BF16))
        block = all_ref[c]
        right.append(jnp.concatenate([block[64 * s : 64 * s + 64] for s in order], axis=0))
    acc_ref[...] += lax.dot_general(
        jnp.concatenate(left, axis=1),
        jnp.concatenate(right, axis=1),
        (((1,), (1,)), ((), ())),
        preferred_element_type=F32,
    )

    @pl.when(step == 3)
    def _():
        core = core_ref[0]
        for s in range(16):
            row = 2 * ((s % 8) // 2) + (core if s < 8 else 1 - core)
            first = pl.multiple_of(32 * row + 16 * (s % 2), 16)
            scaled = (
                acc_ref[16 * s : 16 * s + 16, :] * rows_ref[pl.ds(first, 16), :] * lanes_ref[...]
            )
            tiles = [
                scaled[8 * t : 8 * t + 8, 128 * q : 128 * q + 128]
                for t in range(2)
                for q in range(4)
            ]
            pieces = swapped_pairs(tiles)
            for odd in range(2):
                low = jnp.concatenate([pieces[2 * odd][0], pieces[2 * odd + 1][0]], axis=1)
                high = jnp.concatenate([pieces[2 * odd][1], pieces[2 * odd + 1][1]], axis=1)
                for t in range(2):
                    out_ref[8 * row + 4 * (s % 2) + 2 * t + odd] = jnp.concatenate(
                        [low[4 * t : 4 * t + 4], high[4 * t : 4 * t + 4]], axis=0
                    )


def side_gram(core, mine, other, inner, rows, lanes, by_cols):
    whole = lambda *dims: pl.BlockSpec(dims, lambda i: (0,) * len(dims))
    part = pl.BlockSpec((4, 4, 32, 256), lambda i: (0, i, 0, 0))
    return pl.pallas_call(
        side_kernel,
        grid=(4,),
        out_shape=jax.ShapeDtypeStruct((D, 8, 256), F32),
        in_specs=[
            pl.BlockSpec(memory_space=pltpu.SMEM),
            part,
            part,
            pl.BlockSpec((4, 1, 256), lambda i: (i, 0, 0)),
            whole(256, 1),
            whole(1, 512),
            pl.BlockSpec((4, 512, 256), lambda i: (i, 0, 0)),
        ],
        out_specs=whole(D, 8, 256),
        scratch_shapes=[pltpu.VMEM((256, 512), F32)],
        compiler_params=pltpu.CompilerParams(vmem_limit_bytes=48 << 20),
    )(core, mine, other, inner, rows, lanes, by_cols)


def store_gram(acc_ref, high_ref, low_ref):
    for a_high in range(2):
        for x_high in range(8):
            tiles = []
            for a_low in range(2):
                at = 64 * (2 * a_high + a_low) + 8 * x_high
                for q in range(4):
                    tiles.append(acc_ref[at : at + 8, 128 * q : 128 * q + 128])
            for j, piece in enumerate(swapped_pairs(tiles)):
                high, low = two_parts(jnp.concatenate(piece, axis=0))
                lanes = slice(512 * x_high + 128 * j, 512 * x_high + 128 * j + 128)
                high_ref[16 * a_high : 16 * a_high + 16, lanes] = high
                low_ref[16 * a_high : 16 * a_high + 16, lanes] = low


def left_gram_kernel(up_ref, down_ref, high_ref, low_ref, acc_ref):
    for half in range(2):
        acc_ref[half] = lax.dot_general(
            up_ref[0],
            down_ref[2 * half : 2 * half + 2].reshape(512, 512),
            (((1,), (1,)), ((), ())),
            preferred_element_type=F32,
        )
    for half in range(2):
        rows = pl.ds(32 * half, 32)
        store_gram(acc_ref.at[half], high_ref.at[rows], low_ref.at[rows])


def left_gram(up, down):
    out = jax.ShapeDtypeStruct((256, D * D), BF16)
    out_spec = pl.BlockSpec((64, D * D), lambda i: (i, 0))
    return pl.pallas_call(
        left_gram_kernel,
        grid=(4,),
        out_shape=(out, out),
        in_specs=[
            pl.BlockSpec((1, 256, 512), lambda i: (0, 0, 0)),
            pl.BlockSpec((4, 256, 512), lambda i: (i, 0, 0)),
        ],
        out_specs=(out_spec, out_spec),
        scratch_shapes=[pltpu.VMEM((2, 256, 512), F32)],
        compiler_params=pltpu.CompilerParams(vmem_limit_bytes=48 << 20),
    )(up, down)


def down_gram_kernel(core_ref, mine_ref, other_ref, down_ref, high_ref, low_ref, acc_ref):
    step = pl.program_id(0)

    @pl.when(step == 0)
    def _():
        acc_ref[...] = jnp.zeros_like(acc_ref)

    halves = by_core(core_ref, mine_ref[...].astype(F32), other_ref[...].astype(F32))
    side = jnp.stack([h.reshape(4, 16, 8, 256) for h in halves], axis=1)
    side = jnp.transpose(side.reshape(8, 16, 8, 256), (1, 0, 2, 3)).reshape(1024, 256)
    acc_ref[...] += lax.dot_general(
        side.astype(BF16),
        down_ref[...].reshape(1024, 512),
        (((0,), (0,)), ((), ())),
        preferred_element_type=F32,
    )

    @pl.when(step == 3)
    def _():
        store_gram(acc_ref, high_ref, low_ref)


def down_gram(core, mine, other, down):
    out = jax.ShapeDtypeStruct((32, D * D), BF16)
    out_spec = pl.BlockSpec((32, D * D), lambda i: (0, 0))
    part = pl.BlockSpec((4, 128, 256), lambda i: (0, i, 0))
    return pl.pallas_call(
        down_gram_kernel,
        grid=(4,),
        out_shape=(out, out),
        in_specs=[
            pl.BlockSpec(memory_space=pltpu.SMEM),
            part,
            part,
            pl.BlockSpec((4, 256, 512), lambda i: (i, 0, 0)),
        ],
        out_specs=(out_spec, out_spec),
        scratch_shapes=[pltpu.VMEM((256, 512), F32)],
        compiler_params=pltpu.CompilerParams(vmem_limit_bytes=48 << 20),
    )(core, mine, other, down)


def body(tensor, bond_weights, start_blocks):
    row_index = lax.axis_index(ROW)

    def both_cores(shard):
        mine = from_everyone(shard, "z")
        return mine, lax.ppermute(mine, "core", [(0, 1), (1, 0)])

    where = jnp.reshape(lax.axis_index("core"), (1,)).astype(jnp.int32)
    horizontal = bond_weights[0]
    vertical = bond_weights[1]
    horiz_rows = lax.dynamic_slice_in_dim(horizontal, row_index * 8, 8)
    grid = tensor.reshape(4, 8, D, D)
    flat = jnp.transpose(grid, (1, 2, 0, 3)).reshape(512, 256)
    by_cols = lax.all_gather(flat, COL)

    square = vertical * vertical
    rows_square = horiz_rows * horiz_rows
    turned = flat.T.astype(F32)
    up_scale = (rows_square[:, None] * square[None, :]).reshape(1, 512)
    own_up = (turned * up_scale * jnp.tile(vertical, 4)[:, None]).astype(BF16)
    weighted = (turned * jnp.tile(vertical, 8)[None, :]).astype(BF16)
    top_piece = jnp.swapaxes(weighted.reshape(4, 16, 4, 512), 0, 1).reshape(16, 16, 512)
    side_piece = jnp.swapaxes(flat.reshape(8, 16, 4, 256), 0, 1).reshape(16, 32, 256)
    top_piece = top_piece.reshape(16, 16, 2, 256).swapaxes(1, 2).reshape(16, 32, 256)
    pieces = jnp.concatenate([side_piece, top_piece], axis=1)
    pieces = lax.all_to_all(pieces, COL, 0, 0, tiled=True)
    top_got = pieces[:, 32:].reshape(16, 2, 16, 256).swapaxes(1, 2).reshape(16, 16, 512)
    side_own = both_cores(pieces[:, :32])
    own_down = grid.astype(F32) * rows_square[None, :, None, None] * square
    own_down = jnp.transpose(own_down.astype(BF16), (0, 2, 1, 3)).reshape(256, 512)

    by_cols, side_own = lax.optimization_barrier((by_cols, side_own))
    lane_scale = jnp.tile(vertical, 16)[None, :]
    parts = partials(own_up, own_down, lane_scale, by_cols).reshape(8, 2, 4, D, 512)
    left_both = lax.psum_scatter(parts, ROW, scatter_dimension=0, tiled=True)

    inner = ((horizontal * horizontal)[:, None] * square[None, :]).reshape(16, 1, 256)
    lanes = jnp.repeat(jnp.transpose(horiz_rows.reshape(2, 4)).reshape(8), D)[None, :]
    side = side_gram(
        where, *side_own, inner, jnp.repeat(horizontal, 4)[:, None], lanes, by_cols
    )

    def everywhere(y):
        mine = lax.all_to_all(
            jnp.broadcast_to(y, (64, 32, 2 * RANK)), SAME_CORE, 0, 0, tiled=True
        ).reshape(2048, 2 * RANK)
        return mine, lax.ppermute(mine, "core", [(0, 1), (1, 0)])

    first_vectors = everywhere(start_blocks.reshape(32, 2 * RANK))
    left_both, first_vectors, side = lax.optimization_barrier((left_both, first_vectors, side))
    left_both = left_both.reshape(2, 256, 512)
    down_all = lax.all_gather(left_both[1], COL)
    side_all = both_cores(side.astype(BF16).reshape(512, 256))

    slab_part = by_cols.reshape(16, 8, D, 256)[:, :, :8]
    slab_part = jnp.transpose(slab_part, (2, 0, 1, 3)).reshape(8, 128, 256)
    slab = lax.all_to_all(slab_part, ROW, split_axis=0, concat_axis=0, tiled=True)
    bottom, top_rows = vmem_call(
        fold_kernel,
        (
            jax.ShapeDtypeStruct((16, D, 256), BF16),
            jax.ShapeDtypeStruct((16, 32, 256), BF16),
        ),
        (slab, top_got),
    )
    down_all, bottom, top_rows, side_all = lax.optimization_barrier(
        (down_all, bottom, top_rows, side_all)
    )
    grams = (*left_gram(left_both, down_all), *down_gram(where, *side_all, down_all))
    top_rows, grams = lax.optimization_barrier((top_rows, grams))
    top = lax.all_gather(top_rows, ROW)
    z_outs = (
        jax.ShapeDtypeStruct((8, 16, 2 * RANK), F32),
        jax.ShapeDtypeStruct((32, 2 * RANK), F32),
    )
    inv_out = jax.ShapeDtypeStruct((2 * RANK, 2 * RANK), F32)

    def local_images(z_left, z_down):
        z_left = jnp.sum(lax.all_to_all(z_left, ROW, 0, 0, tiled=True), axis=0)
        z_left = jnp.concatenate([z_left[:, :RANK], z_left[:, RANK:]], axis=0)
        z = jnp.concatenate([z_left, z_down[:, RANK:]], axis=1)
        z = jnp.transpose(z.reshape(2, 2, 2, 4, 2 * RANK), (0, 2, 3, 1, 4))
        return z.reshape(32, 2 * RANK)

    def apply(y, inverse):
        return lax.dot_general(y, inverse, (((1,), (1,)), ((), ())), precision=HIGHEST)

    vectors = first_vectors
    for step in range(3):
        y = local_images(*vmem_call(images_kernel, z_outs, (where, *vectors, *grams), 1))
        if step:
            y = apply(y, vmem_call(factor_kernel, (inv_out,), vectors)[0])
        vectors = everywhere(y)
    basis_out = jax.ShapeDtypeStruct((D * D, RANK), BF16)
    basis, mixed, inverse = vmem_call(
        last_kernel, (basis_out, basis_out, inv_out), (where, *vectors), 1
    )
    projectors = apply(y, inverse).reshape(4, 8, 2 * RANK)
    first = jnp.transpose(mixed.reshape(16, 4, D, RANK), (3, 1, 0, 2)).reshape(RANK, D, D)
    new_tensor = contract(bottom.reshape(1024, 256), first, basis.reshape(D, D, RANK), top)
    return (projectors, new_tensor.reshape(4, 1, RANK * RANK))


def solution(mesh):
    axes = ("z", "core", "col_0", "col_1")
    torus = Mesh(mesh.devices.reshape(mesh.shape["row"] // 2, 2, 4, 4), axes)
    placed = (P(COL, ROW, None), P(), P(COL, ROW, None))
    return jax.shard_map(
        body,
        mesh=torus,
        in_specs=placed,
        out_specs=(P(COL, ROW, None), P(COL, ROW, None)),
        check_vma=False,
    )
```
